512 devices in a mesh: archive: 64 (over z, x, core), dp: 8 (over y).
Axes of the slice: x: 4, y: 8, z: 8, core: 2. Of those that a mesh axis runs over, the one named last changes fastest.
Arguments:
- query_frames: bfloat16 [4096, 32, 512], P(('archive', 'dp')), may hold values from -7 to 7
- line_frames: bfloat16 [512, 128, 512], P('archive'), may hold values from -7 to 7
- frame_count: int32 [512], replicated, may hold values from 1 to 128, 49152 in all
- line_home: int32 [512], replicated, may hold values from 0 to 511, as said below
- mined: int32 [4096, 6], P(('archive', 'dp')), may hold values from 0 to 511, as said below
- positive: int32 [4096], P(('archive', 'dp')), may hold values from 0 to 5
- w_in: bfloat16 [512, 384], replicated, may hold values from -0.25 to 0.25
- bias_in: float32 [384], replicated, may hold values from -0.5 to 0.5
- w_out: bfloat16 [384, 128], replicated, may hold values from -0.3125 to 0.3125
Outputs:
- query_loss: float32 [4096], P(('archive', 'dp'))
- grad_w_in: float32 [512, 384], replicated
- grad_bias: float32 [384], replicated
- grad_w_out: float32 [384, 128], replicated
The draws below stay inside these ranges and needn't reach their ends.
Inputs may be any that keep to these rules, and one draw needn't show every extreme that they name: `line_home`: storage row of each line id: each row once. The 48 mined ids of the queries of one device are distinct lines; at most 2 of them lie on one archive shard (shard line_home[id] // 8), and in every draw one shard receives exactly 2 of them from every device. `frame_count`: frame slots at and beyond a row's count are padding.
All inputs are finite; a program needn't handle non-finite values.
Results may differ from the reference program's by a relative error of at most 0.0064.
Values may be sent and summed in bfloat16 or wider, within the bound.
No kernel may reach another device: no remote copies, remote signals or barrier semaphores. Data moves between devices by JAX's collectives and lax.ppermute only.
A program may use at most 64 MiB of HBM per device.

```python
import math
from functools import partial
import jax
import jax.numpy as jnp
import numpy as np
from jax import lax

FEAT = 512
HID = 384
DIM = 128
QF = 32
LMAX = 128
MINED = 6
QRY_DEV = 8
LINES_DEV = 8
CAP = 2
QUERIES = 4096
LINES = 512


def mined_table(key):
    key_order = jax.random.fold_in(key, 101)
    key_owner = jax.random.fold_in(key, 102)
    key_warm = jax.random.fold_in(key, 103)
    key_noise = jax.random.fold_in(key, 104)
    key_shuffle = jax.random.fold_in(key, 105)
    key_base = jax.random.fold_in(key, 106)
    key_positive = jax.random.fold_in(key, 107)
    line_order = jax.random.permutation(key_order, LINES).astype(jnp.int32)
    line_rows = jnp.argsort(line_order).astype(jnp.int32)
    blocks = QUERIES // QRY_DEV
    owners = LINES // LINES_DEV
    slot_total = owners * CAP
    request_total = QRY_DEV * MINED
    slot_ids = jnp.arange(slot_total, dtype=jnp.int32)
    slot_owner = slot_ids // CAP
    hot_owner = jax.random.randint(key_owner, (), 0, owners)
    warm_owner = (jax.random.randint(key_warm, (owners,), 0, 4) == 0).astype(jnp.int32)
    noise_bits = jax.random.randint(key_noise, (blocks, slot_total), 0, 1 << 14)
    scores = noise_bits + warm_owner[slot_owner][None, :] * (1 << 14) + (slot_owner == hot_owner).astype(jnp.int32)[None, :] * (1 << 15)
    sort_keys = scores * slot_total + slot_ids[None, :]
    _, chosen = lax.top_k(sort_keys, request_total)
    shuffles = jax.vmap(partial(jax.random.permutation, x=request_total))(jax.random.split(key_shuffle, blocks))
    chosen = jnp.take_along_axis(chosen, shuffles.astype(jnp.int32), axis=1)
    owner_pick = chosen // CAP
    rank_pick = chosen % CAP
    base_slot = jax.random.randint(key_base, (blocks, owners), 0, LINES_DEV)
    local_slot = (jnp.take_along_axis(base_slot, owner_pick, axis=1) + rank_pick) % LINES_DEV
    line_ids = line_order[owner_pick * LINES_DEV + local_slot].reshape(QUERIES, MINED)
    positives = jax.random.randint(key_positive, (QUERIES,), 0, MINED)
    return (line_ids.astype(jnp.int32), line_rows, positives.astype(jnp.int32))


def frame_rows(base_key, length, normal_weight, uniform_weight, spread, row):
    sub_key = jax.random.fold_in(base_key, row)
    key_normal = jax.random.fold_in(sub_key, 0)
    normal_part = jnp.clip(jax.random.normal(key_normal, (length, FEAT), jnp.float32), -4.0, 4.0)
    return normal_part * normal_weight


def draw_mined(key, part):
    return mined_table(key)[0]


def draw_line_home(key, part):
    return mined_table(key)[1]


def draw_positive(key, part):
    return mined_table(key)[2]


def draw_line_frames(key, part):
    line_key = jax.random.fold_in(key, 202)
    rows = jnp.arange(LINES, dtype=jnp.int32)
    frames = jax.vmap(partial(frame_rows, line_key, LMAX, 0.7, 0.0, 0.0))(rows)
    return frames.astype(jnp.bfloat16)


def draw_query_frames(key, part):
    query_key = jax.random.fold_in(key, 303)
    rows = jnp.arange(QUERIES, dtype=jnp.int32)
    frames = jax.vmap(partial(frame_rows, query_key, QF, 0.7, 0.0, 0.0))(rows)
    return frames.astype(jnp.bfloat16)


def split_up(count, total, reach, slope):
    portions = [(1 << 20) // math.isqrt(rank ** slope) + 1 for rank in range(2, count + 1)]
    rest, given = total - reach - (count - 1), [1] * (count - 1)
    while rest > 0:
        candidates = [i for i in range(count - 1) if given[i] < reach]
        pool, budget = sum([portions[i] for i in candidates]), rest
        for i in candidates:
            extra = min(reach - given[i], max(1, budget * portions[i] // pool), rest)
            given[i] = given[i] + extra
            rest = rest - extra
    return np.array([reach] + given)


def ragged(rng, count, total, reach, lean):
    if count == 2:
        one = jax.random.randint(rng, (), max(1, total - reach), min(reach, total - 1) + 1)
        return jnp.stack([one, total - one])
    lengths = jnp.asarray(split_up(count, total, reach, lean), jnp.int32)
    couples = (count - 1) // 2
    source_of, sink = lengths[1:1 + 2 * couples:2], lengths[2:2 + 2 * couples:2]
    margin = jnp.minimum(source_of - 1, reach - sink)
    passed = jax.random.randint(jax.random.fold_in(rng, 1), (couples,), 0, 1 << 20) % (margin + 1)
    lengths = lengths.at[1:1 + 2 * couples:2].set(source_of - passed).at[2:2 + 2 * couples:2].set(sink + passed)
    return lengths[jax.random.permutation(jax.random.fold_in(rng, 2), count)]


def noise(key, extent, scale, bound, kind=jnp.bfloat16):
    return jnp.clip(scale * jax.random.normal(key, extent, jnp.float32), -bound, bound).astype(kind)


def setup_inputs(seed: int = 0) -> dict:
    splits = jax.random.split(jax.random.key(seed), 10)
    query_frames = draw_query_frames(jax.random.fold_in(splits[9], 71), 0)
    line_frames = draw_line_frames(jax.random.fold_in(splits[9], 71), 0)
    frame_count = ragged(splits[2], LINES, LINES * LMAX * 3 // 4, LMAX, 0).astype(jnp.int32)
    line_home = draw_line_home(jax.random.fold_in(splits[9], 71), 0)
    mined = draw_mined(jax.random.fold_in(splits[9], 71), 0)
    positive = draw_positive(jax.random.fold_in(splits[9], 71), 0)
    w_in = noise(splits[6], (FEAT, HID), FEAT ** -0.5, 0.25)
    bias_in = jnp.clip(jax.random.uniform(splits[7], (HID,), jnp.float32, -0.5, 0.5), -0.5, 0.5)
    w_out = noise(splits[8], (HID, DIM), HID ** -0.5, 0.3125)
    return {"query_frames": query_frames, "line_frames": line_frames, "frame_count": frame_count, "line_home": line_home, "mined": mined, "positive": positive, "w_in": w_in, "bias_in": bias_in, "w_out": w_out}


LOSS_SCALE = 4096.0
SCORE_SCALE = 4.0

def head_forward(frames, w_in, bias_in, w_out):
    pre_act = jnp.dot(frames, w_in, preferred_element_type=jnp.float32) + bias_in
    hidden = jax.nn.gelu(pre_act).astype(jnp.bfloat16)
    vectors = jnp.dot(hidden, w_out, preferred_element_type=jnp.float32).astype(jnp.bfloat16)
    return (pre_act, hidden, vectors)

def head_backward(frames, pre_act, hidden, grad_vec, w_out):
    highest = lax.Precision.HIGHEST
    grad_w_out = jnp.dot(hidden.astype(jnp.float32).T, grad_vec, precision=highest)
    grad_hidden = jnp.dot(grad_vec, w_out.astype(jnp.float32).T, precision=highest)
    _, pullback = jax.vjp(jax.nn.gelu, pre_act)
    grad_pre = pullback(grad_hidden)[0]
    grad_bias = lax.optimization_barrier(jnp.sum(grad_pre, axis=0))
    grad_w_in = jnp.dot(frames.astype(jnp.float32).T, grad_pre, precision=highest)
    return (grad_w_in, grad_bias, grad_w_out)

def match_forward(query_vec, line_vec, counts):
    vec_width = query_vec.shape[-1]
    slot_total = line_vec.shape[1]
    logits = jnp.einsum('nid,nfd->nif', query_vec.astype(jnp.float32), line_vec.astype(jnp.float32))
    logits = logits * (SCORE_SCALE / math.sqrt(vec_width))
    usable = jnp.arange(slot_total, dtype=jnp.int32)[None, None, :] < counts[:, None, None]
    logits = jnp.where(usable, logits, -jnp.inf)
    peak = lax.optimization_barrier(jnp.max(logits, axis=-1, keepdims=True))
    scaled = jnp.exp(logits - peak)
    totals = lax.optimization_barrier(jnp.sum(scaled, axis=-1, keepdims=True))
    log_total = peak[..., 0] + jnp.log(totals[..., 0])
    return (lax.optimization_barrier(jnp.mean(log_total, axis=-1)), scaled / totals)

def match_backward(weights, grad_match, query_vec, line_vec):
    query_len = query_vec.shape[1]
    vec_width = query_vec.shape[2]
    factor = grad_match * (SCORE_SCALE / (math.sqrt(vec_width) * query_len))
    score_grad = (weights * factor[:, None, None]).astype(jnp.bfloat16).astype(jnp.float32)
    grad_query = jnp.einsum('nif,nfd->nid', score_grad, line_vec.astype(jnp.float32))
    grad_line = jnp.einsum('nif,nid->nfd', score_grad, query_vec.astype(jnp.float32))
    return (grad_query, grad_line)

def cross_entropy(matches, positives, scale):
    peak = lax.optimization_barrier(jnp.max(matches, axis=1, keepdims=True))
    log_total = peak[:, 0] + jnp.log(lax.optimization_barrier(jnp.sum(jnp.exp(matches - peak), axis=1)))
    picked = jnp.arange(matches.shape[1], dtype=jnp.int32)[None, :] == positives[:, None]
    chosen = lax.optimization_barrier(jnp.sum(jnp.where(picked, matches, 0.0), axis=1))
    grads = (jnp.exp(matches - log_total[:, None]) - picked.astype(jnp.float32)) * scale
    return (log_total - chosen, grads)

def reference(query_frames, line_frames, frame_count, line_home, mined, positive, w_in, bias_in, w_out):
    query_flat = query_frames.reshape(QUERIES * QF, FEAT)
    line_flat = line_frames.reshape(LINES * LMAX, FEAT)
    query_pre, query_hidden, query_vec = head_forward(query_flat, w_in, bias_in, w_out)
    line_pre, line_hidden, line_vec = head_forward(line_flat, w_in, bias_in, w_out)
    query_vec = query_vec.reshape(QUERIES, QF, DIM)
    line_vec = line_vec.reshape(LINES, LMAX, DIM)
    line_rows = line_home[mined]
    counts = frame_count[line_rows]
    block_size = math.gcd(QUERIES, 256)
    block_total = QUERIES // block_size
    step_ids = jnp.arange(block_total, dtype=jnp.int32)

    def block_inputs(step_index):
        first_row = (step_index * block_size).astype(jnp.int32)
        queries = lax.dynamic_slice_in_dim(query_vec, first_row, block_size, 0)
        row_block = lax.dynamic_slice_in_dim(line_rows, first_row, block_size, 0).reshape(-1)
        count_block = lax.dynamic_slice_in_dim(counts, first_row, block_size, 0).reshape(-1)
        repeated = jnp.broadcast_to(queries[:, None], (block_size, MINED, QF, DIM)).reshape(block_size * MINED, QF, DIM)
        return (first_row, repeated, line_vec[row_block], count_block, row_block)

    def forward_block(step_index):
        first_row, repeated, lines_here, count_block, row_block = block_inputs(step_index)
        return match_forward(repeated, lines_here, count_block)[0].reshape(block_size, MINED)
    matches = lax.map(forward_block, step_ids).reshape(QUERIES, MINED)
    query_loss, grad_match = cross_entropy(matches, positive, LOSS_SCALE / QUERIES)

    def backward_block(grad_sum, step_index):
        first_row, repeated, lines_here, count_block, row_block = block_inputs(step_index)
        _, weights = match_forward(repeated, lines_here, count_block)
        match_part = lax.dynamic_slice_in_dim(grad_match, first_row, block_size, 0).reshape(-1)
        grad_query, grad_line = match_backward(weights, match_part, repeated, lines_here)
        grad_sum = grad_sum.at[row_block].add(grad_line)
        return (grad_sum, lax.optimization_barrier(jnp.sum(grad_query.reshape(block_size, MINED, QF, DIM), axis=1)))
    grad_lines, grad_queries = lax.scan(backward_block, jnp.zeros((LINES, LMAX, DIM), jnp.float32), step_ids)
    query_terms = head_backward(query_flat, query_pre, query_hidden, grad_queries.reshape(QUERIES * QF, DIM), w_out)
    line_terms = head_backward(line_flat, line_pre, line_hidden, grad_lines.reshape(LINES * LMAX, DIM), w_out)
    return (query_loss, query_terms[0] + line_terms[0], query_terms[1] + line_terms[1], query_terms[2] + line_terms[2])
```

```python
import math

import jax
import jax.numpy as jnp
from jax import lax
from jax.experimental import pallas as pl
from jax.experimental.pallas import tpu as pltpu
from jax.sharding import PartitionSpec as P

LOSS_SCALE = 4096.0
SCORE_SCALE = 4.0
LANES = 128
CAP = 2
HALF = LANES // CAP
META = 8
UNUSED = 100.0
FLOOR = -1e30
GELU_A = math.sqrt(2.0 / math.pi)
GELU_B = 0.044715
GROUP = 4

f32 = jnp.float32
bf16 = jnp.bfloat16


def dot(a, b, ca=1, cb=0):
    return lax.dot_general(a, b, (((ca,), (cb,)), ((), ())), preferred_element_type=f32)


def split2(x):
    hi = x.astype(bf16)
    return hi, (x - hi.astype(f32)).astype(bf16)


def call(body, outs, args, smem_count, scratch=(), flops=0, transcendentals=0):
    nbytes = sum(a.size * a.dtype.itemsize for a in list(args) + list(outs))
    vmem = pl.BlockSpec(memory_space=pltpu.VMEM)
    smem = pl.BlockSpec(memory_space=pltpu.SMEM)
    return pl.pallas_call(
        body,
        out_shape=tuple(outs),
        in_specs=[smem] * smem_count + [vmem] * (len(args) - smem_count),
        out_specs=tuple(vmem for _ in outs),
        scratch_shapes=list(scratch),
        compiler_params=pltpu.CompilerParams(vmem_limit_bytes=40 << 20),
        cost_estimate=pl.CostEstimate(
            flops=flops, bytes_accessed=nbytes, transcendentals=transcendentals
        ),
    )(*args)


def gelu_parts(pre):
    t = jnp.tanh(GELU_A * (pre + GELU_B * pre * pre * pre))
    return t, (0.5 * pre * (1.0 + t)).astype(bf16)


def ask_kernel(mined, home, positive, x, w_in, bias, w_out, send, vec, rid, code, count):
    query_count, mined_count = mined.shape
    owner_count = send.shape[0]
    query_len = x.shape[0] // query_count
    line_count = home.shape[0] // owner_count
    rows = CAP * query_len
    _, hidden = gelu_parts(dot(x[...], w_in[...]) + bias[...])
    vec[...] = dot(hidden, w_out[...]).astype(bf16)
    send[...] = jnp.zeros(send.shape, bf16)

    def clear(owner, carry):
        count[owner] = 0
        for c in range(CAP):
            rid[c, owner] = int(UNUSED)
            code[c, owner] = int(UNUSED)
        return carry

    lax.fori_loop(0, owner_count, clear, 0)

    def place(query, carry):
        block = vec[pl.ds(pl.multiple_of(query * query_len, query_len), query_len), :]
        for j in range(mined_count):
            row = home[mined[query, j]]
            owner = row // line_count
            rank = count[owner]
            count[owner] = rank + 1
            rid[rank, owner] = row - owner * line_count
            code[rank, owner] = query + jnp.where(positive[query] == j, 8, 0)
            send[owner, pl.ds(pl.multiple_of(rank * query_len, query_len), query_len), :] = block
        return carry

    lax.fori_loop(0, query_count, place, 0)
    sub = lax.broadcasted_iota(jnp.int32, (META, LANES), 0)

    def label(owner, carry):
        tile = jnp.where(
            sub == 0,
            rid[0, owner],
            jnp.where(sub == 1, rid[1, owner], jnp.where(sub == 2, code[0, owner], code[1, owner])),
        )
        send[owner, rows : rows + META, :] = tile.astype(f32).astype(bf16)
        return carry

    lax.fori_loop(0, owner_count, label, 0)


def head_kernel(xl, xq, w_in, bias, w_out, line_vec, hidden_all, slope_t):
    step = 256
    line_frames = xl.shape[0]
    for first in range(0, line_frames + xq.shape[0], step):
        if first < line_frames:
            x = xl[first : first + step, :]
        else:
            x = xq[first - line_frames : first - line_frames + step, :]
        size = x.shape[0]
        pre = dot(x, w_in[...]) + bias[...]
        t, hidden = gelu_parts(pre)
        slope = 0.5 * (1.0 + t) + 0.5 * pre * (1.0 - t * t) * GELU_A * (
            1.0 + 3.0 * GELU_B * pre * pre
        )
        hidden_all[first : first + size, :] = hidden
        slope_t[:, first : first + size] = slope.T
        if first < line_frames:
            line_vec[first : first + size, :] = dot(hidden, w_out[...]).astype(bf16)


def spread(meta, first, query_len):
    parts = []
    for b in range(meta.shape[0]):
        for c in range(CAP):
            parts.append(jnp.broadcast_to(meta[b, first + c : first + c + 1, :], (query_len, LANES)))
    return jnp.concatenate(parts, axis=0)


def match_kernel(place, counts, got, line_vec, send, weights, own):
    owner_count = got.shape[0]
    rows = got.shape[1] - META
    query_len = rows // CAP
    line_total = line_vec.shape[0]
    line_count = line_total // LANES
    scale = SCORE_SCALE / math.sqrt(line_vec.shape[1])
    lines = line_vec[...]
    lane1 = lax.broadcasted_iota(jnp.int32, (1, LANES), 1)
    pads = [
        jnp.where(lane1 < counts[place[0] * line_count + r], 0.0, FLOOR) for r in range(line_count)
    ]
    total = GROUP * rows
    lane = lax.broadcasted_iota(jnp.int32, (total, LANES), 1)
    row = lax.broadcasted_iota(jnp.int32, (total, LANES), 0)
    target = row // rows + HALF * ((row // query_len) % CAP)

    def step(g, carry):
        match_row, code_row = carry
        first = g * GROUP
        queries = got[pl.ds(first, GROUP), 0:rows, :].reshape(total, LANES)
        meta = got[pl.ds(first, GROUP), rows : rows + META, :].astype(f32)
        rid = spread(meta, 0, query_len)
        logits = dot(queries, lines, 1, 1) * scale
        chosen = jnp.zeros((total, LANES), f32)
        for r in range(line_count):
            part = logits[:, r * LANES : (r + 1) * LANES] + pads[r]
            chosen = jnp.where(rid == r, part, chosen)
        peak = jnp.max(chosen, axis=1, keepdims=True)
        scaled = jnp.exp(chosen - peak)
        totals = jnp.sum(scaled, axis=1, keepdims=True)
        log_total = peak + jnp.log(totals)
        weight = (scaled * (1.0 / totals)).astype(bf16)
        weights[pl.ds(first, GROUP)] = weight.reshape(GROUP, rows, LANES)
        rid_b = rid.astype(bf16)
        zero = jnp.zeros((total, LANES), bf16)
        wide = jnp.concatenate(
            [jnp.where(rid_b == r, weight, zero) for r in range(line_count)], axis=1
        )
        send[pl.ds(first, GROUP), 0:rows, :] = (
            dot(wide, lines).astype(bf16).reshape(GROUP, rows, LANES)
        )
        mine = (lane == target + first) & (rid < line_count)
        match_row += jnp.sum(
            jnp.where(mine, log_total * (1.0 / query_len), 0.0), axis=0, keepdims=True
        )
        for b in range(GROUP):
            for c in range(CAP):
                code_row = jnp.where(
                    lane1 == first + b + HALF * c, meta[b, 2 + c : 3 + c, :], code_row
                )
        return match_row, code_row

    match_row, code_row = lax.fori_loop(
        0,
        owner_count // GROUP,
        step,
        (jnp.zeros((1, LANES), f32), jnp.full((1, LANES), UNUSED, f32)),
    )
    sub = lax.broadcasted_iota(jnp.int32, (META, LANES), 0)
    own[...] = jnp.where(sub == 0, match_row, code_row)
    high = match_row.astype(bf16).astype(f32)
    middle = (match_row - high).astype(bf16).astype(f32)
    low = match_row - high - middle
    tile = jnp.where(
        sub == 0, high, jnp.where(sub == 1, middle, jnp.where(sub == 2, low, code_row))
    ).astype(bf16)

    def label(b, carry):
        send[b, rows : rows + META, :] = tile
        return carry

    lax.fori_loop(0, owner_count, label, 0)


def grad_kernel(
    place, back, got, weights, own, xl, xq, hidden_all, slope_t, w_out, loss, grads, own_scale, ask_scale, line_acc, query_acc, *, loss_factor
):
    owner_count = got.shape[0]
    rows = got.shape[1] - META
    query_len = rows // CAP
    line_total = xl.shape[0]
    line_count = line_total // LANES
    query_frames = xq.shape[0]
    vec_width = w_out.shape[1]
    hid = w_out.shape[0]
    me = place[0]

    shape3 = (owner_count, META, LANES)
    lane3 = lax.broadcasted_iota(jnp.int32, shape3, 2)
    sub3 = lax.broadcasted_iota(jnp.int32, shape3, 1)
    owner3 = lax.broadcasted_iota(jnp.int32, shape3, 0)
    subf = sub3.astype(f32)
    meta = back[:, rows : rows + META, :].astype(f32)
    match = jnp.sum(jnp.where(sub3 < 3, meta, 0.0), axis=1, keepdims=True)
    code = jnp.sum(jnp.where(sub3 == 3, meta, 0.0), axis=1, keepdims=True)
    match = jnp.broadcast_to(match, shape3)
    code = jnp.broadcast_to(code, shape3)
    is_pos = (code >= 8.0) & (code < 16.0)
    query_of = jnp.where(is_pos, code - 8.0, code)
    here = query_of == subf
    peak = jnp.max(jnp.where(here, match, FLOOR), axis=0)
    peak = jnp.maximum(peak, pltpu.roll(peak, HALF, 1))
    total = jnp.sum(jnp.where(here, jnp.exp(match - peak[None]), 0.0), axis=0)
    total = total + pltpu.roll(total, HALF, 1)
    chosen = jnp.sum(jnp.where(here & is_pos, match, 0.0), axis=0)
    chosen = chosen + pltpu.roll(chosen, HALF, 1)
    log_total = peak + jnp.log(jnp.where(total > 0.0, total, 1.0))
    lane2 = lax.broadcasted_iota(jnp.int32, (META, LANES), 1)
    sub2 = lax.broadcasted_iota(jnp.int32, (META, LANES), 0).astype(f32)
    picked = jnp.sum(jnp.where(lane2 == me, log_total - chosen, 0.0), axis=1, keepdims=True)
    loss[...] = jnp.broadcast_to(picked, (META, LANES))

    factor = loss_factor * SCORE_SCALE / (math.sqrt(vec_width) * query_len)

    own_match = own[0:1, :]
    own_code = own[1:2, :]
    own_pos = (own_code >= 8.0) & (own_code < 16.0)
    own_query = jnp.where(own_pos, own_code - 8.0, own_code)
    own_grad = jnp.exp(jnp.minimum(own_match - log_total, 0.0)) - jnp.where(own_pos, 1.0, 0.0)
    own_grad = factor * jnp.sum(jnp.where(own_query == sub2, own_grad, 0.0), axis=0, keepdims=True)
    aim = lane3 == owner3 + HALF * sub3
    own_scale[...] = jnp.broadcast_to(
        jnp.sum(
            jnp.where(aim, jnp.broadcast_to(own_grad[None], shape3), 0.0), axis=2, keepdims=True
        ),
        shape3,
    )

    ask_grad = jnp.exp(jnp.minimum(match - log_total[None], 0.0)) - jnp.where(is_pos, 1.0, 0.0)
    ask_grad = factor * jnp.sum(jnp.where(here, ask_grad, 0.0), axis=1, keepdims=True)
    both = jnp.where(sub3 < CAP, jnp.broadcast_to(ask_grad, shape3), query_of)
    aim = lane3 == me + HALF * (sub3 % CAP)
    ask_scale[...] = jnp.broadcast_to(
        jnp.sum(jnp.where(aim, both, 0.0), axis=2, keepdims=True), shape3
    )

    size = GROUP * rows
    line_acc[...] = jnp.zeros(line_acc.shape, f32)
    query_acc[...] = jnp.zeros(query_acc.shape, f32)
    frame = (lax.broadcasted_iota(jnp.int32, (size, LANES), 0) % query_len).astype(f32)
    lane = lax.broadcasted_iota(jnp.int32, (size, LANES), 1).astype(f32)
    zero = jnp.zeros((size, LANES), bf16)
    one = jnp.ones((size, LANES), bf16)

    def step(g, carry):
        first = g * GROUP
        queries = got[pl.ds(first, GROUP), 0:rows, :].reshape(size, LANES)
        rid = spread(got[pl.ds(first, GROUP), rows : rows + META, :].astype(f32), 0, query_len)
        rid = rid.astype(bf16)
        scale = spread(own_scale[pl.ds(first, GROUP)], 0, query_len)
        weight = weights[pl.ds(first, GROUP)].reshape(size, LANES).astype(f32)
        score = (weight * scale).astype(bf16)
        wide = jnp.concatenate(
            [jnp.where(rid == r, score, zero) for r in range(line_count)], axis=1
        )
        line_acc[...] += dot(queries, wide, 0, 0)

        labels = ask_scale[pl.ds(first, GROUP)]
        scale = spread(labels, 0, query_len)
        target = spread(labels, CAP, query_len) * float(query_len) + frame
        pulled = back[pl.ds(first, GROUP), 0:rows, :].reshape(size, LANES).astype(f32)
        pulled = (pulled * scale).astype(bf16)
        wide = jnp.concatenate(
            [
                jnp.where(target == lane + float(k), one, zero)
                for k in range(0, query_acc.shape[1], LANES)
            ],
            axis=1,
        )
        query_acc[...] += dot(pulled, wide, 0, 0)
        return carry

    lax.fori_loop(0, owner_count // GROUP, step, 0)

    grad_in = None
    grad_out = None
    grad_bias = None
    ones = jnp.ones((META, 1), bf16)
    spans = ((line_acc, xl, 0, line_total), (query_acc, xq, line_total, query_frames))
    for acc, x, first, span in spans:
        g_hi, g_lo = split2(acc[:, 0:span])
        grad_hidden = dot(w_out[...], g_hi) + dot(w_out[...], g_lo)
        p_hi, p_lo = split2(grad_hidden * slope_t[:, first : first + span])
        hidden = hidden_all[first : first + span, :]
        ones = jnp.ones((META, span), bf16)
        part_in = dot(p_hi, x[...]) + dot(p_lo, x[...])
        part_out = dot(g_hi, hidden) + dot(g_lo, hidden)
        part_bias = dot(ones, p_hi, 1, 1) + dot(ones, p_lo, 1, 1)
        grad_in = part_in if grad_in is None else grad_in + part_in
        grad_out = part_out if grad_out is None else grad_out + part_out
        grad_bias = part_bias if grad_bias is None else grad_bias + part_bias
    base = 0
    for k in range(0, x.shape[1], LANES):
        grads[base : base + hid, :] = grad_in[:, k : k + LANES].astype(bf16)
        base += hid
    for k in range(0, hid, LANES):
        grads[base : base + vec_width, :] = grad_out[:, k : k + LANES].astype(bf16)
        base += vec_width
    rest = grads.shape[0] - base
    sub = lax.broadcasted_iota(jnp.int32, (rest, LANES), 0)
    tile = jnp.zeros((rest, LANES), f32)
    for i, k in enumerate(range(0, hid, LANES)):
        tile = jnp.where(sub == i, grad_bias[0:1, k : k + LANES], tile)
    grads[base:, :] = tile.astype(bf16)


def sum_archive_kernel(got, send):
    part = got[0].astype(f32)
    for k in range(1, got.shape[0]):
        part = part + got[k].astype(f32)
    for k in range(send.shape[0]):
        send[k] = part


def sum_dp_kernel(got, send):
    part = got[0]
    for k in range(1, got.shape[0]):
        part = part + got[k]
    part = part.astype(bf16)
    for k in range(send.shape[0]):
        send[k] = part


def unpack_kernel(got, grad_in, grad_bias, grad_out):
    feat, hid = grad_in.shape
    vec_width = grad_out.shape[1]
    base = 0
    for k in range(0, feat, LANES):
        grad_in[k : k + LANES, :] = got[base : base + hid, :].astype(f32).T
        base += hid
    for k in range(0, hid, LANES):
        grad_out[k : k + LANES, :] = got[base : base + vec_width, :].astype(f32).T
        base += vec_width
    tail = got[base : base + 16, :].astype(f32)
    for i, k in enumerate(range(0, hid, LANES)):
        grad_bias[0:1, k : k + LANES] = tail[i : i + 1, :]


def exchange(x, axis):
    return lax.all_to_all(x, axis, split_axis=0, concat_axis=0, tiled=True)


def shape_of(shape, dtype):
    return jax.ShapeDtypeStruct(shape, dtype)


def local(query_frames, line_frames, frame_count, line_home, mined, positive, w_in, bias_in, w_out):
    query_count, query_len, feat = query_frames.shape
    line_count, line_len, _ = line_frames.shape
    hid, vec_width = w_out.shape
    owner_count = lax.axis_size("archive")
    dp_count = lax.axis_size("dp")
    loss_factor = LOSS_SCALE / (query_count * owner_count * dp_count)
    frames_q = query_count * query_len
    frames_l = line_count * line_len
    frames = frames_q + frames_l
    rows = CAP * query_len
    xq = query_frames.reshape(frames_q, feat)
    xl = line_frames.reshape(frames_l, feat)
    bias = bias_in.reshape(1, hid)
    place = lax.axis_index("archive").astype(jnp.int32).reshape(1)
    wire = shape_of((owner_count, rows + META, vec_width), bf16)
    head_flops = 2 * hid * (feat + vec_width)

    (asked,) = call(
        ask_kernel,
        [wire],
        [mined, line_home, positive, xq, w_in, bias, w_out],
        3,
        [
            pltpu.VMEM((frames_q, vec_width), bf16),
            pltpu.SMEM((CAP, owner_count), jnp.int32),
            pltpu.SMEM((CAP, owner_count), jnp.int32),
            pltpu.SMEM((owner_count,), jnp.int32),
        ],
        flops=frames_q * head_flops,
    )
    got = exchange(asked, "archive")
    line_vec, hidden_all, slope_t = call(
        head_kernel,
        [
            shape_of((frames_l, vec_width), bf16),
            shape_of((frames, hid), bf16),
            shape_of((hid, frames), f32),
        ],
        [xl, xq, w_in, bias, w_out],
        0,
        flops=frames * head_flops,
        transcendentals=frames * hid,
    )
    match_flops = 2 * owner_count * rows * frames_l * vec_width
    answer, weights, own = call(
        match_kernel,
        [
            wire,
            shape_of((owner_count, rows, line_len), bf16),
            shape_of((META, LANES), f32),
        ],
        [place, frame_count, got, line_vec],
        2,
        flops=2 * match_flops,
    )
    back = exchange(answer, "archive")
    flat_rows = owner_count * 16 * -(-(feat * hid + hid * vec_width + hid) // (LANES * 16 * owner_count))

    def grads_body(*refs):
        grad_kernel(*refs, loss_factor=loss_factor)

    loss, partial = call(
        grads_body,
        [shape_of((META, LANES), f32), shape_of((flat_rows, LANES), bf16)],
        [place, back, got, weights, own, xl, xq, hidden_all, slope_t, w_out],
        1,
        [
            pltpu.VMEM((owner_count, META, LANES), f32),
            pltpu.VMEM((owner_count, META, LANES), f32),
            pltpu.VMEM((vec_width, frames_l), f32),
            pltpu.VMEM((vec_width, frames_q), f32),
        ],
        flops=match_flops + 4 * frames * head_flops,
    )
    share = flat_rows // owner_count
    parts = exchange(partial.reshape(owner_count, share, LANES), "archive")
    (sums,) = call(sum_archive_kernel, [shape_of((dp_count, share, LANES), f32)], [parts], 0)
    sums = exchange(sums, "dp")
    (whole,) = call(sum_dp_kernel, [shape_of((owner_count, share, LANES), bf16)], [sums], 0)
    whole = exchange(whole, "archive")
    grad_in, grad_bias, grad_out = call(
        unpack_kernel,
        [shape_of((feat, hid), f32), shape_of((1, hid), f32), shape_of((hid, vec_width), f32)],
        [whole.reshape(flat_rows, LANES)],
        0,
    )
    return (loss[:query_count, 0], grad_in, grad_bias.reshape(hid), grad_out)


def solution(mesh):
    placed = (
        P(("archive", "dp"), None, None),
        P("archive", None, None),
        P(),
        P(),
        P(("archive", "dp"), None),
        P(("archive", "dp")),
        P(),
        P(),
        P(),
    )
    return jax.shard_map(
        local,
        mesh=mesh,
        in_specs=placed,
        out_specs=(P(("archive", "dp")), P(), P(), P()),
        check_vma=False,
    )
```

```python
import math

import jax
import jax.numpy as jnp
from jax import lax
from jax.experimental import pallas as pl
from jax.experimental.pallas import tpu as pltpu
from jax.sharding import Mesh, PartitionSpec as P

LOSS_SCALE = 4096.0
SCORE_SCALE = 4.0
LANES = 128
CAP = 2
HALF = LANES // CAP
META = 8
UNUSED = 100.0
FLOOR = -1e30
GELU_A = math.sqrt(2.0 / math.pi)
GELU_B = 0.044715
GROUP = 4
ARCHIVE = ("chip", "core")

f32 = jnp.float32
bf16 = jnp.bfloat16


def dot(a, b, ca=1, cb=0):
    return lax.dot_general(a, b, (((ca,), (cb,)), ((), ())), preferred_element_type=f32)


def split2(x):
    hi = x.astype(bf16)
    return hi, (x - hi.astype(f32)).astype(bf16)


def split3(x):
    hi = x.astype(bf16).astype(f32)
    mid = (x - hi).astype(bf16).astype(f32)
    return hi, mid, (x - hi - mid).astype(bf16).astype(f32)


def call(body, outs, args, smem_count, scratch=(), flops=0, transcendentals=0, where=pltpu.VMEM):
    nbytes = sum(a.size * a.dtype.itemsize for a in list(args) + list(outs))
    vmem = pl.BlockSpec(memory_space=pltpu.VMEM)
    smem = pl.BlockSpec(memory_space=pltpu.SMEM)
    rest = pl.BlockSpec(memory_space=where)
    return pl.pallas_call(
        body,
        out_shape=tuple(outs),
        in_specs=[smem] * smem_count + [rest] * (len(args) - smem_count),
        out_specs=tuple(vmem for _ in outs),
        scratch_shapes=list(scratch),
        compiler_params=pltpu.CompilerParams(vmem_limit_bytes=40 << 20),
        cost_estimate=pl.CostEstimate(
            flops=flops, bytes_accessed=nbytes, transcendentals=transcendentals
        ),
    )(*args)


def gelu_parts(pre):
    t = jnp.tanh(GELU_A * (pre + GELU_B * pre * pre * pre))
    return t, (0.5 * pre * (1.0 + t)).astype(bf16)


def ask_kernel(
    mined, home, positive, x_hbm, w_in_hbm, bias_hbm, w_out_hbm, send, x, w_in, bias, w_out, vec, rid, code, count, goal, sems
):
    query_count, mined_count = mined.shape
    owner_count = send.shape[0]
    query_len = x.shape[0] // query_count
    line_count = home.shape[0] // owner_count
    rows = CAP * query_len
    pairs = ((x_hbm, x), (w_in_hbm, w_in), (bias_hbm, bias), (w_out_hbm, w_out))
    copies = [pltpu.make_async_copy(a, b, sems.at[i]) for i, (a, b) in enumerate(pairs)]
    for copy in copies:
        copy.start()

    def clear(owner, carry):
        count[owner] = 0
        for c in range(CAP):
            rid[c, owner] = int(UNUSED)
            code[c, owner] = int(UNUSED)
        return carry

    lax.fori_loop(0, owner_count, clear, 0, unroll=8)

    def assign(query, carry):
        for j in range(mined_count):
            row = home[mined[query, j]]
            owner = row // line_count
            rank = count[owner]
            count[owner] = rank + 1
            rid[rank, owner] = row - owner * line_count
            code[rank, owner] = query + jnp.where(positive[query] == j, 8, 0)
            goal[query, j] = owner * CAP + rank
        return carry

    lax.fori_loop(0, query_count, assign, 0)
    send[...] = jnp.zeros(send.shape, bf16)
    sub = lax.broadcasted_iota(jnp.int32, (META, LANES), 0)

    def label(owner, carry):
        tile = jnp.where(
            sub == 0,
            rid[0, owner],
            jnp.where(sub == 1, rid[1, owner], jnp.where(sub == 2, code[0, owner], code[1, owner])),
        )
        send[owner, rows : rows + META, :] = tile.astype(f32).astype(bf16)
        return carry

    lax.fori_loop(0, owner_count, label, 0, unroll=8)
    for copy in copies:
        copy.wait()
    _, hidden = gelu_parts(dot(x[...], w_in[...]) + bias[...])
    vec[...] = dot(hidden, w_out[...]).astype(bf16)

    def place(query, carry):
        block = vec[pl.ds(pl.multiple_of(query * query_len, query_len), query_len), :]
        for j in range(mined_count):
            owner = goal[query, j] // CAP
            rank = goal[query, j] % CAP
            send[owner, pl.ds(pl.multiple_of(rank * query_len, query_len), query_len), :] = block
        return carry

    lax.fori_loop(0, query_count, place, 0)


def head_kernel(xl, xq, w_in, bias, w_out, line_vec, hidden_all, slope_t, mean):
    step = 256
    line_frames = xl.shape[0]
    total = jnp.zeros((1, hidden_all.shape[1]), f32)
    for first in range(0, line_frames + xq.shape[0], step):
        if first < line_frames:
            x = xl[first : first + step, :]
        else:
            x = xq[first - line_frames : first - line_frames + step, :]
        size = x.shape[0]
        pre = dot(x, w_in[...]) + bias[...]
        t, hidden = gelu_parts(pre)
        slope = 0.5 * (1.0 + t) + 0.5 * pre * (1.0 - t * t) * GELU_A * (
            1.0 + 3.0 * GELU_B * pre * pre
        )
        hidden_all[first : first + size, :] = hidden
        slope_t[:, first : first + size] = slope.T
        if first < line_frames:
            line_vec[first : first + size, :] = dot(hidden, w_out[...]).astype(bf16)
            total += jnp.sum(hidden.astype(f32), axis=0, keepdims=True)
    mean[...] = jnp.zeros(mean.shape, f32)
    for i, k in enumerate(range(0, hidden_all.shape[1], LANES)):
        mean[4 + i : 5 + i, :] = total[:, k : k + LANES] * (1.0 / line_frames)


def spread(meta, first, query_len):
    parts = []
    for b in range(meta.shape[0]):
        for c in range(CAP):
            parts.append(jnp.broadcast_to(meta[b, first + c : first + c + 1, :], (query_len, LANES)))
    return jnp.concatenate(parts, axis=0)


def match_kernel(place, counts, got, line_vec, mean, send, weights, own):
    owner_count = got.shape[0]
    rows = got.shape[1] - META
    query_len = rows // CAP
    line_total = line_vec.shape[0]
    line_count = line_total // LANES
    scale = SCORE_SCALE / math.sqrt(line_vec.shape[1])
    lines = line_vec[...]
    lane1 = lax.broadcasted_iota(jnp.int32, (1, LANES), 1)
    pads = [
        jnp.where(lane1 < counts[place[0] * line_count + r], 0.0, FLOOR) for r in range(line_count)
    ]
    total = GROUP * rows
    lane = lax.broadcasted_iota(jnp.int32, (total, LANES), 1)
    row = lax.broadcasted_iota(jnp.int32, (total, LANES), 0)
    target = row // rows + HALF * ((row // query_len) % CAP)

    def step(g, carry):
        match_row, code_row = carry
        first = g * GROUP
        queries = got[pl.ds(first, GROUP), 0:rows, :].reshape(total, LANES)
        meta = got[pl.ds(first, GROUP), rows : rows + META, :].astype(f32)
        rid = spread(meta, 0, query_len)
        logits = dot(queries, lines, 1, 1) * scale
        chosen = jnp.zeros((total, LANES), f32)
        for r in range(line_count):
            part = logits[:, r * LANES : (r + 1) * LANES] + pads[r]
            chosen = jnp.where(rid == r, part, chosen)
        peak = jnp.max(chosen, axis=1, keepdims=True)
        scaled = jnp.exp(chosen - peak)
        totals = jnp.sum(scaled, axis=1, keepdims=True)
        log_total = peak + jnp.log(totals)
        weight = (scaled * (1.0 / totals)).astype(bf16)
        weights[pl.ds(first, GROUP)] = weight.reshape(GROUP, rows, LANES)
        rid_b = rid.astype(bf16)
        zero = jnp.zeros((total, LANES), bf16)
        wide = jnp.concatenate(
            [jnp.where(rid_b == r, weight, zero) for r in range(line_count)], axis=1
        )
        send[pl.ds(first, GROUP), 0:rows, :] = (
            dot(wide, lines).astype(bf16).reshape(GROUP, rows, LANES)
        )
        mine = (lane == target + first) & (rid < line_count)
        match_row += jnp.sum(
            jnp.where(mine, log_total * (1.0 / query_len), 0.0), axis=0, keepdims=True
        )
        for b in range(GROUP):
            for c in range(CAP):
                code_row = jnp.where(
                    lane1 == first + b + HALF * c, meta[b, 2 + c : 3 + c, :], code_row
                )
        return match_row, code_row

    match_row, code_row = lax.fori_loop(
        0,
        owner_count // GROUP,
        step,
        (jnp.zeros((1, LANES), f32), jnp.full((1, LANES), UNUSED, f32)),
        unroll=2,
    )
    sub = lax.broadcasted_iota(jnp.int32, (META, LANES), 0)
    own[...] = jnp.where(sub == 0, match_row, code_row)
    high = match_row.astype(bf16).astype(f32)
    middle = (match_row - high).astype(bf16).astype(f32)
    low = match_row - high - middle
    tile = jnp.where(
        sub == 0, high, jnp.where(sub == 1, middle, jnp.where(sub == 2, low, code_row))
    )
    tile = jnp.where(sub < 4, tile, mean[...]).astype(bf16)

    def label(b, carry):
        send[b, rows : rows + META, :] = tile
        return carry

    lax.fori_loop(0, owner_count, label, 0)


def grad_kernel(
    place, back, got, weights, own, xl, xq, hidden_all, slope_t, w_out, loss, keep, give, base_row, grads, own_scale, ask_scale, line_acc, query_acc, *, loss_factor
):
    owner_count = got.shape[0]
    rows = got.shape[1] - META
    query_len = rows // CAP
    line_total = xl.shape[0]
    line_count = line_total // LANES
    query_frames = xq.shape[0]
    vec_width = w_out.shape[1]
    hid = w_out.shape[0]
    me = place[0]

    shape3 = (owner_count, META, LANES)
    lane3 = lax.broadcasted_iota(jnp.int32, shape3, 2)
    sub3 = lax.broadcasted_iota(jnp.int32, shape3, 1)
    owner3 = lax.broadcasted_iota(jnp.int32, shape3, 0)
    subf = sub3.astype(f32)
    meta = back[:, rows : rows + META, :].astype(f32)
    match = jnp.sum(jnp.where(sub3 < 3, meta, 0.0), axis=1, keepdims=True)
    code = jnp.sum(jnp.where(sub3 == 3, meta, 0.0), axis=1, keepdims=True)
    match = jnp.broadcast_to(match, shape3)
    code = jnp.broadcast_to(code, shape3)
    is_pos = (code >= 8.0) & (code < 16.0)
    query_of = jnp.where(is_pos, code - 8.0, code)
    here = query_of == subf
    peak = jnp.max(jnp.where(here, match, FLOOR), axis=0)
    peak = jnp.maximum(peak, pltpu.roll(peak, HALF, 1))
    total = jnp.sum(jnp.where(here, jnp.exp(match - peak[None]), 0.0), axis=0)
    total = total + pltpu.roll(total, HALF, 1)
    chosen = jnp.sum(jnp.where(here & is_pos, match, 0.0), axis=0)
    chosen = chosen + pltpu.roll(chosen, HALF, 1)
    log_total = peak + jnp.log(jnp.where(total > 0.0, total, 1.0))
    lane2 = lax.broadcasted_iota(jnp.int32, (META, LANES), 1)
    sub2 = lax.broadcasted_iota(jnp.int32, (META, LANES), 0).astype(f32)
    picked = jnp.sum(jnp.where(lane2 == me, log_total - chosen, 0.0), axis=1, keepdims=True)
    loss[...] = jnp.broadcast_to(picked, (META, LANES))

    factor = loss_factor * SCORE_SCALE / (math.sqrt(vec_width) * query_len)

    own_match = own[0:1, :]
    own_code = own[1:2, :]
    own_pos = (own_code >= 8.0) & (own_code < 16.0)
    own_query = jnp.where(own_pos, own_code - 8.0, own_code)
    own_grad = jnp.exp(jnp.minimum(own_match - log_total, 0.0)) - jnp.where(own_pos, 1.0, 0.0)
    own_grad = factor * jnp.sum(jnp.where(own_query == sub2, own_grad, 0.0), axis=0, keepdims=True)
    aim = lane3 == owner3 + HALF * sub3
    own_scale[...] = jnp.broadcast_to(
        jnp.sum(
            jnp.where(aim, jnp.broadcast_to(own_grad[None], shape3), 0.0), axis=2, keepdims=True
        ),
        shape3,
    )

    ask_grad = jnp.exp(jnp.minimum(match - log_total[None], 0.0)) - jnp.where(is_pos, 1.0, 0.0)
    ask_grad = factor * jnp.sum(jnp.where(here, ask_grad, 0.0), axis=1, keepdims=True)
    both = jnp.where(sub3 < CAP, jnp.broadcast_to(ask_grad, shape3), query_of)
    aim = lane3 == me + HALF * (sub3 % CAP)
    ask_scale[...] = jnp.broadcast_to(
        jnp.sum(jnp.where(aim, both, 0.0), axis=2, keepdims=True), shape3
    )

    size = GROUP * rows
    line_acc[...] = jnp.zeros(line_acc.shape, f32)
    query_acc[...] = jnp.zeros(query_acc.shape, f32)
    frame = (lax.broadcasted_iota(jnp.int32, (size, LANES), 0) % query_len).astype(f32)
    lane = lax.broadcasted_iota(jnp.int32, (size, LANES), 1).astype(f32)
    zero = jnp.zeros((size, LANES), bf16)
    one = jnp.ones((size, LANES), bf16)

    def step(g, carry):
        first = g * GROUP
        queries = got[pl.ds(first, GROUP), 0:rows, :].reshape(size, LANES)
        rid = spread(got[pl.ds(first, GROUP), rows : rows + META, :].astype(f32), 0, query_len)
        rid = rid.astype(bf16)
        scale = spread(own_scale[pl.ds(first, GROUP)], 0, query_len)
        weight = weights[pl.ds(first, GROUP)].reshape(size, LANES).astype(f32)
        score = (weight * scale).astype(bf16)
        wide = jnp.concatenate(
            [jnp.where(rid == r, score, zero) for r in range(line_count)], axis=1
        )
        line_acc[...] += dot(queries, wide, 0, 0)

        labels = ask_scale[pl.ds(first, GROUP)]
        scale = spread(labels, 0, query_len)
        target = spread(labels, CAP, query_len) * float(query_len) + frame
        pulled = back[pl.ds(first, GROUP), 0:rows, :].reshape(size, LANES).astype(f32)
        pulled = (pulled * scale).astype(bf16)
        wide = jnp.concatenate(
            [
                jnp.where(target == lane + float(k), one, zero)
                for k in range(0, query_acc.shape[1], LANES)
            ],
            axis=1,
        )
        query_acc[...] += dot(pulled, wide, 0, 0)
        return carry

    lax.fori_loop(0, owner_count // GROUP, step, 0)

    grad_in = None
    grad_out = None
    grad_bias = None
    vec_sum = None
    shared = jnp.sum(jnp.where(sub3 >= 4, meta, 0.0), axis=0) * (1.0 / owner_count)
    shared = shared.astype(bf16).astype(f32)
    shared = jnp.concatenate([shared[4 + i : 5 + i, :] for i in range(hid // LANES)], axis=1)
    base_row[...] = jnp.broadcast_to(shared, base_row.shape)
    spans = ((line_acc, xl, 0, line_total), (query_acc, xq, line_total, query_frames))
    for acc, x, first, span in spans:
        g_hi, g_lo = split2(acc[:, 0:span])
        grad_hidden = dot(w_out[...], g_hi) + dot(w_out[...], g_lo)
        p_hi, p_lo = split2(grad_hidden * slope_t[:, first : first + span])
        hidden = hidden_all[first : first + span, :]
        ones = jnp.ones((META, span), bf16)
        part_in = dot(p_hi, x[...]) + dot(p_lo, x[...])
        part_out = dot(g_hi, hidden) + dot(g_lo, hidden)
        part_out -= jnp.sum(g_hi.astype(f32) + g_lo.astype(f32), axis=1, keepdims=True) * shared
        part_sum = dot(ones, g_hi, 1, 1) + dot(ones, g_lo, 1, 1)
        vec_sum = part_sum if vec_sum is None else vec_sum + part_sum
        part_bias = dot(ones, p_hi, 1, 1) + dot(ones, p_lo, 1, 1)
        grad_in = part_in if grad_in is None else grad_in + part_in
        grad_out = part_out if grad_out is None else grad_out + part_out
        grad_bias = part_bias if grad_bias is None else grad_bias + part_bias
    base = 0
    for k in range(0, x.shape[1], LANES):
        grads[base : base + hid, :] = grad_in[:, k : k + LANES]
        base += hid
    for k in range(0, hid, LANES):
        grads[base : base + vec_width, :] = grad_out[:, k : k + LANES]
        base += vec_width
    rest = grads.shape[0] - base
    singles = [grad_bias[0:1, k : k + LANES] for k in range(0, hid, LANES)] + [vec_sum[0:1, :]]
    grads[base:, :] = tail_tile(singles, rest)
    half = keep.shape[0]
    core = place[1]
    keep[...] = grads[pl.ds(pl.multiple_of(core * half, half), half), :]
    give[...] = grads[pl.ds(pl.multiple_of((1 - core) * half, half), half), :].astype(bf16)


def tail_tile(values, size):
    sub = lax.broadcasted_iota(jnp.int32, (size, LANES), 0)
    tile = jnp.zeros((size, LANES), f32)
    for i, value in enumerate(values):
        for p, part in enumerate(split3(value)):
            tile = jnp.where(sub == 3 * i + p, part, tile)
    return tile


def tail_values(tile, count):
    return [
        tile[3 * i : 3 * i + 1] + tile[3 * i + 1 : 3 * i + 2] + tile[3 * i + 2 : 3 * i + 3]
        for i in range(count)
    ]


def sum_core_kernel(place, keep, got, send, *, tail_rows, tail_count):
    total = keep[...] + got[...].astype(f32)
    send[...] = total.astype(bf16)

    @pl.when(place[1] == 1)
    def _():
        first = total.shape[0] - tail_rows
        values = tail_values(total[first:, :], tail_count)
        send[first:, :] = tail_tile(values, tail_rows).astype(bf16)


def sum_kernel(got, send):
    part = got[0].astype(f32)
    for k in range(1, got.shape[0]):
        part = part + got[k].astype(f32)
    part = part.astype(bf16)
    for k in range(send.shape[0]):
        send[k] = part


def unpack_kernel(place, mine, other, base_row, grad_in, grad_bias, grad_out, got):
    feat, hid = grad_in.shape
    vec_width = grad_out.shape[1]
    half = mine.shape[0]
    core = place[1]
    got[pl.ds(pl.multiple_of(core * half, half), half), :] = mine[...]
    got[pl.ds(pl.multiple_of((1 - core) * half, half), half), :] = other[...]
    base = 0
    for k in range(0, feat, LANES):
        grad_in[k : k + LANES, :] = got[base : base + hid, :].astype(f32).T
        base += hid
    start = base + vec_width * (hid // LANES)
    values = tail_values(got[start : start + 16, :].astype(f32), hid // LANES + 1)
    vec_sum = values[-1]
    sub = lax.broadcasted_iota(jnp.int32, (META, LANES), 0)
    zero = jnp.zeros((META, LANES), f32)
    vec_rows = zero
    for p, part in enumerate(split3(vec_sum)):
        vec_rows = jnp.where(sub == p, part, vec_rows)
    vec_rows = vec_rows.astype(bf16)
    for i, k in enumerate(range(0, hid, LANES)):
        base_rows = base_row[:, k : k + LANES].astype(bf16)
        outer = dot(base_rows, vec_rows, 0, 0)
        grad_out[k : k + LANES, :] = got[base : base + vec_width, :].astype(f32).T + outer
        grad_bias[0:1, k : k + LANES] = values[i]
        base += vec_width


def exchange(x, axis):
    return lax.all_to_all(x, axis, split_axis=0, concat_axis=0, tiled=True)


def shape_of(shape, dtype):
    return jax.ShapeDtypeStruct(shape, dtype)


def local(query_frames, line_frames, frame_count, line_home, mined, positive, w_in, bias_in, w_out):
    query_count, query_len, feat = query_frames.shape
    line_count, line_len, _ = line_frames.shape
    hid, vec_width = w_out.shape
    chip_count = lax.axis_size("chip")
    owner_count = chip_count * lax.axis_size("core")
    dp_count = lax.axis_size("dp")
    loss_factor = LOSS_SCALE / (query_count * owner_count * dp_count)
    frames_q = query_count * query_len
    frames_l = line_count * line_len
    frames = frames_q + frames_l
    rows = CAP * query_len
    xq = query_frames.reshape(frames_q, feat)
    xl = line_frames.reshape(frames_l, feat)
    bias = bias_in.reshape(1, hid)
    place = jnp.stack([lax.axis_index(ARCHIVE), lax.axis_index("core")]).astype(jnp.int32)
    wire = shape_of((owner_count, rows + META, vec_width), bf16)
    head_flops = 2 * hid * (feat + vec_width)

    (asked,) = call(
        ask_kernel,
        [wire],
        [mined, line_home, positive, xq, w_in, bias, w_out],
        3,
        [
            pltpu.VMEM(xq.shape, bf16),
            pltpu.VMEM(w_in.shape, bf16),
            pltpu.VMEM(bias.shape, f32),
            pltpu.VMEM(w_out.shape, bf16),
            pltpu.VMEM((frames_q, vec_width), bf16),
            pltpu.SMEM((CAP, owner_count), jnp.int32),
            pltpu.SMEM((CAP, owner_count), jnp.int32),
            pltpu.SMEM((owner_count,), jnp.int32),
            pltpu.SMEM(mined.shape, jnp.int32),
            pltpu.SemaphoreType.DMA((4,)),
        ],
        flops=frames_q * head_flops,
        where=pl.ANY,
    )
    got = exchange(asked, ARCHIVE)
    line_vec, hidden_all, slope_t, mean = call(
        head_kernel,
        [
            shape_of((frames_l, vec_width), bf16),
            shape_of((frames, hid), bf16),
            shape_of((hid, frames), f32),
            shape_of((META, LANES), f32),
        ],
        [xl, xq, w_in, bias, w_out],
        0,
        flops=frames * head_flops,
        transcendentals=frames * hid,
    )
    match_flops = 2 * owner_count * rows * frames_l * vec_width
    answer, weights, own = call(
        match_kernel,
        [
            wire,
            shape_of((owner_count, rows, line_len), bf16),
            shape_of((META, LANES), f32),
        ],
        [place, frame_count, got, line_vec, mean],
        2,
        flops=2 * match_flops,
    )
    back = exchange(answer, ARCHIVE)
    unit = 16 * owner_count
    flat_rows = unit * -(-(LANES + (feat + vec_width) * hid // LANES) // unit)
    half = flat_rows // 2

    def grads_body(*refs):
        grad_kernel(*refs, loss_factor=loss_factor)

    loss, keep, give, base_row = call(
        grads_body,
        [
            shape_of((META, LANES), f32),
            shape_of((half, LANES), f32),
            shape_of((half, LANES), bf16),
            shape_of((META, hid), f32),
        ],
        [place, back, got, weights, own, xl, xq, hidden_all, slope_t, w_out],
        1,
        [
            pltpu.VMEM((flat_rows, LANES), f32),
            pltpu.VMEM((owner_count, META, LANES), f32),
            pltpu.VMEM((owner_count, META, LANES), f32),
            pltpu.VMEM((vec_width, frames_l), f32),
            pltpu.VMEM((vec_width, frames_q), f32),
        ],
        flops=match_flops + 4 * frames * head_flops,
    )
    swap = [(0, 1), (1, 0)]
    share = half // chip_count
    taken = lax.ppermute(give, "core", swap)
    tail_rows = flat_rows - (feat + vec_width) * hid // LANES

    def sum_core_body(*refs):
        sum_core_kernel(*refs, tail_rows=tail_rows, tail_count=hid // LANES + 1)

    (part,) = call(sum_core_body, [shape_of((half, LANES), bf16)], [place, keep, taken], 1)
    parts = exchange(part.reshape(chip_count, share, LANES), "chip")
    (part,) = call(sum_kernel, [shape_of((dp_count, share, LANES), bf16)], [parts], 0)
    parts = exchange(part, "dp")
    (part,) = call(sum_kernel, [shape_of((chip_count, share, LANES), bf16)], [parts], 0)
    mine = exchange(part, "chip").reshape(half, LANES)
    other = lax.ppermute(mine, "core", swap)
    grad_in, grad_bias, grad_out = call(
        unpack_kernel,
        [shape_of((feat, hid), f32), shape_of((1, hid), f32), shape_of((hid, vec_width), f32)],
        [place, mine, other, base_row],
        1,
        [pltpu.VMEM((flat_rows, LANES), bf16)],
    )
    return (loss[:query_count, 0], grad_in, grad_bias.reshape(hid), grad_out)


def solution(mesh):
    devices = mesh.devices
    archive, dp = devices.shape
    mesh = Mesh(devices.reshape(archive // 2, 2, dp), ("chip", "core", "dp"))
    everywhere = ARCHIVE + ("dp",)
    placed = (
        P(everywhere, None, None),
        P(ARCHIVE, None, None),
        P(),
        P(),
        P(everywhere, None),
        P(everywhere),
        P(),
        P(),
        P(),
    )
    return jax.shard_map(
        local,
        mesh=mesh,
        in_specs=placed,
        out_specs=(P(everywhere), P(), P(), P()),
        check_vma=False,
    )
```

```python
import math

import jax
import jax.numpy as jnp
from jax import lax
from jax.experimental import pallas as pl
from jax.experimental.pallas import tpu as pltpu
from jax.sharding import Mesh, PartitionSpec as P

LOSS_SCALE = 4096.0
SCORE_SCALE = 4.0
LANES = 128
CAP = 2
HALF = LANES // CAP
META = 8
UNUSED = 100.0
FLOOR = -1e30
GELU_A = math.sqrt(2.0 / math.pi)
GELU_B = 0.044715
GROUP = 32
WIDE = 64
ARCHIVE = ("chip", "core")

f32 = jnp.float32
bf16 = jnp.bfloat16


def dot(a, b, ca=1, cb=0):
    return lax.dot_general(a, b, (((ca,), (cb,)), ((), ())), preferred_element_type=f32)


def split2(x):
    hi = x.astype(bf16)
    return hi, (x - hi.astype(f32)).astype(bf16)


def split3(x):
    hi = x.astype(bf16).astype(f32)
    mid = (x - hi).astype(bf16).astype(f32)
    return hi, mid, (x - hi - mid).astype(bf16).astype(f32)


def call(body, outs, args, smem_count, scratch=(), flops=0, transcendentals=0, where=pltpu.VMEM, limit=40 << 20):
    nbytes = sum(a.size * a.dtype.itemsize for a in list(args) + list(outs))
    vmem = pl.BlockSpec(memory_space=pltpu.VMEM)
    smem = pl.BlockSpec(memory_space=pltpu.SMEM)
    rest = pl.BlockSpec(memory_space=where)
    return pl.pallas_call(
        body,
        out_shape=tuple(outs),
        in_specs=[smem] * smem_count + [rest] * (len(args) - smem_count),
        out_specs=tuple(vmem for _ in outs),
        scratch_shapes=list(scratch),
        compiler_params=pltpu.CompilerParams(vmem_limit_bytes=limit),
        cost_estimate=pl.CostEstimate(
            flops=flops, bytes_accessed=nbytes, transcendentals=transcendentals
        ),
    )(*args)


def gelu_parts(pre):
    t = jnp.tanh(GELU_A * (pre + GELU_B * pre * pre * pre))
    return t, (0.5 * pre * (1.0 + t)).astype(bf16)


def ask_kernel(
    mined_hbm, home_hbm, positive_hbm, x_hbm, w_in_hbm, bias_hbm, w_out_hbm, send, mined, home, positive, x, w_in, bias, w_out, vec, rid, code, count, goal, sems
):
    query_count, mined_count = mined.shape
    owner_count = send.shape[0]
    query_len = x.shape[0] // query_count
    line_count = home.shape[0] // owner_count
    rows = CAP * query_len
    pairs = (
        (mined_hbm, mined),
        (home_hbm, home),
        (positive_hbm, positive),
        (x_hbm, x),
        (w_in_hbm, w_in),
        (bias_hbm, bias),
        (w_out_hbm, w_out),
    )
    copies = [pltpu.make_async_copy(a, b, sems.at[i]) for i, (a, b) in enumerate(pairs)]
    for copy in copies:
        copy.start()

    def clear(owner, carry):
        count[owner] = 0
        for c in range(CAP):
            rid[c, owner] = int(UNUSED)
            code[c, owner] = int(UNUSED)
        return carry

    lax.fori_loop(0, owner_count, clear, 0, unroll=8)
    send[...] = jnp.zeros(send.shape, bf16)
    for copy in copies[:3]:
        copy.wait()

    def assign(query, carry):
        for j in range(mined_count):
            row = home[mined[query, j]]
            owner = row // line_count
            rank = count[owner]
            count[owner] = rank + 1
            rid[rank, owner] = row - owner * line_count
            code[rank, owner] = query + jnp.where(positive[query] == j, 8, 0)
            goal[query, j] = owner * CAP + rank
        return carry

    lax.fori_loop(0, query_count, assign, 0)
    sub = lax.broadcasted_iota(jnp.int32, (META, LANES), 0)

    def label(owner, carry):
        tile = jnp.where(
            sub == 0,
            rid[0, owner],
            jnp.where(sub == 1, rid[1, owner], jnp.where(sub == 2, code[0, owner], code[1, owner])),
        )
        send[owner, rows : rows + META, :] = tile.astype(f32).astype(bf16)
        return carry

    lax.fori_loop(0, owner_count, label, 0, unroll=8)
    for copy in copies[3:]:
        copy.wait()
    _, hidden = gelu_parts(dot(x[...], w_in[...]) + bias[...].reshape(1, -1))
    vec[...] = dot(hidden, w_out[...]).astype(bf16)

    def place(query, carry):
        block = vec[pl.ds(pl.multiple_of(query * query_len, query_len), query_len), :]
        for j in range(mined_count):
            owner = goal[query, j] // CAP
            rank = goal[query, j] % CAP
            send[owner, pl.ds(pl.multiple_of(rank * query_len, query_len), query_len), :] = block
        return carry

    lax.fori_loop(0, query_count, place, 0)


def head_kernel(xl, xq, w_in, bias, w_out, line_vec, line_vec_t, hidden_all, slope_t, mean):
    step = 256
    line_frames = xl.shape[0]
    total = jnp.zeros((1, hidden_all.shape[1]), f32)
    for first in range(0, line_frames + xq.shape[0], step):
        if first < line_frames:
            x = xl[first : first + step, :]
        else:
            x = xq[first - line_frames : first - line_frames + step, :]
        size = x.shape[0]
        pre = dot(x, w_in[...]) + bias[...].reshape(1, -1)
        t, hidden = gelu_parts(pre)
        slope = 0.5 * (1.0 + t) + 0.5 * pre * (1.0 - t * t) * GELU_A * (
            1.0 + 3.0 * GELU_B * pre * pre
        )
        hidden_all[first : first + size, :] = hidden
        slope_t[:, first : first + size] = slope.T
        if first < line_frames:
            vec = dot(hidden, w_out[...])
            for k in range(0, size, LANES):
                line = (first + k) // LANES
                line_vec[line] = vec[k : k + LANES].astype(bf16)
                line_vec_t[line] = vec[k : k + LANES].T.astype(bf16)
            total += jnp.sum(hidden.astype(f32), axis=0, keepdims=True)
    mean[...] = jnp.zeros(mean.shape, f32)
    for i, k in enumerate(range(0, hidden_all.shape[1], LANES)):
        mean[4 + i : 5 + i, :] = total[:, k : k + LANES] * (1.0 / line_frames)


def spread(meta, first, query_len):
    parts = []
    for b in range(meta.shape[0]):
        for c in range(CAP):
            parts.append(jnp.broadcast_to(meta[b, first + c : first + c + 1, :], (query_len, LANES)))
    return jnp.concatenate(parts, axis=0)


def match_kernel(
    place, counts, got, line_vec, line_vec_t, mean, send, weights, own, pads, label_rows, ids, sums, sem
):
    owner_count = got.shape[0]
    rows = got.shape[1] - META
    group = min(GROUP, owner_count)
    query_len = rows // CAP
    line_count, _, vec_width = line_vec.shape
    scale = SCORE_SCALE / math.sqrt(vec_width)
    shape3 = (owner_count, META, LANES)
    lane3 = lax.broadcasted_iota(jnp.int32, shape3, 2)
    sub3 = lax.broadcasted_iota(jnp.int32, shape3, 1)
    owner3 = lax.broadcasted_iota(jnp.int32, shape3, 0)
    lane1 = lax.broadcasted_iota(jnp.int32, (1, LANES), 1)
    sub = lax.broadcasted_iota(jnp.int32, (META, LANES), 0)
    meta = got[:, rows : rows + META, :].astype(f32)
    labels = jnp.sum(jnp.where(lane3 == owner3 + HALF * (sub3 % CAP), meta, 0.0), axis=0)
    covered = lane1 % HALF < owner_count
    rid_row = labels[0:1] + labels[1:2]
    rid_row = jnp.where(covered & (rid_row < line_count), rid_row, 0.0)
    code_row = jnp.where(covered, labels[2:3] + labels[3:4], UNUSED)
    label_rows[...] = jnp.broadcast_to(rid_row, (META, LANES)).astype(jnp.int32)
    copy = pltpu.make_async_copy(label_rows, ids, sem)
    copy.start()
    for r in range(line_count):
        pads[r : r + 1, :] = jnp.where(lane1 < counts[place[0] * line_count + r], 0.0, FLOOR)
    sums[...] = jnp.zeros(sums.shape, f32)
    copy.wait()

    def step(g, carry):
        first = g * group
        for b in range(group):
            for c in range(CAP):
                slot = first + b + HALF * c
                r = ids[0, slot]
                span = pl.ds(c * query_len, query_len)
                logits = dot(got[first + b, span, :], line_vec_t[r]) * scale
                logits = logits + pads[pl.ds(r, 1), :]
                peak = jnp.max(logits, axis=1, keepdims=True)
                scaled = jnp.exp(logits - peak)
                totals = jnp.sum(scaled, axis=1, keepdims=True)
                log_total = peak + jnp.log(totals)
                weight = (scaled * (1.0 / totals)).astype(bf16)
                weights[first + b, span, :] = weight
                send[first + b, span, :] = dot(weight, line_vec[r]).astype(bf16)
                mean_log = jnp.sum(log_total, axis=0, keepdims=True) * (1.0 / query_len)
                sums[pl.ds(slot, 1), :] = jnp.broadcast_to(mean_log, (1, LANES))
        return carry

    lax.fori_loop(0, owner_count // group, step, 0)
    lane = lax.broadcasted_iota(jnp.int32, sums.shape, 1)
    row = lax.broadcasted_iota(jnp.int32, sums.shape, 0)
    match_row = jnp.sum(jnp.where(lane == row, sums[...], 0.0), axis=0, keepdims=True)
    own[...] = jnp.where(sub == 0, match_row, code_row)
    tile = mean[...]
    for p, part in enumerate(split3(match_row)):
        tile = jnp.where(sub == p, part, tile)
    tile = jnp.where(sub == 3, code_row, tile).astype(bf16)

    def label(b, carry):
        send[b, rows : rows + META, :] = tile
        return carry

    lax.fori_loop(0, owner_count, label, 0, unroll=8)


def grad_kernel(
    place, back, got, weights, own, xl, xq, hidden_all, slope_t, w_out, loss, keep, give, base_row, grads, own_scale, ask_scale, line_acc, query_acc, *, loss_factor
):
    owner_count = got.shape[0]
    rows = got.shape[1] - META
    wide_count = min(WIDE, owner_count)
    query_len = rows // CAP
    line_total = xl.shape[0]
    line_count = line_total // LANES
    query_frames = xq.shape[0]
    vec_width = w_out.shape[1]
    hid = w_out.shape[0]
    me = place[0]

    shape3 = (owner_count, META, LANES)
    lane3 = lax.broadcasted_iota(jnp.int32, shape3, 2)
    sub3 = lax.broadcasted_iota(jnp.int32, shape3, 1)
    owner3 = lax.broadcasted_iota(jnp.int32, shape3, 0)
    subf = sub3.astype(f32)
    meta = back[:, rows : rows + META, :].astype(f32)
    match = jnp.sum(jnp.where(sub3 < 3, meta, 0.0), axis=1, keepdims=True)
    code = jnp.sum(jnp.where(sub3 == 3, meta, 0.0), axis=1, keepdims=True)
    match = jnp.broadcast_to(match, shape3)
    code = jnp.broadcast_to(code, shape3)
    is_pos = (code >= 8.0) & (code < 16.0)
    query_of = jnp.where(is_pos, code - 8.0, code)
    here = query_of == subf
    peak = jnp.max(jnp.where(here, match, FLOOR), axis=0)
    peak = jnp.maximum(peak, pltpu.roll(peak, HALF, 1))
    total = jnp.sum(jnp.where(here, jnp.exp(match - peak[None]), 0.0), axis=0)
    total = total + pltpu.roll(total, HALF, 1)
    chosen = jnp.sum(jnp.where(here & is_pos, match, 0.0), axis=0)
    chosen = chosen + pltpu.roll(chosen, HALF, 1)
    log_total = peak + jnp.log(jnp.where(total > 0.0, total, 1.0))
    lane2 = lax.broadcasted_iota(jnp.int32, (META, LANES), 1)
    sub2 = lax.broadcasted_iota(jnp.int32, (META, LANES), 0).astype(f32)
    picked = jnp.sum(jnp.where(lane2 == me, log_total - chosen, 0.0), axis=1, keepdims=True)
    loss[...] = jnp.broadcast_to(picked, (META, LANES))

    factor = loss_factor * SCORE_SCALE / (math.sqrt(vec_width) * query_len)

    own_match = own[0:1, :]
    own_code = own[1:2, :]
    own_pos = (own_code >= 8.0) & (own_code < 16.0)
    own_query = jnp.where(own_pos, own_code - 8.0, own_code)
    own_grad = jnp.exp(jnp.minimum(own_match - log_total, 0.0)) - jnp.where(own_pos, 1.0, 0.0)
    own_grad = factor * jnp.sum(jnp.where(own_query == sub2, own_grad, 0.0), axis=0, keepdims=True)
    aim = lane3 == owner3 + HALF * sub3
    own_scale[...] = jnp.broadcast_to(
        jnp.sum(
            jnp.where(aim, jnp.broadcast_to(own_grad[None], shape3), 0.0), axis=2, keepdims=True
        ),
        shape3,
    )

    ask_grad = jnp.exp(jnp.minimum(match - log_total[None], 0.0)) - jnp.where(is_pos, 1.0, 0.0)
    ask_grad = factor * jnp.sum(jnp.where(here, ask_grad, 0.0), axis=1, keepdims=True)
    both = jnp.where(sub3 < CAP, jnp.broadcast_to(ask_grad, shape3), query_of)
    aim = lane3 == me + HALF * (sub3 % CAP)
    ask_scale[...] = jnp.broadcast_to(
        jnp.sum(jnp.where(aim, both, 0.0), axis=2, keepdims=True), shape3
    )

    size = wide_count * rows
    line_acc[...] = jnp.zeros(line_acc.shape, f32)
    query_acc[...] = jnp.zeros(query_acc.shape, f32)
    frame = (lax.broadcasted_iota(jnp.int32, (size, LANES), 0) % query_len).astype(f32)
    lane = lax.broadcasted_iota(jnp.int32, (size, LANES), 1).astype(f32)
    zero = jnp.zeros((size, LANES), bf16)
    one = jnp.ones((size, LANES), bf16)

    def step(g, carry):
        first = g * wide_count
        queries = got[pl.ds(first, wide_count), 0:rows, :].reshape(size, LANES)
        rid = spread(got[pl.ds(first, wide_count), rows : rows + META, :].astype(f32), 0, query_len)
        rid = rid.astype(bf16)
        scale = spread(own_scale[pl.ds(first, wide_count)], 0, query_len)
        weight = weights[pl.ds(first, wide_count)].reshape(size, LANES).astype(f32)
        score = (weight * scale).astype(bf16)
        wide = jnp.concatenate(
            [jnp.where(rid == r, score, zero) for r in range(line_count)], axis=1
        )
        line_acc[...] += dot(queries, wide, 0, 0)

        labels = ask_scale[pl.ds(first, wide_count)]
        scale = spread(labels, 0, query_len)
        target = spread(labels, CAP, query_len) * float(query_len) + frame
        pulled = back[pl.ds(first, wide_count), 0:rows, :].reshape(size, LANES).astype(f32)
        pulled = (pulled * scale).astype(bf16)
        wide = jnp.concatenate(
            [
                jnp.where(target == lane + float(k), one, zero)
                for k in range(0, query_acc.shape[1], LANES)
            ],
            axis=1,
        )
        query_acc[...] += dot(pulled, wide, 0, 0)
        return carry

    lax.fori_loop(0, owner_count // wide_count, step, 0)

    grad_in = None
    grad_out = None
    grad_bias = None
    vec_sum = None
    shared = jnp.sum(jnp.where(sub3 >= 4, meta, 0.0), axis=0) * (1.0 / owner_count)
    shared = shared.astype(bf16).astype(f32)
    shared = jnp.concatenate([shared[4 + i : 5 + i, :] for i in range(hid // LANES)], axis=1)
    base_row[...] = jnp.broadcast_to(shared, base_row.shape)
    spans = ((line_acc, xl, 0, line_total), (query_acc, xq, line_total, query_frames))
    for acc, x, first, span in spans:
        g_hi, g_lo = split2(acc[:, 0:span])
        grad_hidden = dot(w_out[...], g_hi) + dot(w_out[...], g_lo)
        p_hi, p_lo = split2(grad_hidden * slope_t[:, first : first + span])
        hidden = hidden_all[first : first + span, :]
        ones = jnp.ones((META, span), bf16)
        part_in = dot(p_hi, x[...]) + dot(p_lo, x[...])
        part_out = dot(g_hi, hidden) + dot(g_lo, hidden)
        part_out -= jnp.sum(g_hi.astype(f32) + g_lo.astype(f32), axis=1, keepdims=True) * shared
        part_sum = dot(ones, g_hi, 1, 1) + dot(ones, g_lo, 1, 1)
        vec_sum = part_sum if vec_sum is None else vec_sum + part_sum
        part_bias = dot(ones, p_hi, 1, 1) + dot(ones, p_lo, 1, 1)
        grad_in = part_in if grad_in is None else grad_in + part_in
        grad_out = part_out if grad_out is None else grad_out + part_out
        grad_bias = part_bias if grad_bias is None else grad_bias + part_bias
    base = 0
    for k in range(0, x.shape[1], LANES):
        grads[base : base + hid, :] = grad_in[:, k : k + LANES]
        base += hid
    for k in range(0, hid, LANES):
        grads[base : base + vec_width, :] = grad_out[:, k : k + LANES]
        base += vec_width
    rest = grads.shape[0] - base
    singles = [grad_bias[0:1, k : k + LANES] for k in range(0, hid, LANES)] + [vec_sum[0:1, :]]
    grads[base:, :] = tail_tile(singles, rest)
    half = keep.shape[0]
    core = place[1]
    keep[...] = grads[pl.ds(pl.multiple_of(core * half, half), half), :]
    give[...] = grads[pl.ds(pl.multiple_of((1 - core) * half, half), half), :].astype(bf16)


def tail_tile(values, size):
    sub = lax.broadcasted_iota(jnp.int32, (size, LANES), 0)
    tile = jnp.zeros((size, LANES), f32)
    for i, value in enumerate(values):
        for p, part in enumerate(split3(value)):
            tile = jnp.where(sub == 3 * i + p, part, tile)
    return tile


def tail_values(tile, count):
    return [
        tile[3 * i : 3 * i + 1] + tile[3 * i + 1 : 3 * i + 2] + tile[3 * i + 2 : 3 * i + 3]
        for i in range(count)
    ]


def sum_core_kernel(place, keep, got, send, *, tail_rows, tail_count):
    total = keep[...] + got[...].astype(f32)
    send[...] = total.astype(bf16)

    @pl.when(place[1] == 1)
    def _():
        first = total.shape[0] - tail_rows
        values = tail_values(total[first:, :], tail_count)
        send[first:, :] = tail_tile(values, tail_rows).astype(bf16)


def sum_kernel(got, send, *, share):
    rows = got.shape[0]
    block = max(share, META)
    part = jnp.sum(got[...].astype(f32).reshape(rows // block, block, LANES), axis=0)
    if share < block:
        part = sum(part[i : i + share] for i in range(0, block, share))
        part = jnp.concatenate([part] * (block // share), axis=0)
    part = jnp.broadcast_to(part[None], (rows // block, block, LANES)).reshape(rows, LANES)
    send[...] = part.astype(bf16)


def unpack_kernel(place, mine, other, base_row, grad_in, grad_bias, grad_out, got):
    feat, hid = grad_in.shape
    vec_width = grad_out.shape[1]
    half = mine.shape[0]
    core = place[1]
    got[pl.ds(pl.multiple_of(core * half, half), half), :] = mine[...]
    got[pl.ds(pl.multiple_of((1 - core) * half, half), half), :] = other[...]
    base = 0
    for k in range(0, feat, LANES):
        grad_in[k : k + LANES, :] = got[base : base + hid, :].astype(f32).T
        base += hid
    start = base + vec_width * (hid // LANES)
    values = tail_values(got[start : start + 16, :].astype(f32), hid // LANES + 1)
    vec_sum = values[-1]
    sub = lax.broadcasted_iota(jnp.int32, (META, LANES), 0)
    zero = jnp.zeros((META, LANES), f32)
    vec_rows = zero
    for p, part in enumerate(split3(vec_sum)):
        vec_rows = jnp.where(sub == p, part, vec_rows)
    vec_rows = vec_rows.astype(bf16)
    for i, k in enumerate(range(0, hid, LANES)):
        base_rows = base_row[:, k : k + LANES].astype(bf16)
        outer = dot(base_rows, vec_rows, 0, 0)
        grad_out[k : k + LANES, :] = got[base : base + vec_width, :].astype(f32).T + outer
        grad_bias[k : k + LANES] = values[i].reshape(LANES)
        base += vec_width


def exchange(x, axis):
    return lax.all_to_all(x, axis, split_axis=0, concat_axis=0, tiled=True)


def shape_of(shape, dtype):
    return jax.ShapeDtypeStruct(shape, dtype)


def local(query_frames, line_frames, frame_count, line_home, mined, positive, w_in, bias_in, w_out):
    query_count, query_len, feat = query_frames.shape
    line_count, line_len, _ = line_frames.shape
    hid, vec_width = w_out.shape
    chip_count = lax.axis_size("chip")
    owner_count = chip_count * lax.axis_size("core")
    dp_count = lax.axis_size("dp")
    loss_factor = LOSS_SCALE / (query_count * owner_count * dp_count)
    frames_q = query_count * query_len
    frames_l = line_count * line_len
    frames = frames_q + frames_l
    rows = CAP * query_len
    xq = query_frames.reshape(frames_q, feat)
    xl = line_frames.reshape(frames_l, feat)
    place = jnp.stack([lax.axis_index(ARCHIVE), lax.axis_index("core")]).astype(jnp.int32)
    wire = shape_of((owner_count, rows + META, vec_width), bf16)
    head_flops = 2 * hid * (feat + vec_width)

    (asked,) = call(
        ask_kernel,
        [wire],
        [mined, line_home, positive, xq, w_in, bias_in, w_out],
        0,
        [
            pltpu.SMEM(mined.shape, jnp.int32),
            pltpu.SMEM(line_home.shape, jnp.int32),
            pltpu.SMEM(positive.shape, jnp.int32),
            pltpu.VMEM(xq.shape, bf16),
            pltpu.VMEM(w_in.shape, bf16),
            pltpu.VMEM(bias_in.shape, f32),
            pltpu.VMEM(w_out.shape, bf16),
            pltpu.VMEM((frames_q, vec_width), bf16),
            pltpu.SMEM((CAP, owner_count), jnp.int32),
            pltpu.SMEM((CAP, owner_count), jnp.int32),
            pltpu.SMEM((owner_count,), jnp.int32),
            pltpu.SMEM(mined.shape, jnp.int32),
            pltpu.SemaphoreType.DMA((7,)),
        ],
        flops=frames_q * head_flops,
        where=pltpu.HBM,
        limit=63 << 20,
    )
    got = exchange(asked, ARCHIVE)
    line_vec, line_vec_t, hidden_all, slope_t, mean = call(
        head_kernel,
        [
            shape_of((line_count, line_len, vec_width), bf16),
            shape_of((line_count, vec_width, line_len), bf16),
            shape_of((frames, hid), bf16),
            shape_of((hid, frames), f32),
            shape_of((META, LANES), f32),
        ],
        [xl, xq, w_in, bias_in, w_out],
        0,
        flops=frames * head_flops,
        transcendentals=frames * hid,
    )
    match_flops = 2 * owner_count * rows * frames_l * vec_width
    answer, weights, own = call(
        match_kernel,
        [
            wire,
            shape_of((owner_count, rows, line_len), bf16),
            shape_of((META, LANES), f32),
        ],
        [place, frame_count, got, line_vec, line_vec_t, mean],
        2,
        [
            pltpu.VMEM((line_count, LANES), f32),
            pltpu.VMEM((META, LANES), jnp.int32),
            pltpu.SMEM((META, LANES), jnp.int32),
            pltpu.VMEM((LANES, LANES), f32),
            pltpu.SemaphoreType.DMA(()),
        ],
        flops=2 * match_flops,
    )
    back = exchange(answer, ARCHIVE)
    unit = 16 * owner_count
    flat_rows = unit * -(-(LANES + (feat + vec_width) * hid // LANES) // unit)
    half = flat_rows // 2

    def grads_body(*refs):
        grad_kernel(*refs, loss_factor=loss_factor)

    loss, keep, give, base_row = call(
        grads_body,
        [
            shape_of((META, LANES), f32),
            shape_of((half, LANES), f32),
            shape_of((half, LANES), bf16),
            shape_of((META, hid), f32),
        ],
        [place, back, got, weights, own, xl, xq, hidden_all, slope_t, w_out],
        1,
        [
            pltpu.VMEM((flat_rows, LANES), f32),
            pltpu.VMEM((owner_count, META, LANES), f32),
            pltpu.VMEM((owner_count, META, LANES), f32),
            pltpu.VMEM((vec_width, frames_l), f32),
            pltpu.VMEM((vec_width, frames_q), f32),
        ],
        flops=match_flops + 4 * frames * head_flops,
    )
    swap = [(0, 1), (1, 0)]
    peers = chip_count * dp_count
    share = half // peers
    taken = lax.ppermute(give, "core", swap)
    tail_rows = flat_rows - (feat + vec_width) * hid // LANES

    def sum_core_body(*refs):
        sum_core_kernel(*refs, tail_rows=tail_rows, tail_count=hid // LANES + 1)

    (part,) = call(sum_core_body, [shape_of((half, LANES), bf16)], [place, keep, taken], 1)
    spread_out = ("chip", "dp")
    parts = exchange(part.reshape(peers, share, LANES), spread_out).reshape(half, LANES)

    def sum_body(*refs):
        sum_kernel(*refs, share=share)

    (part,) = call(sum_body, [shape_of((half, LANES), bf16)], [parts], 0)
    mine = exchange(part.reshape(peers, share, LANES), spread_out).reshape(half, LANES)
    other = lax.ppermute(mine, "core", swap)
    grad_in, grad_bias, grad_out = call(
        unpack_kernel,
        [shape_of((feat, hid), f32), shape_of((hid,), f32), shape_of((hid, vec_width), f32)],
        [place, mine, other, base_row],
        1,
        [pltpu.VMEM((flat_rows, LANES), bf16)],
    )
    return (loss[:query_count, 0], grad_in, grad_bias, grad_out)


def solution(mesh):
    devices = mesh.devices
    archive, dp = devices.shape
    mesh = Mesh(devices.reshape(archive // 2, 2, dp), ("chip", "core", "dp"))
    everywhere = ARCHIVE + ("dp",)
    placed = (
        P(everywhere, None, None),
        P(ARCHIVE, None, None),
        P(),
        P(),
        P(everywhere, None),
        P(everywhere),
        P(),
        P(),
        P(),
    )
    return jax.shard_map(
        local,
        mesh=mesh,
        in_specs=placed,
        out_specs=(P(everywhere), P(), P(), P()),
        check_vma=False,
    )
```

```python
import math

import jax
import jax.numpy as jnp
from jax import lax
from jax.experimental import pallas as pl
from jax.experimental.pallas import tpu as pltpu
from jax.sharding import Mesh, PartitionSpec as P

LOSS_SCALE = 4096.0
SCORE_SCALE = 4.0
LANES = 128
CAP = 2
HALF = LANES // CAP
META = 8
UNUSED = 100.0
FLOOR = -1e30
GELU_A = math.sqrt(2.0 / math.pi)
GELU_B = 0.044715
GROUP = 64
WIDE = 64
ARCHIVE = ("chip", "core")

f32 = jnp.float32
bf16 = jnp.bfloat16


def dot(a, b, ca=1, cb=0):
    return lax.dot_general(a, b, (((ca,), (cb,)), ((), ())), preferred_element_type=f32)


def split2(x):
    hi = x.astype(bf16)
    return hi, (x - hi.astype(f32)).astype(bf16)


def split3(x):
    hi = x.astype(bf16).astype(f32)
    mid = (x - hi).astype(bf16).astype(f32)
    return hi, mid, (x - hi - mid).astype(bf16).astype(f32)


def call(body, outs, args, smem_count, scratch=(), flops=0, transcendentals=0, where=pltpu.VMEM, limit=40 << 20):
    nbytes = sum(a.size * a.dtype.itemsize for a in list(args) + list(outs))
    vmem = pl.BlockSpec(memory_space=pltpu.VMEM)
    smem = pl.BlockSpec(memory_space=pltpu.SMEM)
    rest = pl.BlockSpec(memory_space=where)
    return pl.pallas_call(
        body,
        out_shape=tuple(outs),
        in_specs=[smem] * smem_count + [rest] * (len(args) - smem_count),
        out_specs=tuple(vmem for _ in outs),
        scratch_shapes=list(scratch),
        compiler_params=pltpu.CompilerParams(vmem_limit_bytes=limit),
        cost_estimate=pl.CostEstimate(
            flops=flops, bytes_accessed=nbytes, transcendentals=transcendentals
        ),
    )(*args)


def gelu_parts(pre):
    t = jnp.tanh(GELU_A * (pre + GELU_B * pre * pre * pre))
    return t, (0.5 * pre * (1.0 + t)).astype(bf16)


def ask_kernel(
    mined_hbm, home_hbm, positive_hbm, x_hbm, w_in_hbm, bias_hbm, w_out_hbm, send, mined, home, positive, x, w_in, bias, w_out, vec, rid, code, count, goal, sems
):
    query_count, mined_count = mined.shape
    owner_count = send.shape[0]
    query_len = x.shape[0] // query_count
    line_count = home.shape[0] // owner_count
    rows = CAP * query_len
    pairs = (
        (mined_hbm, mined),
        (home_hbm, home),
        (positive_hbm, positive),
        (x_hbm, x),
        (w_in_hbm, w_in),
        (bias_hbm, bias),
        (w_out_hbm, w_out),
    )
    copies = [pltpu.make_async_copy(a, b, sems.at[i]) for i, (a, b) in enumerate(pairs)]
    for copy in copies:
        copy.start()

    def clear(owner, carry):
        count[owner] = 0
        for c in range(CAP):
            rid[c, owner] = int(UNUSED)
            code[c, owner] = int(UNUSED)
        return carry

    lax.fori_loop(0, owner_count, clear, 0, unroll=8)
    send[...] = jnp.zeros(send.shape, bf16)
    for copy in copies[:3]:
        copy.wait()

    def assign(query, carry):
        for j in range(mined_count):
            row = home[mined[query, j]]
            owner = row // line_count
            rank = count[owner]
            count[owner] = rank + 1
            rid[rank, owner] = row - owner * line_count
            code[rank, owner] = query + jnp.where(positive[query] == j, 8, 0)
            goal[query, j] = owner * CAP + rank
        return carry

    lax.fori_loop(0, query_count, assign, 0)
    sub = lax.broadcasted_iota(jnp.int32, (META, LANES), 0)

    def label(owner, carry):
        tile = jnp.where(
            sub == 0,
            rid[0, owner],
            jnp.where(sub == 1, rid[1, owner], jnp.where(sub == 2, code[0, owner], code[1, owner])),
        )
        send[owner, rows : rows + META, :] = tile.astype(f32).astype(bf16)
        return carry

    lax.fori_loop(0, owner_count, label, 0, unroll=8)
    for copy in copies[3:]:
        copy.wait()
    _, hidden = gelu_parts(dot(x[...], w_in[...]) + bias[...].reshape(1, -1))
    vec[...] = dot(hidden, w_out[...]).astype(bf16)

    def place(query, carry):
        block = vec[pl.ds(pl.multiple_of(query * query_len, query_len), query_len), :]
        for j in range(mined_count):
            owner = goal[query, j] // CAP
            rank = goal[query, j] % CAP
            send[owner, pl.ds(pl.multiple_of(rank * query_len, query_len), query_len), :] = block
        return carry

    lax.fori_loop(0, query_count, place, 0)


def head_kernel(xl, xq, w_in, bias, w_out, line_vec, line_vec_t, hidden_all, slope_t, mean):
    step = 256
    line_frames = xl.shape[0]
    total = jnp.zeros((1, hidden_all.shape[1]), f32)
    for first in range(0, line_frames + xq.shape[0], step):
        if first < line_frames:
            x = xl[first : first + step, :]
        else:
            x = xq[first - line_frames : first - line_frames + step, :]
        size = x.shape[0]
        pre = dot(x, w_in[...]) + bias[...].reshape(1, -1)
        t, hidden = gelu_parts(pre)
        slope = 0.5 * (1.0 + t) + 0.5 * pre * (1.0 - t * t) * GELU_A * (
            1.0 + 3.0 * GELU_B * pre * pre
        )
        hidden_all[first : first + size, :] = hidden
        slope_t[:, first : first + size] = slope.T
        if first < line_frames:
            vec = dot(hidden, w_out[...])
            for k in range(0, size, LANES):
                line = (first + k) // LANES
                line_vec[line] = vec[k : k + LANES].astype(bf16)
                line_vec_t[line] = vec[k : k + LANES].T.astype(bf16)
            total += jnp.sum(hidden.astype(f32), axis=0, keepdims=True)
    mean[...] = jnp.zeros(mean.shape, f32)
    for i, k in enumerate(range(0, hidden_all.shape[1], LANES)):
        mean[4 + i : 5 + i, :] = total[:, k : k + LANES] * (1.0 / line_frames)


def spread(meta, first, query_len):
    parts = []
    for b in range(meta.shape[0]):
        for c in range(CAP):
            parts.append(jnp.broadcast_to(meta[b, first + c : first + c + 1, :], (query_len, LANES)))
    return jnp.concatenate(parts, axis=0)


def match_kernel(
    place, counts, got, line_vec, line_vec_t, mean, send, weights, own, pads, label_rows, ids, sums, sem
):
    owner_count = got.shape[0]
    rows = got.shape[1] - META
    group = min(GROUP, owner_count)
    query_len = rows // CAP
    line_count, _, vec_width = line_vec.shape
    scale = SCORE_SCALE / math.sqrt(vec_width)
    shape3 = (owner_count, META, LANES)
    lane3 = lax.broadcasted_iota(jnp.int32, shape3, 2)
    sub3 = lax.broadcasted_iota(jnp.int32, shape3, 1)
    owner3 = lax.broadcasted_iota(jnp.int32, shape3, 0)
    lane1 = lax.broadcasted_iota(jnp.int32, (1, LANES), 1)
    sub = lax.broadcasted_iota(jnp.int32, (META, LANES), 0)
    meta = got[:, rows : rows + META, :].astype(f32)
    labels = jnp.sum(jnp.where(lane3 == owner3 + HALF * (sub3 % CAP), meta, 0.0), axis=0)
    covered = lane1 % HALF < owner_count
    rid_row = labels[0:1] + labels[1:2]
    rid_row = jnp.where(covered & (rid_row < line_count), rid_row, 0.0)
    code_row = jnp.where(covered, labels[2:3] + labels[3:4], UNUSED)
    label_rows[...] = jnp.broadcast_to(rid_row, (META, LANES)).astype(jnp.int32)
    copy = pltpu.make_async_copy(label_rows, ids, sem)
    copy.start()
    for r in range(line_count):
        pads[r : r + 1, :] = jnp.where(lane1 < counts[place[0] * line_count + r], 0.0, FLOOR)
    sums[...] = jnp.zeros(sums.shape, f32)
    copy.wait()
    ones = jnp.ones((LANES, LANES), bf16)

    def step(g, carry):
        first = g * group
        for b in range(group):
            for c in range(CAP):
                slot = first + b + HALF * c
                r = ids[0, slot]
                span = pl.ds(c * query_len, query_len)
                logits = dot(got[first + b, span, :], line_vec_t[r]) * scale
                logits = logits + pads[pl.ds(r, 1), :]
                peak = jnp.max(logits, axis=1, keepdims=True)
                scaled = jnp.exp(logits - peak)
                scaled = scaled.astype(bf16)
                both = dot(scaled, jnp.concatenate([line_vec[r], ones], axis=1))
                totals = both[:, vec_width:]
                inverse = 1.0 / totals
                weights[first + b, span, :] = (scaled.astype(f32) * inverse).astype(bf16)
                send[first + b, span, :] = (both[:, :vec_width] * inverse).astype(bf16)
                log_total = peak + jnp.log(totals)
                mean_log = jnp.sum(log_total, axis=0, keepdims=True) * (1.0 / query_len)
                sums[pl.ds(slot, 1), :] = mean_log
        return carry

    lax.fori_loop(0, owner_count // group, step, 0)
    lane = lax.broadcasted_iota(jnp.int32, sums.shape, 1)
    row = lax.broadcasted_iota(jnp.int32, sums.shape, 0)
    match_row = jnp.sum(jnp.where(lane == row, sums[...], 0.0), axis=0, keepdims=True)
    own[...] = jnp.where(sub == 0, match_row, code_row)
    tile = mean[...]
    for p, part in enumerate(split3(match_row)):
        tile = jnp.where(sub == p, part, tile)
    tile = jnp.where(sub == 3, code_row, tile).astype(bf16)

    def label(b, carry):
        send[b, rows : rows + META, :] = tile
        return carry

    lax.fori_loop(0, owner_count, label, 0, unroll=8)


def grad_kernel(
    place, back, got, weights, own, xl, xq, hidden_all, slope_t, w_out, loss, keep, give, base_row, grads, own_scale, ask_scale, line_acc, query_acc, *, loss_factor
):
    owner_count = got.shape[0]
    rows = got.shape[1] - META
    wide_count = min(WIDE, owner_count)
    query_len = rows // CAP
    line_total = xl.shape[0]
    line_count = line_total // LANES
    query_frames = xq.shape[0]
    vec_width = w_out.shape[1]
    hid = w_out.shape[0]
    me = place[0]

    shape3 = (owner_count, META, LANES)
    lane3 = lax.broadcasted_iota(jnp.int32, shape3, 2)
    sub3 = lax.broadcasted_iota(jnp.int32, shape3, 1)
    owner3 = lax.broadcasted_iota(jnp.int32, shape3, 0)
    subf = sub3.astype(f32)
    meta = back[:, rows : rows + META, :].astype(f32)
    match = jnp.sum(jnp.where(sub3 < 3, meta, 0.0), axis=1, keepdims=True)
    code = jnp.sum(jnp.where(sub3 == 3, meta, 0.0), axis=1, keepdims=True)
    match = jnp.broadcast_to(match, shape3)
    code = jnp.broadcast_to(code, shape3)
    is_pos = (code >= 8.0) & (code < 16.0)
    query_of = jnp.where(is_pos, code - 8.0, code)
    here = query_of == subf
    peak = jnp.max(jnp.where(here, match, FLOOR), axis=0)
    peak = jnp.maximum(peak, pltpu.roll(peak, HALF, 1))
    total = jnp.sum(jnp.where(here, jnp.exp(match - peak[None]), 0.0), axis=0)
    total = total + pltpu.roll(total, HALF, 1)
    chosen = jnp.sum(jnp.where(here & is_pos, match, 0.0), axis=0)
    chosen = chosen + pltpu.roll(chosen, HALF, 1)
    log_total = peak + jnp.log(jnp.where(total > 0.0, total, 1.0))
    lane2 = lax.broadcasted_iota(jnp.int32, (META, LANES), 1)
    sub2 = lax.broadcasted_iota(jnp.int32, (META, LANES), 0).astype(f32)
    picked = jnp.sum(jnp.where(lane2 == me, log_total - chosen, 0.0), axis=1, keepdims=True)
    loss[...] = jnp.broadcast_to(picked, (META, LANES))

    factor = loss_factor * SCORE_SCALE / (math.sqrt(vec_width) * query_len)

    own_match = own[0:1, :]
    own_code = own[1:2, :]
    own_pos = (own_code >= 8.0) & (own_code < 16.0)
    own_query = jnp.where(own_pos, own_code - 8.0, own_code)
    own_grad = jnp.exp(jnp.minimum(own_match - log_total, 0.0)) - jnp.where(own_pos, 1.0, 0.0)
    own_grad = factor * jnp.sum(jnp.where(own_query == sub2, own_grad, 0.0), axis=0, keepdims=True)
    aim = lane3 == owner3 + HALF * sub3
    own_scale[...] = jnp.broadcast_to(
        jnp.sum(
            jnp.where(aim, jnp.broadcast_to(own_grad[None], shape3), 0.0), axis=2, keepdims=True
        ),
        shape3,
    )

    ask_grad = jnp.exp(jnp.minimum(match - log_total[None], 0.0)) - jnp.where(is_pos, 1.0, 0.0)
    ask_grad = factor * jnp.sum(jnp.where(here, ask_grad, 0.0), axis=1, keepdims=True)
    both = jnp.where(sub3 < CAP, jnp.broadcast_to(ask_grad, shape3), query_of)
    aim = lane3 == me + HALF * (sub3 % CAP)
    ask_scale[...] = jnp.broadcast_to(
        jnp.sum(jnp.where(aim, both, 0.0), axis=2, keepdims=True), shape3
    )

    size = wide_count * rows
    line_acc[...] = jnp.zeros(line_acc.shape, f32)
    query_acc[...] = jnp.zeros(query_acc.shape, f32)
    frame = (lax.broadcasted_iota(jnp.int32, (size, LANES), 0) % query_len).astype(f32)
    lane = lax.broadcasted_iota(jnp.int32, (size, LANES), 1).astype(f32)
    zero = jnp.zeros((size, LANES), bf16)
    one = jnp.ones((size, LANES), bf16)

    def step(g, carry):
        first = g * wide_count
        queries = got[pl.ds(first, wide_count), 0:rows, :].reshape(size, LANES)
        rid = spread(got[pl.ds(first, wide_count), rows : rows + META, :].astype(f32), 0, query_len)
        rid = rid.astype(bf16)
        scale = spread(own_scale[pl.ds(first, wide_count)], 0, query_len)
        weight = weights[pl.ds(first, wide_count)].reshape(size, LANES).astype(f32)
        score = (weight * scale).astype(bf16)
        wide = jnp.concatenate(
            [jnp.where(rid == r, score, zero) for r in range(line_count)], axis=1
        )
        line_acc[...] += dot(queries, wide, 0, 0)

        labels = ask_scale[pl.ds(first, wide_count)]
        scale = spread(labels, 0, query_len)
        target = spread(labels, CAP, query_len) * float(query_len) + frame
        pulled = back[pl.ds(first, wide_count), 0:rows, :].reshape(size, LANES).astype(f32)
        pulled = (pulled * scale).astype(bf16)
        wide = jnp.concatenate(
            [
                jnp.where(target == lane + float(k), one, zero)
                for k in range(0, query_acc.shape[1], LANES)
            ],
            axis=1,
        )
        query_acc[...] += dot(pulled, wide, 0, 0)
        return carry

    lax.fori_loop(0, owner_count // wide_count, step, 0)

    grad_in = None
    grad_out = None
    grad_bias = None
    vec_sum = None
    shared = jnp.sum(jnp.where(sub3 >= 4, meta, 0.0), axis=0) * (1.0 / owner_count)
    shared = shared.astype(bf16).astype(f32)
    shared = jnp.concatenate([shared[4 + i : 5 + i, :] for i in range(hid // LANES)], axis=1)
    base_row[...] = jnp.broadcast_to(shared, base_row.shape)
    spans = ((line_acc, xl, 0, line_total), (query_acc, xq, line_total, query_frames))
    for acc, x, first, span in spans:
        g_hi, g_lo = split2(acc[:, 0:span])
        grad_hidden = dot(w_out[...], g_hi) + dot(w_out[...], g_lo)
        p_hi, p_lo = split2(grad_hidden * slope_t[:, first : first + span])
        hidden = hidden_all[first : first + span, :]
        ones = jnp.ones((META, span), bf16)
        part_in = dot(p_hi, x[...]) + dot(p_lo, x[...])
        part_out = dot(g_hi, hidden) + dot(g_lo, hidden)
        part_out -= jnp.sum(g_hi.astype(f32) + g_lo.astype(f32), axis=1, keepdims=True) * shared
        part_sum = dot(ones, g_hi, 1, 1) + dot(ones, g_lo, 1, 1)
        vec_sum = part_sum if vec_sum is None else vec_sum + part_sum
        part_bias = dot(ones, p_hi, 1, 1) + dot(ones, p_lo, 1, 1)
        grad_in = part_in if grad_in is None else grad_in + part_in
        grad_out = part_out if grad_out is None else grad_out + part_out
        grad_bias = part_bias if grad_bias is None else grad_bias + part_bias
    base = 0
    for k in range(0, x.shape[1], LANES):
        grads[base : base + hid, :] = grad_in[:, k : k + LANES]
        base += hid
    for k in range(0, hid, LANES):
        grads[base : base + vec_width, :] = grad_out[:, k : k + LANES]
        base += vec_width
    rest = grads.shape[0] - base
    singles = [grad_bias[0:1, k : k + LANES] for k in range(0, hid, LANES)] + [vec_sum[0:1, :]]
    grads[base:, :] = tail_tile(singles, rest)
    half = keep.shape[0]
    core = place[1]
    keep[...] = grads[pl.ds(pl.multiple_of(core * half, half), half), :]
    give[...] = grads[pl.ds(pl.multiple_of((1 - core) * half, half), half), :].astype(bf16)


def tail_tile(values, size):
    sub = lax.broadcasted_iota(jnp.int32, (size, LANES), 0)
    tile = jnp.zeros((size, LANES), f32)
    for i, value in enumerate(values):
        for p, part in enumerate(split3(value)):
            tile = jnp.where(sub == 3 * i + p, part, tile)
    return tile


def tail_values(tile, count):
    return [
        tile[3 * i : 3 * i + 1] + tile[3 * i + 1 : 3 * i + 2] + tile[3 * i + 2 : 3 * i + 3]
        for i in range(count)
    ]


def sum_core_kernel(place, keep, got, send, *, tail_rows, tail_count):
    total = keep[...] + got[...].astype(f32)
    send[...] = total.astype(bf16)

    @pl.when(place[1] == 1)
    def _():
        first = total.shape[0] - tail_rows
        values = tail_values(total[first:, :], tail_count)
        send[first:, :] = tail_tile(values, tail_rows).astype(bf16)


def sum_kernel(got, send):
    part = jnp.sum(got[...].astype(f32), axis=0).astype(bf16)
    for k in range(send.shape[0]):
        send[k] = part


def unpack_kernel(place, mine, other, base_row, grad_in, grad_bias, grad_out, got):
    feat, hid = grad_in.shape
    vec_width = grad_out.shape[1]
    half = mine.shape[0]
    core = place[1]
    got[pl.ds(pl.multiple_of(core * half, half), half), :] = mine[...]
    got[pl.ds(pl.multiple_of((1 - core) * half, half), half), :] = other[...]
    base = 0
    for k in range(0, feat, LANES):
        grad_in[k : k + LANES, :] = got[base : base + hid, :].astype(f32).T
        base += hid
    start = base + vec_width * (hid // LANES)
    values = tail_values(got[start : start + 16, :].astype(f32), hid // LANES + 1)
    vec_sum = values[-1]
    sub = lax.broadcasted_iota(jnp.int32, (META, LANES), 0)
    zero = jnp.zeros((META, LANES), f32)
    vec_rows = zero
    for p, part in enumerate(split3(vec_sum)):
        vec_rows = jnp.where(sub == p, part, vec_rows)
    vec_rows = vec_rows.astype(bf16)
    for i, k in enumerate(range(0, hid, LANES)):
        base_rows = base_row[:, k : k + LANES].astype(bf16)
        outer = dot(base_rows, vec_rows, 0, 0)
        grad_out[k : k + LANES, :] = got[base : base + vec_width, :].astype(f32).T + outer
        grad_bias[k : k + LANES] = values[i].reshape(LANES)
        base += vec_width


def exchange(x, axis):
    return lax.all_to_all(x, axis, split_axis=0, concat_axis=0, tiled=True)


def shape_of(shape, dtype):
    return jax.ShapeDtypeStruct(shape, dtype)


def local(query_frames, line_frames, frame_count, line_home, mined, positive, w_in, bias_in, w_out):
    query_count, query_len, feat = query_frames.shape
    line_count, line_len, _ = line_frames.shape
    hid, vec_width = w_out.shape
    chip_count = lax.axis_size("chip")
    owner_count = chip_count * lax.axis_size("core")
    dp_count = lax.axis_size("dp")
    loss_factor = LOSS_SCALE / (query_count * owner_count * dp_count)
    frames_q = query_count * query_len
    frames_l = line_count * line_len
    frames = frames_q + frames_l
    rows = CAP * query_len
    xq = query_frames.reshape(frames_q, feat)
    xl = line_frames.reshape(frames_l, feat)
    place = jnp.stack([lax.axis_index(ARCHIVE), lax.axis_index("core")]).astype(jnp.int32)
    wire = shape_of((owner_count, rows + META, vec_width), bf16)
    head_flops = 2 * hid * (feat + vec_width)

    (asked,) = call(
        ask_kernel,
        [wire],
        [mined, line_home, positive, xq, w_in, bias_in, w_out],
        0,
        [
            pltpu.SMEM(mined.shape, jnp.int32),
            pltpu.SMEM(line_home.shape, jnp.int32),
            pltpu.SMEM(positive.shape, jnp.int32),
            pltpu.VMEM(xq.shape, bf16),
            pltpu.VMEM(w_in.shape, bf16),
            pltpu.VMEM(bias_in.shape, f32),
            pltpu.VMEM(w_out.shape, bf16),
            pltpu.VMEM((frames_q, vec_width), bf16),
            pltpu.SMEM((CAP, owner_count), jnp.int32),
            pltpu.SMEM((CAP, owner_count), jnp.int32),
            pltpu.SMEM((owner_count,), jnp.int32),
            pltpu.SMEM(mined.shape, jnp.int32),
            pltpu.SemaphoreType.DMA((7,)),
        ],
        flops=frames_q * head_flops,
        where=pltpu.HBM,
        limit=63 << 20,
    )
    got = exchange(asked, ARCHIVE)
    line_vec, line_vec_t, hidden_all, slope_t, mean = call(
        head_kernel,
        [
            shape_of((line_count, line_len, vec_width), bf16),
            shape_of((line_count, vec_width, line_len), bf16),
            shape_of((frames, hid), bf16),
            shape_of((hid, frames), f32),
            shape_of((META, LANES), f32),
        ],
        [xl, xq, w_in, bias_in, w_out],
        0,
        flops=frames * head_flops,
        transcendentals=frames * hid,
    )
    match_flops = 2 * owner_count * rows * frames_l * vec_width
    answer, weights, own = call(
        match_kernel,
        [
            wire,
            shape_of((owner_count, rows, line_len), bf16),
            shape_of((META, LANES), f32),
        ],
        [place, frame_count, got, line_vec, line_vec_t, mean],
        2,
        [
            pltpu.VMEM((line_count, LANES), f32),
            pltpu.VMEM((META, LANES), jnp.int32),
            pltpu.SMEM((META, LANES), jnp.int32),
            pltpu.VMEM((LANES, LANES), f32),
            pltpu.SemaphoreType.DMA(()),
        ],
        flops=2 * match_flops,
    )
    back = exchange(answer, ARCHIVE)
    unit = 16 * owner_count
    flat_rows = unit * -(-(LANES + (feat + vec_width) * hid // LANES) // unit)
    half = flat_rows // 2

    def grads_body(*refs):
        grad_kernel(*refs, loss_factor=loss_factor)

    loss, keep, give, base_row = call(
        grads_body,
        [
            shape_of((META, LANES), f32),
            shape_of((half, LANES), f32),
            shape_of((half, LANES), bf16),
            shape_of((META, hid), f32),
        ],
        [place, back, got, weights, own, xl, xq, hidden_all, slope_t, w_out],
        1,
        [
            pltpu.VMEM((flat_rows, LANES), f32),
            pltpu.VMEM((owner_count, META, LANES), f32),
            pltpu.VMEM((owner_count, META, LANES), f32),
            pltpu.VMEM((vec_width, frames_l), f32),
            pltpu.VMEM((vec_width, frames_q), f32),
        ],
        flops=match_flops + 4 * frames * head_flops,
    )
    swap = [(0, 1), (1, 0)]
    share = half // chip_count
    taken = lax.ppermute(give, "core", swap)
    tail_rows = flat_rows - (feat + vec_width) * hid // LANES

    def sum_core_body(*refs):
        sum_core_kernel(*refs, tail_rows=tail_rows, tail_count=hid // LANES + 1)

    (part,) = call(sum_core_body, [shape_of((half, LANES), bf16)], [place, keep, taken], 1)
    parts = exchange(part.reshape(chip_count, share, LANES), "chip")
    (part,) = call(sum_kernel, [shape_of((dp_count, share, LANES), bf16)], [parts], 0)
    parts = exchange(part, "dp")
    (part,) = call(sum_kernel, [shape_of((chip_count, share, LANES), bf16)], [parts], 0)
    mine = exchange(part, "chip").reshape(half, LANES)
    other = lax.ppermute(mine, "core", swap)
    grad_in, grad_bias, grad_out = call(
        unpack_kernel,
        [shape_of((feat, hid), f32), shape_of((hid,), f32), shape_of((hid, vec_width), f32)],
        [place, mine, other, base_row],
        1,
        [pltpu.VMEM((flat_rows, LANES), bf16)],
    )
    return (loss[:query_count, 0], grad_in, grad_bias, grad_out)


def solution(mesh):
    devices = mesh.devices
    archive, dp = devices.shape
    mesh = Mesh(devices.reshape(archive // 2, 2, dp), ("chip", "core", "dp"))
    everywhere = ARCHIVE + ("dp",)
    placed = (
        P(everywhere, None, None),
        P(ARCHIVE, None, None),
        P(),
        P(),
        P(everywhere, None),
        P(everywhere),
        P(),
        P(),
        P(),
    )
    return jax.shard_map(
        local,
        mesh=mesh,
        in_specs=placed,
        out_specs=(P(everywhere), P(), P(), P()),
        check_vma=False,
    )
```

```python
import math

import jax
import jax.numpy as jnp
from jax import lax
from jax.experimental import pallas as pl
from jax.experimental.pallas import tpu as pltpu
from jax.sharding import Mesh, PartitionSpec as P

LOSS_SCALE = 4096.0
SCORE_SCALE = 4.0
LANES = 128
CAP = 2
HALF = LANES // CAP
META = 8
ASK_ROWS = 2
BACK_ROWS = 4
UNUSED = 100.0
FLOOR = -1e30
GELU_A = math.sqrt(2.0 / math.pi)
GELU_B = 0.044715
ARCHIVE = ("chip", "core")

f32 = jnp.float32
bf16 = jnp.bfloat16


def dot(a, b, ca=1, cb=0):
    return lax.dot_general(a, b, (((ca,), (cb,)), ((), ())), preferred_element_type=f32)


def split2(x):
    hi = x.astype(bf16)
    return hi, (x - hi.astype(f32)).astype(bf16)


def split3(x):
    hi = x.astype(bf16).astype(f32)
    mid = (x - hi).astype(bf16).astype(f32)
    return hi, mid, (x - hi - mid).astype(bf16).astype(f32)


def call(body, outs, args, smem_count, scratch=(), flops=0, transcendentals=0, where=pltpu.VMEM, limit=40 << 20):
    nbytes = sum(a.size * a.dtype.itemsize for a in list(args) + list(outs))
    vmem = pl.BlockSpec(memory_space=pltpu.VMEM)
    smem = pl.BlockSpec(memory_space=pltpu.SMEM)
    rest = pl.BlockSpec(memory_space=where)
    return pl.pallas_call(
        body,
        out_shape=tuple(outs),
        in_specs=[smem] * smem_count + [rest] * (len(args) - smem_count),
        out_specs=tuple(vmem for _ in outs),
        scratch_shapes=list(scratch),
        compiler_params=pltpu.CompilerParams(vmem_limit_bytes=limit),
        cost_estimate=pl.CostEstimate(
            flops=flops, bytes_accessed=nbytes, transcendentals=transcendentals
        ),
    )(*args)


def gelu_parts(pre):
    t = jnp.tanh(GELU_A * (pre + GELU_B * pre * pre * pre))
    return t, (0.5 * pre * (1.0 + t)).astype(bf16)


def ask_kernel(
    mined_hbm, home_hbm, positive_hbm, x_hbm, w_in_hbm, bias_hbm, w_out_hbm, send, mined, home, positive, x, w_in, bias, w_out, vec, stage, rid, code, count, goal_owner, goal_rank, sems
):
    query_count, mined_count = mined.shape
    owner_count, rows, _ = stage.shape
    query_len = x.shape[0] // query_count
    line_count = home.shape[0] // owner_count
    stride = rows + ASK_ROWS
    pairs = (
        (mined_hbm, mined),
        (home_hbm, home),
        (positive_hbm, positive),
        (x_hbm, x),
        (w_in_hbm, w_in),
        (bias_hbm, bias),
        (w_out_hbm, w_out),
    )
    copies = [pltpu.make_async_copy(a, b, sems.at[i]) for i, (a, b) in enumerate(pairs)]
    for copy in copies:
        copy.start()

    def clear(owner, carry):
        count[owner] = 0
        for c in range(CAP):
            rid[c, owner] = int(UNUSED)
            code[c, owner] = int(UNUSED)
        return carry

    lax.fori_loop(0, owner_count, clear, 0, unroll=8)
    stage[...] = jnp.zeros(stage.shape, bf16)
    for copy in copies[:3]:
        copy.wait()

    def assign(query, carry):
        for j in range(mined_count):
            row = home[mined[query, j]]
            owner = row // line_count
            rank = count[owner]
            count[owner] = rank + 1
            rid[rank, owner] = row - owner * line_count
            code[rank, owner] = query + jnp.where(positive[query] == j, 8, 0)
            goal_owner[query, j] = owner
            goal_rank[query, j] = rank * query_len
        return carry

    lax.fori_loop(0, query_count, assign, 0, unroll=2)
    sub = lax.broadcasted_iota(jnp.int32, (ASK_ROWS, LANES), 0)
    low = lax.broadcasted_iota(jnp.int32, (ASK_ROWS, LANES), 1) < HALF
    for owner in range(owner_count):
        tile = jnp.where(
            sub == 0,
            jnp.where(low, rid[0, owner], rid[1, owner]),
            jnp.where(low, code[0, owner], code[1, owner]),
        )
        first = owner * stride + rows
        send[first : first + ASK_ROWS, :] = tile.astype(f32).astype(bf16)
    for copy in copies[3:]:
        copy.wait()
    _, hidden = gelu_parts(dot(x[...], w_in[...]) + bias[...].reshape(1, -1))
    vec[...] = dot(hidden, w_out[...]).astype(bf16)

    def place(query, carry):
        block = vec[pl.ds(pl.multiple_of(query * query_len, query_len), query_len), :]
        for j in range(mined_count):
            first = pl.multiple_of(goal_rank[query, j], query_len)
            stage[goal_owner[query, j], pl.ds(first, query_len), :] = block
        return carry

    lax.fori_loop(0, query_count, place, 0, unroll=4)
    for owner in range(owner_count):
        send[owner * stride : owner * stride + rows, :] = stage[owner]


def head_kernel(xl, xq, w_in, bias, w_out, line_vec, line_vec_t, hidden_all, slope_t, mean):
    step = 256
    line_frames = xl.shape[0]
    total = jnp.zeros((1, hidden_all.shape[1]), f32)
    for first in range(0, line_frames + xq.shape[0], step):
        if first < line_frames:
            x = xl[first : first + step, :]
        else:
            x = xq[first - line_frames : first - line_frames + step, :]
        size = x.shape[0]
        pre = dot(x, w_in[...]) + bias[...].reshape(1, -1)
        t, hidden = gelu_parts(pre)
        slope = 0.5 * (1.0 + t) + 0.5 * pre * (1.0 - t * t) * GELU_A * (
            1.0 + 3.0 * GELU_B * pre * pre
        )
        hidden_all[first : first + size, :] = hidden
        slope_t[:, first : first + size] = slope.T
        if first < line_frames:
            vec = dot(hidden, w_out[...])
            for k in range(0, size, LANES):
                line = (first + k) // LANES
                line_vec[line] = vec[k : k + LANES].astype(bf16)
                line_vec_t[line] = vec[k : k + LANES].T.astype(bf16)
            total += jnp.sum(hidden.astype(f32), axis=0, keepdims=True)
    mean[...] = jnp.broadcast_to(total * (1.0 / line_frames), mean.shape)


def spread(meta, first, query_len):
    parts = []
    for b in range(meta.shape[0]):
        for c in range(CAP):
            parts.append(jnp.broadcast_to(meta[b, first + c : first + c + 1, :], (query_len, LANES)))
    return jnp.concatenate(parts, axis=0)


def match_kernel(
    place, counts, got, line_vec, line_vec_t, mean, send, weights, own, pads, label_rows, ids, sums, sem
):
    owner_count, rows, _ = weights.shape
    query_len = rows // CAP
    stride, out_stride = rows + ASK_ROWS, rows + BACK_ROWS
    line_count, _, vec_width = line_vec.shape
    scale = SCORE_SCALE / math.sqrt(vec_width)
    lane1 = lax.broadcasted_iota(jnp.int32, (1, LANES), 1)
    lane2 = lax.broadcasted_iota(jnp.int32, (ASK_ROWS, LANES), 1) % HALF
    labels = jnp.full((ASK_ROWS, LANES), UNUSED, f32)
    for b in range(owner_count):
        first = b * stride + rows
        labels = jnp.where(lane2 == b, got[first : first + ASK_ROWS, :].astype(f32), labels)
    rid_row, code_row = labels[0:1], labels[1:2]
    rid_row = jnp.where(rid_row < line_count, rid_row, 0.0)
    label_rows[...] = jnp.broadcast_to(rid_row, (META, LANES)).astype(jnp.int32)
    copy = pltpu.make_async_copy(label_rows, ids, sem)
    copy.start()
    for r in range(line_count):
        pads[r : r + 1, :] = jnp.where(lane1 < counts[place[0] * line_count + r], 0.0, FLOOR)
    sums[...] = jnp.zeros(sums.shape, f32)
    ones = jnp.ones((LANES, LANES), bf16)
    copy.wait()
    for b in range(owner_count):
        for c in range(CAP):
            slot = b + HALF * c
            r = ids[0, slot]
            first = b * stride + c * query_len
            logits = dot(got[first : first + query_len, :], line_vec_t[r]) * scale
            logits = logits + pads[pl.ds(r, 1), :]
            peak = jnp.max(logits, axis=1, keepdims=True)
            scaled = jnp.exp(logits - peak).astype(bf16)
            both = dot(scaled, jnp.concatenate([line_vec[r], ones], axis=1))
            totals = both[:, vec_width:]
            inverse = 1.0 / totals
            weights[b, c * query_len : (c + 1) * query_len, :] = (
                scaled.astype(f32) * inverse
            ).astype(bf16)
            first = b * out_stride + c * query_len
            send[first : first + query_len, :] = (both[:, :vec_width] * inverse).astype(bf16)
            log_total = peak + jnp.log(totals)
            sums[slot : slot + 1, :] = jnp.sum(log_total, axis=0, keepdims=True) * (1.0 / query_len)
    lane = lax.broadcasted_iota(jnp.int32, sums.shape, 1)
    row = lax.broadcasted_iota(jnp.int32, sums.shape, 0)
    match_row = jnp.sum(jnp.where(lane == row, sums[...], 0.0), axis=0, keepdims=True)
    high, low = (part.astype(f32) for part in split2(match_row))
    blocks = own_blocks(mean.shape[1])
    mean_row = mean[:, 0:LANES]
    for k in range(1, blocks):
        mean_row = jnp.where(place[0] % blocks == k, mean[:, k * LANES : (k + 1) * LANES], mean_row)
    sub = lax.broadcasted_iota(jnp.int32, (META, LANES), 0)
    own[...] = jnp.where(sub == 0, high + low, jnp.where(sub == 1, code_row, rid_row))
    sub = lax.broadcasted_iota(jnp.int32, (BACK_ROWS, LANES), 0)
    tile = jnp.where(
        sub == 0, high, jnp.where(sub == 1, low, jnp.where(sub == 2, code_row, mean_row[0:1]))
    ).astype(bf16)
    for b in range(owner_count):
        first = b * out_stride + rows
        send[first : first + BACK_ROWS, :] = tile


def own_blocks(hid):
    return hid // LANES


def grad_kernel(
    place, back, got, weights, own, xl, xq, hidden_all, slope_t, w_out, loss, keep, give, base_row, grads, own_scale, ask_scale, line_acc, query_acc, *, loss_factor
):
    owner_count, rows, _ = weights.shape
    stride, back_stride = rows + ASK_ROWS, rows + BACK_ROWS
    query_len = rows // CAP
    line_total = xl.shape[0]
    line_count = line_total // LANES
    query_frames = xq.shape[0]
    vec_width = w_out.shape[1]
    hid = w_out.shape[0]
    blocks = own_blocks(hid)
    me = place[0]

    shape3 = (owner_count, META, LANES)
    lane3 = lax.broadcasted_iota(jnp.int32, shape3, 2)
    sub3 = lax.broadcasted_iota(jnp.int32, shape3, 1)
    owner3 = lax.broadcasted_iota(jnp.int32, shape3, 0)
    subf = sub3.astype(f32)
    matches, codes = [], []
    shared = [jnp.zeros((1, LANES), f32) for _ in range(blocks)]
    for owner in range(owner_count):
        first = owner * back_stride + rows
        tile = back[first : first + BACK_ROWS, :].astype(f32)
        matches.append(jnp.broadcast_to(tile[0:1] + tile[1:2], (1, META, LANES)))
        codes.append(jnp.broadcast_to(tile[2:3], (1, META, LANES)))
        shared[owner % blocks] += tile[3:4]
    match = jnp.concatenate(matches, axis=0)
    code = jnp.concatenate(codes, axis=0)
    shared = [
        part * (1.0 / ((owner_count - k + blocks - 1) // blocks)) for k, part in enumerate(shared)
    ]
    shared = jnp.concatenate(shared, axis=1).astype(bf16).astype(f32)
    base_row[...] = jnp.broadcast_to(shared, base_row.shape)
    is_pos = (code >= 8.0) & (code < 16.0)
    query_of = jnp.where(is_pos, code - 8.0, code)
    here = query_of == subf
    peak = jnp.max(jnp.where(here, match, FLOOR), axis=0)
    peak = jnp.maximum(peak, pltpu.roll(peak, HALF, 1))
    raised = jnp.where(here, jnp.exp(match - peak[None]), 0.0)
    total = jnp.sum(raised, axis=0)
    total = total + pltpu.roll(total, HALF, 1)
    total = jnp.where(total > 0.0, total, 1.0)
    chosen = jnp.sum(jnp.where(here & is_pos, match, 0.0), axis=0)
    chosen = chosen + pltpu.roll(chosen, HALF, 1)
    log_total = peak + jnp.log(total)
    lane2 = lax.broadcasted_iota(jnp.int32, (META, LANES), 1)
    sub2 = lax.broadcasted_iota(jnp.int32, (META, LANES), 0).astype(f32)
    picked = jnp.sum(jnp.where(lane2 == me, log_total - chosen, 0.0), axis=1, keepdims=True)
    loss[...] = jnp.broadcast_to(picked, (META, LANES))

    factor = loss_factor * SCORE_SCALE / (math.sqrt(vec_width) * query_len)

    own_match = own[0:1, :]
    own_code = own[1:2, :]
    own_pos = (own_code >= 8.0) & (own_code < 16.0)
    own_query = jnp.where(own_pos, own_code - 8.0, own_code)
    own_grad = jnp.exp(jnp.minimum(own_match - log_total, 0.0)) - jnp.where(own_pos, 1.0, 0.0)
    own_grad = factor * jnp.sum(jnp.where(own_query == sub2, own_grad, 0.0), axis=0, keepdims=True)
    both = jnp.where(lane2 >= 0, jnp.where(sub2 < CAP, own_grad, own[2:3, :]), 0.0)
    slot3 = HALF * (sub3 % CAP)
    own_scale[...] = jnp.broadcast_to(
        jnp.sum(
            jnp.where(lane3 == owner3 + slot3, jnp.broadcast_to(both[None], shape3), 0.0),
            axis=2,
            keepdims=True,
        ),
        shape3,
    )

    ask_grad = raised * (1.0 / total)[None] - jnp.where(here & is_pos, 1.0, 0.0)
    ask_grad = factor * jnp.sum(ask_grad, axis=1, keepdims=True)
    both = jnp.where(sub3 < CAP, jnp.broadcast_to(ask_grad, shape3), query_of)
    ask_scale[...] = jnp.broadcast_to(
        jnp.sum(jnp.where(lane3 == me + slot3, both, 0.0), axis=2, keepdims=True), shape3
    )

    size = owner_count * rows
    frame = (lax.broadcasted_iota(jnp.int32, (size, LANES), 0) % query_len).astype(f32)
    lane = lax.broadcasted_iota(jnp.int32, (size, LANES), 1).astype(f32)
    zero = jnp.zeros((size, LANES), bf16)
    one = jnp.ones((size, LANES), bf16)

    labels = own_scale[...]
    queries = jnp.concatenate(
        [got[b * stride : b * stride + rows, :] for b in range(owner_count)], axis=0
    )
    rid = spread(labels, CAP, query_len).astype(bf16)
    weight = weights[...].reshape(size, LANES).astype(f32)
    score = (weight * spread(labels, 0, query_len)).astype(bf16)
    wide = jnp.concatenate([jnp.where(rid == r, score, zero) for r in range(line_count)], axis=1)
    line_acc[...] = dot(queries, wide, 0, 0)

    labels = ask_scale[...]
    target = spread(labels, CAP, query_len) * float(query_len) + frame
    pulled = jnp.concatenate(
        [back[b * back_stride : b * back_stride + rows, :] for b in range(owner_count)], axis=0
    )
    pulled = (pulled.astype(f32) * spread(labels, 0, query_len)).astype(bf16)
    wide = jnp.concatenate(
        [
            jnp.where(target == lane + float(k), one, zero)
            for k in range(0, query_acc.shape[1], LANES)
        ],
        axis=1,
    )
    query_acc[...] = dot(pulled, wide, 0, 0)

    grad_in = None
    grad_out = None
    grad_bias = None
    vec_sum = None
    spans = ((line_acc, xl, 0, line_total), (query_acc, xq, line_total, query_frames))
    for acc, x, first, span in spans:
        g_hi, g_lo = split2(acc[:, 0:span])
        grad_hidden = dot(w_out[...], g_hi) + dot(w_out[...], g_lo)
        p_hi, p_lo = split2(grad_hidden * slope_t[:, first : first + span])
        hidden = hidden_all[first : first + span, :]
        ones = jnp.ones((META, span), bf16)
        part_in = dot(p_hi, x[...])
        part_out = dot(g_hi, hidden) + dot(g_lo, hidden)
        part_out -= jnp.sum(g_hi.astype(f32) + g_lo.astype(f32), axis=1, keepdims=True) * shared
        part_sum = dot(ones, g_hi, 1, 1) + dot(ones, g_lo, 1, 1)
        vec_sum = part_sum if vec_sum is None else vec_sum + part_sum
        part_bias = dot(ones, p_hi, 1, 1) + dot(ones, p_lo, 1, 1)
        grad_in = part_in if grad_in is None else grad_in + part_in
        grad_out = part_out if grad_out is None else grad_out + part_out
        grad_bias = part_bias if grad_bias is None else grad_bias + part_bias
    base = 0
    for k in range(0, x.shape[1], LANES):
        grads[base : base + hid, :] = grad_in[:, k : k + LANES]
        base += hid
    for k in range(0, hid, LANES):
        grads[base : base + vec_width, :] = grad_out[:, k : k + LANES]
        base += vec_width
    rest = grads.shape[0] - base
    singles = [grad_bias[0:1, k : k + LANES] for k in range(0, hid, LANES)] + [vec_sum[0:1, :]]
    grads[base:, :] = tail_tile(singles, rest)
    half = keep.shape[0]
    core = place[1]
    keep[...] = grads[pl.ds(pl.multiple_of(core * half, half), half), :]
    give[...] = grads[pl.ds(pl.multiple_of((1 - core) * half, half), half), :].astype(bf16)


def tail_tile(values, size):
    sub = lax.broadcasted_iota(jnp.int32, (size, LANES), 0)
    tile = jnp.zeros((size, LANES), f32)
    for i, value in enumerate(values):
        for p, part in enumerate(split3(value)):
            tile = jnp.where(sub == 3 * i + p, part, tile)
    return tile


def tail_values(tile, count):
    return [
        tile[3 * i : 3 * i + 1] + tile[3 * i + 1 : 3 * i + 2] + tile[3 * i + 2 : 3 * i + 3]
        for i in range(count)
    ]


def sum_core_kernel(place, keep, got, send, *, tail_rows, tail_count):
    total = keep[...] + got[...].astype(f32)
    send[...] = total.astype(bf16)

    @pl.when(place[1] == 1)
    def _():
        first = total.shape[0] - tail_rows
        values = tail_values(total[first:, :], tail_count)
        send[first:, :] = tail_tile(values, tail_rows).astype(bf16)


def sum_kernel(got, send):
    part = jnp.sum(got[...].astype(f32), axis=0).astype(bf16)
    for k in range(send.shape[0]):
        send[k] = part


def unpack_kernel(place, mine, other, base_row, grad_in, grad_bias, grad_out, got):
    feat, hid = grad_in.shape
    vec_width = grad_out.shape[1]
    half = mine.shape[0]
    core = place[1]
    got[pl.ds(pl.multiple_of(core * half, half), half), :] = mine[...]
    got[pl.ds(pl.multiple_of((1 - core) * half, half), half), :] = other[...]
    base = 0
    for k in range(0, feat, LANES):
        grad_in[k : k + LANES, :] = got[base : base + hid, :].astype(f32).T
        base += hid
    start = base + vec_width * (hid // LANES)
    values = tail_values(got[start : start + 16, :].astype(f32), hid // LANES + 1)
    vec_sum = values[-1]
    sub = lax.broadcasted_iota(jnp.int32, (META, LANES), 0)
    zero = jnp.zeros((META, LANES), f32)
    vec_rows = zero
    for p, part in enumerate(split3(vec_sum)):
        vec_rows = jnp.where(sub == p, part, vec_rows)
    vec_rows = vec_rows.astype(bf16)
    for i, k in enumerate(range(0, hid, LANES)):
        base_rows = base_row[:, k : k + LANES].astype(bf16)
        outer = dot(base_rows, vec_rows, 0, 0)
        grad_out[k : k + LANES, :] = got[base : base + vec_width, :].astype(f32).T + outer
        grad_bias[k : k + LANES] = values[i].reshape(LANES)
        base += vec_width


def exchange(x, axis):
    return lax.all_to_all(x, axis, split_axis=0, concat_axis=0, tiled=True)


def exchange_rows(x, axis, peers, tile):
    blocks = x.reshape(peers, x.shape[0] // (peers * tile), tile, x.shape[1])
    return exchange(blocks, axis).reshape(x.shape)


def shape_of(shape, dtype):
    return jax.ShapeDtypeStruct(shape, dtype)


def local(query_frames, line_frames, frame_count, line_home, mined, positive, w_in, bias_in, w_out):
    query_count, query_len, feat = query_frames.shape
    line_count, line_len, _ = line_frames.shape
    hid, vec_width = w_out.shape
    chip_count = lax.axis_size("chip")
    owner_count = chip_count * lax.axis_size("core")
    dp_count = lax.axis_size("dp")
    loss_factor = LOSS_SCALE / (query_count * owner_count * dp_count)
    frames_q = query_count * query_len
    frames_l = line_count * line_len
    frames = frames_q + frames_l
    rows = CAP * query_len
    xq = query_frames.reshape(frames_q, feat)
    xl = line_frames.reshape(frames_l, feat)
    place = jnp.stack([lax.axis_index(ARCHIVE), lax.axis_index("core")]).astype(jnp.int32)
    ask_wire = shape_of((owner_count * (rows + ASK_ROWS), vec_width), bf16)
    back_wire = shape_of((owner_count * (rows + BACK_ROWS), vec_width), bf16)
    head_flops = 2 * hid * (feat + vec_width)

    (asked,) = call(
        ask_kernel,
        [ask_wire],
        [mined, line_home, positive, xq, w_in, bias_in, w_out],
        0,
        [
            pltpu.SMEM(mined.shape, jnp.int32),
            pltpu.SMEM(line_home.shape, jnp.int32),
            pltpu.SMEM(positive.shape, jnp.int32),
            pltpu.VMEM(xq.shape, bf16),
            pltpu.VMEM(w_in.shape, bf16),
            pltpu.VMEM(bias_in.shape, f32),
            pltpu.VMEM(w_out.shape, bf16),
            pltpu.VMEM((frames_q, vec_width), bf16),
            pltpu.VMEM((owner_count, rows, vec_width), bf16),
            pltpu.SMEM((CAP, owner_count), jnp.int32),
            pltpu.SMEM((CAP, owner_count), jnp.int32),
            pltpu.SMEM((owner_count,), jnp.int32),
            pltpu.SMEM(mined.shape, jnp.int32),
            pltpu.SMEM(mined.shape, jnp.int32),
            pltpu.SemaphoreType.DMA((7,)),
        ],
        flops=frames_q * head_flops,
        where=pltpu.HBM,
        limit=63 << 20,
    )
    got = exchange_rows(asked, ARCHIVE, owner_count, ASK_ROWS)
    line_vec, line_vec_t, hidden_all, slope_t, mean = call(
        head_kernel,
        [
            shape_of((line_count, line_len, vec_width), bf16),
            shape_of((line_count, vec_width, line_len), bf16),
            shape_of((frames, hid), bf16),
            shape_of((hid, frames), f32),
            shape_of((META, hid), f32),
        ],
        [xl, xq, w_in, bias_in, w_out],
        0,
        flops=frames * head_flops,
        transcendentals=frames * hid,
    )
    match_flops = 2 * owner_count * rows * frames_l * vec_width
    answer, weights, own = call(
        match_kernel,
        [
            back_wire,
            shape_of((owner_count, rows, line_len), bf16),
            shape_of((META, LANES), f32),
        ],
        [place, frame_count, got, line_vec, line_vec_t, mean],
        2,
        [
            pltpu.VMEM((line_count, LANES), f32),
            pltpu.VMEM((META, LANES), jnp.int32),
            pltpu.SMEM((META, LANES), jnp.int32),
            pltpu.VMEM((LANES, LANES), f32),
            pltpu.SemaphoreType.DMA(()),
        ],
        flops=2 * match_flops,
    )
    back = exchange_rows(answer, ARCHIVE, owner_count, BACK_ROWS)
    unit = 16 * owner_count
    flat_rows = unit * -(-(LANES + (feat + vec_width) * hid // LANES) // unit)
    half = flat_rows // 2

    def grads_body(*refs):
        grad_kernel(*refs, loss_factor=loss_factor)

    loss, keep, give, base_row = call(
        grads_body,
        [
            shape_of((META, LANES), f32),
            shape_of((half, LANES), f32),
            shape_of((half, LANES), bf16),
            shape_of((META, hid), f32),
        ],
        [place, back, got, weights, own, xl, xq, hidden_all, slope_t, w_out],
        1,
        [
            pltpu.VMEM((flat_rows, LANES), f32),
            pltpu.VMEM((owner_count, META, LANES), f32),
            pltpu.VMEM((owner_count, META, LANES), f32),
            pltpu.VMEM((vec_width, frames_l), f32),
            pltpu.VMEM((vec_width, frames_q), f32),
        ],
        flops=match_flops + 4 * frames * head_flops,
    )
    swap = [(0, 1), (1, 0)]
    share = half // chip_count
    taken = lax.ppermute(give, "core", swap)
    tail_rows = flat_rows - (feat + vec_width) * hid // LANES

    def sum_core_body(*refs):
        sum_core_kernel(*refs, tail_rows=tail_rows, tail_count=hid // LANES + 1)

    (part,) = call(sum_core_body, [shape_of((half, LANES), bf16)], [place, keep, taken], 1)
    parts = exchange(part.reshape(chip_count, share, LANES), "chip")
    (part,) = call(sum_kernel, [shape_of((dp_count, share, LANES), bf16)], [parts], 0)
    parts = exchange(part, "dp")
    (part,) = call(sum_kernel, [shape_of((chip_count, share, LANES), bf16)], [parts], 0)
    mine = exchange(part, "chip").reshape(half, LANES)
    other = lax.ppermute(mine, "core", swap)
    grad_in, grad_bias, grad_out = call(
        unpack_kernel,
        [shape_of((feat, hid), f32), shape_of((hid,), f32), shape_of((hid, vec_width), f32)],
        [place, mine, other, base_row],
        1,
        [pltpu.VMEM((flat_rows, LANES), bf16)],
    )
    return (loss[:query_count, 0], grad_in, grad_bias, grad_out)


def solution(mesh):
    devices = mesh.devices
    archive, dp = devices.shape
    mesh = Mesh(devices.reshape(archive // 2, 2, dp), ("chip", "core", "dp"))
    everywhere = ARCHIVE + ("dp",)
    placed = (
        P(everywhere, None, None),
        P(ARCHIVE, None, None),
        P(),
        P(),
        P(everywhere, None),
        P(everywhere),
        P(),
        P(),
        P(),
    )
    return jax.shard_map(
        local,
        mesh=mesh,
        in_specs=placed,
        out_specs=(P(everywhere), P(), P(), P()),
        check_vma=False,
    )
```

```python
import math

import jax
import jax.numpy as jnp
from jax import lax
from jax.experimental import pallas as pl
from jax.experimental.pallas import tpu as pltpu
from jax.sharding import Mesh, PartitionSpec as P

LOSS_SCALE = 4096.0
SCORE_SCALE = 4.0
LANES = 128
CAP = 2
HALF = LANES // CAP
META = 8
ASK_ROWS = 2
BACK_ROWS = 4
GROUP = 8
UNUSED = 100.0
FLOOR = -1e30
GELU_A = math.sqrt(2.0 / math.pi)
GELU_B = 0.044715
ARCHIVE = ("chip", "core")

f32 = jnp.float32
bf16 = jnp.bfloat16


def dot(a, b, ca=1, cb=0):
    return lax.dot_general(a, b, (((ca,), (cb,)), ((), ())), preferred_element_type=f32)


def split2(x):
    hi = x.astype(bf16)
    return hi, (x - hi.astype(f32)).astype(bf16)


def split3(x):
    hi = x.astype(bf16).astype(f32)
    mid = (x - hi).astype(bf16).astype(f32)
    return hi, mid, (x - hi - mid).astype(bf16).astype(f32)


def call(body, outs, args, smem_count, scratch=(), flops=0, transcendentals=0, where=pltpu.VMEM, limit=40 << 20):
    nbytes = sum(a.size * a.dtype.itemsize for a in list(args) + list(outs))
    vmem = pl.BlockSpec(memory_space=pltpu.VMEM)
    smem = pl.BlockSpec(memory_space=pltpu.SMEM)
    rest = pl.BlockSpec(memory_space=where)
    return pl.pallas_call(
        body,
        out_shape=tuple(outs),
        in_specs=[smem] * smem_count + [rest] * (len(args) - smem_count),
        out_specs=tuple(vmem for _ in outs),
        scratch_shapes=list(scratch),
        compiler_params=pltpu.CompilerParams(vmem_limit_bytes=limit),
        cost_estimate=pl.CostEstimate(
            flops=flops, bytes_accessed=nbytes, transcendentals=transcendentals
        ),
    )(*args)


def gelu_parts(pre):
    t = jnp.tanh(GELU_A * (pre + GELU_B * pre * pre * pre))
    return t, (0.5 * pre * (1.0 + t)).astype(bf16)


def ask_kernel(
    mined_hbm, home_hbm, positive_hbm, x_hbm, w_in_hbm, bias_hbm, w_out_hbm, send, mined, home, positive, x, w_in, bias, w_out, vec, stage, rid, code, count, goal_owner, goal_rank, sems
):
    query_count, mined_count = mined.shape
    owner_count, rows, _ = stage.shape
    query_len = x.shape[0] // query_count
    line_count = home.shape[0] // owner_count
    stride = rows + ASK_ROWS
    pairs = (
        (mined_hbm, mined),
        (home_hbm, home),
        (positive_hbm, positive),
        (x_hbm, x),
        (w_in_hbm, w_in),
        (bias_hbm, bias),
        (w_out_hbm, w_out),
    )
    copies = [pltpu.make_async_copy(a, b, sems.at[i]) for i, (a, b) in enumerate(pairs)]
    for copy in copies:
        copy.start()

    def clear(owner, carry):
        count[owner] = 0
        for c in range(CAP):
            rid[c, owner] = int(UNUSED)
            code[c, owner] = int(UNUSED)
        return carry

    lax.fori_loop(0, owner_count, clear, 0, unroll=8)
    stage[...] = jnp.zeros(stage.shape, bf16)
    for copy in copies[:3]:
        copy.wait()

    def assign(query, carry):
        for j in range(mined_count):
            row = home[mined[query, j]]
            owner = row // line_count
            rank = count[owner]
            count[owner] = rank + 1
            rid[rank, owner] = row - owner * line_count
            code[rank, owner] = query + jnp.where(positive[query] == j, 8, 0)
            goal_owner[query, j] = owner
            goal_rank[query, j] = rank * query_len
        return carry

    lax.fori_loop(0, query_count, assign, 0, unroll=2)
    sub = lax.broadcasted_iota(jnp.int32, (ASK_ROWS, LANES), 0)
    low = lax.broadcasted_iota(jnp.int32, (ASK_ROWS, LANES), 1) < HALF
    for owner in range(owner_count):
        tile = jnp.where(
            sub == 0,
            jnp.where(low, rid[0, owner], rid[1, owner]),
            jnp.where(low, code[0, owner], code[1, owner]),
        )
        first = owner * stride + rows
        send[first : first + ASK_ROWS, :] = tile.astype(f32).astype(bf16)
    for copy in copies[3:]:
        copy.wait()
    _, hidden = gelu_parts(dot(x[...], w_in[...]) + bias[...].reshape(1, -1))
    vec[...] = dot(hidden, w_out[...]).astype(bf16)

    def place(query, carry):
        block = vec[pl.ds(pl.multiple_of(query * query_len, query_len), query_len), :]
        for j in range(mined_count):
            first = pl.multiple_of(goal_rank[query, j], query_len)
            stage[goal_owner[query, j], pl.ds(first, query_len), :] = block
        return carry

    lax.fori_loop(0, query_count, place, 0, unroll=4)
    for owner in range(owner_count):
        send[owner * stride : owner * stride + rows, :] = stage[owner]


def head_kernel(xl, xq, w_in, bias, w_out, line_vec, line_vec_t, hidden_all, slope_t, mean):
    step = 256
    line_frames = xl.shape[0]
    total = jnp.zeros((1, hidden_all.shape[1]), f32)
    for first in range(0, line_frames + xq.shape[0], step):
        if first < line_frames:
            x = xl[first : first + step, :]
        else:
            x = xq[first - line_frames : first - line_frames + step, :]
        size = x.shape[0]
        pre = dot(x, w_in[...]) + bias[...].reshape(1, -1)
        t, hidden = gelu_parts(pre)
        slope = 0.5 * (1.0 + t) + 0.5 * pre * (1.0 - t * t) * GELU_A * (
            1.0 + 3.0 * GELU_B * pre * pre
        )
        hidden_all[first : first + size, :] = hidden
        slope_t[:, first : first + size] = slope.T
        if first < line_frames:
            vec = dot(hidden, w_out[...])
            for k in range(0, size, LANES):
                line = (first + k) // LANES
                line_vec[line] = vec[k : k + LANES].astype(bf16)
                line_vec_t[line] = vec[k : k + LANES].T.astype(bf16)
            total += jnp.sum(hidden.astype(f32), axis=0, keepdims=True)
    mean[...] = jnp.broadcast_to(total * (1.0 / line_frames), mean.shape)


def spread(meta, first, query_len):
    parts = []
    for b in range(meta.shape[0]):
        for c in range(CAP):
            parts.append(jnp.broadcast_to(meta[b, first + c : first + c + 1, :], (query_len, LANES)))
    return jnp.concatenate(parts, axis=0)


def match_kernel(
    place, counts, got, line_vec, line_vec_t, mean, send, weights, own, pads, label_rows, ids, sums, sem
):
    owner_count, rows, _ = weights.shape
    query_len = rows // CAP
    stride, out_stride = rows + ASK_ROWS, rows + BACK_ROWS
    line_count, _, vec_width = line_vec.shape
    scale = SCORE_SCALE / math.sqrt(vec_width)
    lane1 = lax.broadcasted_iota(jnp.int32, (1, LANES), 1)
    lane2 = lax.broadcasted_iota(jnp.int32, (ASK_ROWS, LANES), 1) % HALF
    labels = jnp.full((ASK_ROWS, LANES), UNUSED, f32)
    for b in range(owner_count):
        first = b * stride + rows
        labels = jnp.where(lane2 == b, got[first : first + ASK_ROWS, :].astype(f32), labels)
    rid_row, code_row = labels[0:1], labels[1:2]
    rid_row = jnp.where(rid_row < line_count, rid_row, 0.0)
    label_rows[...] = jnp.broadcast_to(rid_row, (META, LANES)).astype(jnp.int32)
    copy = pltpu.make_async_copy(label_rows, ids, sem)
    copy.start()
    for r in range(line_count):
        pads[r : r + 1, :] = jnp.where(lane1 < counts[place[0] * line_count + r], 0.0, FLOOR)
    sums[...] = jnp.zeros(sums.shape, f32)
    ones = jnp.ones((LANES, LANES), bf16)
    copy.wait()
    for b in range(owner_count):
        for c in range(CAP):
            slot = b + HALF * c
            r = ids[0, slot]
            first = b * stride + c * query_len
            logits = dot(got[first : first + query_len, :], line_vec_t[r]) * scale
            logits = logits + pads[pl.ds(r, 1), :]
            peak = jnp.max(logits, axis=1, keepdims=True)
            scaled = jnp.exp(logits - peak).astype(bf16)
            both = dot(scaled, jnp.concatenate([line_vec[r], ones], axis=1))
            totals = both[:, vec_width:]
            inverse = 1.0 / totals
            weights[b, c * query_len : (c + 1) * query_len, :] = (
                scaled.astype(f32) * inverse
            ).astype(bf16)
            first = b * out_stride + c * query_len
            send[first : first + query_len, :] = (both[:, :vec_width] * inverse).astype(bf16)
            log_total = peak + jnp.log(totals)
            sums[slot : slot + 1, :] = jnp.sum(log_total, axis=0, keepdims=True) * (1.0 / query_len)
    lane = lax.broadcasted_iota(jnp.int32, sums.shape, 1)
    row = lax.broadcasted_iota(jnp.int32, sums.shape, 0)
    match_row = jnp.sum(jnp.where(lane == row, sums[...], 0.0), axis=0, keepdims=True)
    high, low = (part.astype(f32) for part in split2(match_row))
    blocks = own_blocks(mean.shape[1])
    mean_row = mean[:, 0:LANES]
    for k in range(1, blocks):
        mean_row = jnp.where(place[0] % blocks == k, mean[:, k * LANES : (k + 1) * LANES], mean_row)
    sub = lax.broadcasted_iota(jnp.int32, (META, LANES), 0)
    own[...] = jnp.where(sub == 0, high + low, jnp.where(sub == 1, code_row, rid_row))
    sub = lax.broadcasted_iota(jnp.int32, (BACK_ROWS, LANES), 0)
    tile = jnp.where(
        sub == 0, high, jnp.where(sub == 1, low, jnp.where(sub == 2, code_row, mean_row[0:1]))
    ).astype(bf16)
    for b in range(owner_count):
        first = b * out_stride + rows
        send[first : first + BACK_ROWS, :] = tile


def widen_kernel(weights, own, got, wide, queries, labels):
    owner_count, rows, _ = weights.shape
    query_len = rows // CAP
    stride = rows + ASK_ROWS
    size = GROUP * rows
    lane = lax.broadcasted_iota(jnp.int32, (LANES, LANES), 1)
    row = lax.broadcasted_iota(jnp.int32, (LANES, LANES), 0)
    rid = jnp.sum(jnp.where(lane == row, own[2:3, :], 0.0), axis=1, keepdims=True)
    labels[...] = jnp.broadcast_to(rid, (LANES, LANES))
    zero = jnp.zeros((size, LANES), bf16)
    for first in range(0, owner_count, GROUP):
        weight = weights[first : first + GROUP].reshape(size, LANES)
        parts = []
        for b in range(first, first + GROUP):
            for c in range(CAP):
                slot = b + HALF * c
                parts.append(jnp.broadcast_to(labels[slot : slot + 1, :], (query_len, LANES)))
            queries[b * rows : (b + 1) * rows, :] = got[b * stride : b * stride + rows, :]
        rid = jnp.concatenate(parts, axis=0).astype(bf16)
        for r in range(wide.shape[1] // LANES):
            wide[first * rows : first * rows + size, r * LANES : (r + 1) * LANES] = jnp.where(
                rid == r, weight, zero
            )


def own_blocks(hid):
    return hid // LANES


def grad_kernel(
    place, back, queries, wide, own, xl, xq, hidden_all, slope_t, w_out, loss, keep, give, base_row, grads, own_scale, ask_scale, line_acc, query_acc, *, loss_factor
):
    owner_count = own_scale.shape[0]
    rows = queries.shape[0] // owner_count
    back_stride = rows + BACK_ROWS
    query_len = rows // CAP
    line_total = xl.shape[0]
    line_count = line_total // LANES
    query_frames = xq.shape[0]
    vec_width = w_out.shape[1]
    hid = w_out.shape[0]
    blocks = own_blocks(hid)
    me = place[0]

    shape3 = (owner_count, META, LANES)
    lane3 = lax.broadcasted_iota(jnp.int32, shape3, 2)
    sub3 = lax.broadcasted_iota(jnp.int32, shape3, 1)
    owner3 = lax.broadcasted_iota(jnp.int32, shape3, 0)
    subf = sub3.astype(f32)
    matches, codes = [], []
    shared = [jnp.zeros((1, LANES), f32) for _ in range(blocks)]
    for owner in range(owner_count):
        first = owner * back_stride + rows
        tile = back[first : first + BACK_ROWS, :].astype(f32)
        matches.append(jnp.broadcast_to(tile[0:1] + tile[1:2], (1, META, LANES)))
        codes.append(jnp.broadcast_to(tile[2:3], (1, META, LANES)))
        shared[owner % blocks] += tile[3:4]
    match = jnp.concatenate(matches, axis=0)
    code = jnp.concatenate(codes, axis=0)
    shared = [
        part * (1.0 / ((owner_count - k + blocks - 1) // blocks)) for k, part in enumerate(shared)
    ]
    shared = jnp.concatenate(shared, axis=1).astype(bf16).astype(f32)
    base_row[...] = jnp.broadcast_to(shared, base_row.shape)
    is_pos = (code >= 8.0) & (code < 16.0)
    query_of = jnp.where(is_pos, code - 8.0, code)
    here = query_of == subf
    peak = jnp.max(jnp.where(here, match, FLOOR), axis=0)
    peak = jnp.maximum(peak, pltpu.roll(peak, HALF, 1))
    raised = jnp.where(here, jnp.exp(match - peak[None]), 0.0)
    total = jnp.sum(raised, axis=0)
    total = total + pltpu.roll(total, HALF, 1)
    total = jnp.where(total > 0.0, total, 1.0)
    chosen = jnp.sum(jnp.where(here & is_pos, match, 0.0), axis=0)
    chosen = chosen + pltpu.roll(chosen, HALF, 1)
    log_total = peak + jnp.log(total)
    lane2 = lax.broadcasted_iota(jnp.int32, (META, LANES), 1)
    sub2 = lax.broadcasted_iota(jnp.int32, (META, LANES), 0).astype(f32)
    picked = jnp.sum(jnp.where(lane2 == me, log_total - chosen, 0.0), axis=1, keepdims=True)
    loss[...] = jnp.broadcast_to(picked, (META, LANES))

    factor = loss_factor * SCORE_SCALE / (math.sqrt(vec_width) * query_len)

    own_match = own[0:1, :]
    own_code = own[1:2, :]
    own_pos = (own_code >= 8.0) & (own_code < 16.0)
    own_query = jnp.where(own_pos, own_code - 8.0, own_code)
    own_grad = jnp.exp(jnp.minimum(own_match - log_total, 0.0)) - jnp.where(own_pos, 1.0, 0.0)
    own_grad = factor * jnp.sum(jnp.where(own_query == sub2, own_grad, 0.0), axis=0, keepdims=True)
    both = jnp.broadcast_to(own_grad, (META, LANES))
    slot3 = HALF * (sub3 % CAP)
    own_scale[...] = jnp.broadcast_to(
        jnp.sum(
            jnp.where(lane3 == owner3 + slot3, jnp.broadcast_to(both[None], shape3), 0.0),
            axis=2,
            keepdims=True,
        ),
        shape3,
    )

    ask_grad = raised * (1.0 / total)[None] - jnp.where(here & is_pos, 1.0, 0.0)
    ask_grad = factor * jnp.sum(ask_grad, axis=1, keepdims=True)
    both = jnp.where(sub3 < CAP, jnp.broadcast_to(ask_grad, shape3), query_of)
    ask_scale[...] = jnp.broadcast_to(
        jnp.sum(jnp.where(lane3 == me + slot3, both, 0.0), axis=2, keepdims=True), shape3
    )

    size = owner_count * rows
    frame = (lax.broadcasted_iota(jnp.int32, (size, LANES), 0) % query_len).astype(f32)
    lane = lax.broadcasted_iota(jnp.int32, (size, LANES), 1).astype(f32)
    one = jnp.ones((size, LANES), bf16)
    zero = jnp.zeros((size, LANES), bf16)

    scaled = (queries[...].astype(f32) * spread(own_scale[...], 0, query_len)).astype(bf16)
    line_acc[...] = dot(scaled, wide[...], 0, 0)

    labels = ask_scale[...]
    target = spread(labels, CAP, query_len) * float(query_len) + frame
    pulled = jnp.concatenate(
        [back[b * back_stride : b * back_stride + rows, :] for b in range(owner_count)], axis=0
    )
    pulled = (pulled.astype(f32) * spread(labels, 0, query_len)).astype(bf16)
    hits = jnp.concatenate(
        [
            jnp.where(target == lane + float(k), one, zero)
            for k in range(0, query_acc.shape[1], LANES)
        ],
        axis=1,
    )
    query_acc[...] = dot(pulled, hits, 0, 0)

    grad_in = None
    grad_out = None
    grad_bias = None
    vec_sum = None
    spans = ((line_acc, xl, 0, line_total), (query_acc, xq, line_total, query_frames))
    for acc, x, first, span in spans:
        g_hi, g_lo = split2(acc[:, 0:span])
        grad_hidden = dot(w_out[...], g_hi) + dot(w_out[...], g_lo)
        grad_pre = grad_hidden * slope_t[:, first : first + span]
        p_hi = grad_pre.astype(bf16)
        hidden = hidden_all[first : first + span, :]
        ones = jnp.ones((META, span), bf16)
        part_in = dot(p_hi, x[...])
        part_out = dot(g_hi, hidden) + dot(g_lo, hidden)
        part_out -= jnp.sum(g_hi.astype(f32) + g_lo.astype(f32), axis=1, keepdims=True) * shared
        part_sum = dot(ones, g_hi, 1, 1) + dot(ones, g_lo, 1, 1)
        vec_sum = part_sum if vec_sum is None else vec_sum + part_sum
        part_bias = sum(grad_pre[:, k : k + LANES] for k in range(0, span, LANES))
        grad_in = part_in if grad_in is None else grad_in + part_in
        grad_out = part_out if grad_out is None else grad_out + part_out
        grad_bias = part_bias if grad_bias is None else grad_bias + part_bias
    grad_bias = jnp.sum(grad_bias.T, axis=0, keepdims=True)
    base = 0
    for k in range(0, x.shape[1], LANES):
        grads[base : base + hid, :] = grad_in[:, k : k + LANES]
        base += hid
    for k in range(0, hid, LANES):
        grads[base : base + vec_width, :] = grad_out[:, k : k + LANES]
        base += vec_width
    rest = grads.shape[0] - base
    singles = [grad_bias[0:1, k : k + LANES] for k in range(0, hid, LANES)] + [vec_sum[0:1, :]]
    grads[base:, :] = tail_tile(singles, rest)
    half = keep.shape[0]
    core = place[1]
    keep[...] = grads[pl.ds(pl.multiple_of(core * half, half), half), :]
    give[...] = grads[pl.ds(pl.multiple_of((1 - core) * half, half), half), :].astype(bf16)


def tail_tile(values, size):
    sub = lax.broadcasted_iota(jnp.int32, (size, LANES), 0)
    tile = jnp.zeros((size, LANES), f32)
    for i, value in enumerate(values):
        for p, part in enumerate(split3(value)):
            tile = jnp.where(sub == 3 * i + p, part, tile)
    return tile


def tail_values(tile, count):
    return [
        tile[3 * i : 3 * i + 1] + tile[3 * i + 1 : 3 * i + 2] + tile[3 * i + 2 : 3 * i + 3]
        for i in range(count)
    ]


def sum_core_kernel(place, keep, got, send, *, tail_rows, tail_count):
    total = keep[...] + got[...].astype(f32)
    send[...] = total.astype(bf16)

    @pl.when(place[1] == 1)
    def _():
        first = total.shape[0] - tail_rows
        values = tail_values(total[first:, :], tail_count)
        send[first:, :] = tail_tile(values, tail_rows).astype(bf16)


def sum_kernel(got, send):
    part = jnp.sum(got[...].astype(f32), axis=0).astype(bf16)
    for k in range(send.shape[0]):
        send[k] = part


def unpack_kernel(place, mine, other, base_row, grad_in, grad_bias, grad_out, got):
    feat, hid = grad_in.shape
    vec_width = grad_out.shape[1]
    half = mine.shape[0]
    core = place[1]
    got[pl.ds(pl.multiple_of(core * half, half), half), :] = mine[...]
    got[pl.ds(pl.multiple_of((1 - core) * half, half), half), :] = other[...]
    base = 0
    for k in range(0, feat, LANES):
        grad_in[k : k + LANES, :] = got[base : base + hid, :].astype(f32).T
        base += hid
    start = base + vec_width * (hid // LANES)
    values = tail_values(got[start : start + 16, :].astype(f32), hid // LANES + 1)
    vec_sum = values[-1]
    sub = lax.broadcasted_iota(jnp.int32, (META, LANES), 0)
    zero = jnp.zeros((META, LANES), f32)
    vec_rows = zero
    for p, part in enumerate(split3(vec_sum)):
        vec_rows = jnp.where(sub == p, part, vec_rows)
    vec_rows = vec_rows.astype(bf16)
    for i, k in enumerate(range(0, hid, LANES)):
        base_rows = base_row[:, k : k + LANES].astype(bf16)
        outer = dot(base_rows, vec_rows, 0, 0)
        grad_out[k : k + LANES, :] = got[base : base + vec_width, :].astype(f32).T + outer
        grad_bias[k : k + LANES] = values[i].reshape(LANES)
        base += vec_width


def exchange(x, axis):
    return lax.all_to_all(x, axis, split_axis=0, concat_axis=0, tiled=True)


def exchange_rows(x, axis, peers, tile):
    blocks = x.reshape(peers, x.shape[0] // (peers * tile), tile, x.shape[1])
    return exchange(blocks, axis).reshape(x.shape)


def shape_of(shape, dtype):
    return jax.ShapeDtypeStruct(shape, dtype)


def local(query_frames, line_frames, frame_count, line_home, mined, positive, w_in, bias_in, w_out):
    query_count, query_len, feat = query_frames.shape
    line_count, line_len, _ = line_frames.shape
    hid, vec_width = w_out.shape
    chip_count = lax.axis_size("chip")
    owner_count = chip_count * lax.axis_size("core")
    dp_count = lax.axis_size("dp")
    loss_factor = LOSS_SCALE / (query_count * owner_count * dp_count)
    frames_q = query_count * query_len
    frames_l = line_count * line_len
    frames = frames_q + frames_l
    rows = CAP * query_len
    xq = query_frames.reshape(frames_q, feat)
    xl = line_frames.reshape(frames_l, feat)
    place = jnp.stack([lax.axis_index(ARCHIVE), lax.axis_index("core")]).astype(jnp.int32)
    ask_wire = shape_of((owner_count * (rows + ASK_ROWS), vec_width), bf16)
    back_wire = shape_of((owner_count * (rows + BACK_ROWS), vec_width), bf16)
    head_flops = 2 * hid * (feat + vec_width)

    (asked,) = call(
        ask_kernel,
        [ask_wire],
        [mined, line_home, positive, xq, w_in, bias_in, w_out],
        0,
        [
            pltpu.SMEM(mined.shape, jnp.int32),
            pltpu.SMEM(line_home.shape, jnp.int32),
            pltpu.SMEM(positive.shape, jnp.int32),
            pltpu.VMEM(xq.shape, bf16),
            pltpu.VMEM(w_in.shape, bf16),
            pltpu.VMEM(bias_in.shape, f32),
            pltpu.VMEM(w_out.shape, bf16),
            pltpu.VMEM((frames_q, vec_width), bf16),
            pltpu.VMEM((owner_count, rows, vec_width), bf16),
            pltpu.SMEM((CAP, owner_count), jnp.int32),
            pltpu.SMEM((CAP, owner_count), jnp.int32),
            pltpu.SMEM((owner_count,), jnp.int32),
            pltpu.SMEM(mined.shape, jnp.int32),
            pltpu.SMEM(mined.shape, jnp.int32),
            pltpu.SemaphoreType.DMA((7,)),
        ],
        flops=frames_q * head_flops,
        where=pltpu.HBM,
        limit=63 << 20,
    )
    got = exchange_rows(asked, ARCHIVE, owner_count, ASK_ROWS)
    line_vec, line_vec_t, hidden_all, slope_t, mean = call(
        head_kernel,
        [
            shape_of((line_count, line_len, vec_width), bf16),
            shape_of((line_count, vec_width, line_len), bf16),
            shape_of((frames, hid), bf16),
            shape_of((hid, frames), f32),
            shape_of((META, hid), f32),
        ],
        [xl, xq, w_in, bias_in, w_out],
        0,
        flops=frames * head_flops,
        transcendentals=frames * hid,
    )
    match_flops = 2 * owner_count * rows * frames_l * vec_width
    answer, weights, own = call(
        match_kernel,
        [
            back_wire,
            shape_of((owner_count, rows, line_len), bf16),
            shape_of((META, LANES), f32),
        ],
        [place, frame_count, got, line_vec, line_vec_t, mean],
        2,
        [
            pltpu.VMEM((line_count, LANES), f32),
            pltpu.VMEM((META, LANES), jnp.int32),
            pltpu.SMEM((META, LANES), jnp.int32),
            pltpu.VMEM((LANES, LANES), f32),
            pltpu.SemaphoreType.DMA(()),
        ],
        flops=2 * match_flops,
    )
    back = exchange_rows(answer, ARCHIVE, owner_count, BACK_ROWS)
    slot_rows = owner_count * rows
    wide, queries = call(
        widen_kernel,
        [shape_of((slot_rows, frames_l), bf16), shape_of((slot_rows, vec_width), bf16)],
        [weights, own, got],
        0,
        [pltpu.VMEM((LANES, LANES), f32)],
        flops=slot_rows * frames_l,
    )
    unit = 16 * owner_count
    flat_rows = unit * -(-(LANES + (feat + vec_width) * hid // LANES) // unit)
    half = flat_rows // 2

    def grads_body(*refs):
        grad_kernel(*refs, loss_factor=loss_factor)

    loss, keep, give, base_row = call(
        grads_body,
        [
            shape_of((META, LANES), f32),
            shape_of((half, LANES), f32),
            shape_of((half, LANES), bf16),
            shape_of((META, hid), f32),
        ],
        [place, back, queries, wide, own, xl, xq, hidden_all, slope_t, w_out],
        1,
        [
            pltpu.VMEM((flat_rows, LANES), f32),
            pltpu.VMEM((owner_count, META, LANES), f32),
            pltpu.VMEM((owner_count, META, LANES), f32),
            pltpu.VMEM((vec_width, frames_l), f32),
            pltpu.VMEM((vec_width, frames_q), f32),
        ],
        flops=match_flops + 4 * frames * head_flops,
    )
    swap = [(0, 1), (1, 0)]
    share = half // chip_count
    taken = lax.ppermute(give, "core", swap)
    tail_rows = flat_rows - (feat + vec_width) * hid // LANES

    def sum_core_body(*refs):
        sum_core_kernel(*refs, tail_rows=tail_rows, tail_count=hid // LANES + 1)

    (part,) = call(sum_core_body, [shape_of((half, LANES), bf16)], [place, keep, taken], 1)
    parts = exchange(part.reshape(chip_count, share, LANES), "chip")
    (part,) = call(sum_kernel, [shape_of((dp_count, share, LANES), bf16)], [parts], 0)
    parts = exchange(part, "dp")
    (part,) = call(sum_kernel, [shape_of((chip_count, share, LANES), bf16)], [parts], 0)
    mine = exchange(part, "chip").reshape(half, LANES)
    other = lax.ppermute(mine, "core", swap)
    grad_in, grad_bias, grad_out = call(
        unpack_kernel,
        [shape_of((feat, hid), f32), shape_of((hid,), f32), shape_of((hid, vec_width), f32)],
        [place, mine, other, base_row],
        1,
        [pltpu.VMEM((flat_rows, LANES), bf16)],
    )
    return (loss[:query_count, 0], grad_in, grad_bias, grad_out)


def solution(mesh):
    devices = mesh.devices
    archive, dp = devices.shape
    mesh = Mesh(devices.reshape(archive // 2, 2, dp), ("chip", "core", "dp"))
    everywhere = ARCHIVE + ("dp",)
    placed = (
        P(everywhere, None, None),
        P(ARCHIVE, None, None),
        P(),
        P(),
        P(everywhere, None),
        P(everywhere),
        P(),
        P(),
        P(),
    )
    return jax.shard_map(
        local,
        mesh=mesh,
        in_specs=placed,
        out_specs=(P(everywhere), P(), P(), P()),
        check_vma=False,
    )
```

```python
import math

import jax
import jax.numpy as jnp
from jax import lax
from jax.experimental import pallas as pl
from jax.experimental.pallas import tpu as pltpu
from jax.sharding import Mesh, PartitionSpec as P

LOSS_SCALE = 4096.0
SCORE_SCALE = 4.0
LANES = 128
CAP = 2
HALF = LANES // CAP
META = 8
ASK_ROWS = 2
BACK_ROWS = 4
UNUSED = 100.0
FLOOR = -1e30
GELU_A = math.sqrt(2.0 / math.pi)
GELU_B = 0.044715
ARCHIVE = ("chip", "core")

f32 = jnp.float32
bf16 = jnp.bfloat16


def dot(a, b, ca=1, cb=0):
    return lax.dot_general(a, b, (((ca,), (cb,)), ((), ())), preferred_element_type=f32)


def split2(x):
    hi = x.astype(bf16)
    return hi, (x - hi.astype(f32)).astype(bf16)


def split3(x):
    hi = x.astype(bf16).astype(f32)
    mid = (x - hi).astype(bf16).astype(f32)
    return hi, mid, (x - hi - mid).astype(bf16).astype(f32)


def call(body, outs, args, smem_count, scratch=(), flops=0, transcendentals=0, where=pltpu.VMEM, limit=40 << 20):
    nbytes = sum(a.size * a.dtype.itemsize for a in list(args) + list(outs))
    vmem = pl.BlockSpec(memory_space=pltpu.VMEM)
    smem = pl.BlockSpec(memory_space=pltpu.SMEM)
    rest = pl.BlockSpec(memory_space=where)
    return pl.pallas_call(
        body,
        out_shape=tuple(outs),
        in_specs=[smem] * smem_count + [rest] * (len(args) - smem_count),
        out_specs=tuple(vmem for _ in outs),
        scratch_shapes=list(scratch),
        compiler_params=pltpu.CompilerParams(vmem_limit_bytes=limit),
        cost_estimate=pl.CostEstimate(
            flops=flops, bytes_accessed=nbytes, transcendentals=transcendentals
        ),
    )(*args)


def gelu_parts(pre):
    t = jnp.tanh(GELU_A * (pre + GELU_B * pre * pre * pre))
    return t, (0.5 * pre * (1.0 + t)).astype(bf16)


def ask_kernel(
    mined_hbm, home_hbm, positive_hbm, x_hbm, w_in_hbm, bias_hbm, w_out_hbm, send, mined, home, positive, x, w_in, bias, w_out, vec, stage, rid, code, count, goal_owner, goal_rank, sems
):
    query_count, mined_count = mined.shape
    owner_count, rows, _ = stage.shape
    query_len = x.shape[0] // query_count
    line_count = home.shape[0] // owner_count
    stride = rows + ASK_ROWS
    pairs = (
        (mined_hbm, mined),
        (home_hbm, home),
        (positive_hbm, positive),
        (x_hbm, x),
        (w_in_hbm, w_in),
        (bias_hbm, bias),
        (w_out_hbm, w_out),
    )
    copies = [pltpu.make_async_copy(a, b, sems.at[i]) for i, (a, b) in enumerate(pairs)]
    for copy in copies:
        copy.start()

    def clear(owner, carry):
        count[owner] = 0
        for c in range(CAP):
            rid[c, owner] = int(UNUSED)
            code[c, owner] = int(UNUSED)
        return carry

    lax.fori_loop(0, owner_count, clear, 0, unroll=8)
    stage[...] = jnp.zeros(stage.shape, bf16)
    for copy in copies[:3]:
        copy.wait()

    def assign(query, carry):
        for j in range(mined_count):
            row = home[mined[query, j]]
            owner = row // line_count
            rank = count[owner]
            count[owner] = rank + 1
            rid[rank, owner] = row - owner * line_count
            code[rank, owner] = query + jnp.where(positive[query] == j, 8, 0)
            goal_owner[query, j] = owner
            goal_rank[query, j] = rank * query_len
        return carry

    lax.fori_loop(0, query_count, assign, 0, unroll=2)
    sub = lax.broadcasted_iota(jnp.int32, (ASK_ROWS, LANES), 0)
    low = lax.broadcasted_iota(jnp.int32, (ASK_ROWS, LANES), 1) < HALF
    for owner in range(owner_count):
        tile = jnp.where(
            sub == 0,
            jnp.where(low, rid[0, owner], rid[1, owner]),
            jnp.where(low, code[0, owner], code[1, owner]),
        )
        first = owner * stride + rows
        send[first : first + ASK_ROWS, :] = tile.astype(f32).astype(bf16)
    for copy in copies[3:]:
        copy.wait()
    _, hidden = gelu_parts(dot(x[...], w_in[...]) + bias[...].reshape(1, -1))
    vec[...] = dot(hidden, w_out[...]).astype(bf16)

    def place(query, carry):
        block = vec[pl.ds(pl.multiple_of(query * query_len, query_len), query_len), :]
        for j in range(mined_count):
            first = pl.multiple_of(goal_rank[query, j], query_len)
            stage[goal_owner[query, j], pl.ds(first, query_len), :] = block
        return carry

    lax.fori_loop(0, query_count, place, 0, unroll=4)
    for owner in range(owner_count):
        send[owner * stride : owner * stride + rows, :] = stage[owner]


def head_kernel(xl, xq, w_in, bias, w_out, line_vec, line_vec_t, hidden_all, slope_t, mean):
    step = 256
    line_frames = xl.shape[0]
    total = jnp.zeros((1, hidden_all.shape[1]), f32)
    for first in range(0, line_frames + xq.shape[0], step):
        if first < line_frames:
            x = xl[first : first + step, :]
        else:
            x = xq[first - line_frames : first - line_frames + step, :]
        size = x.shape[0]
        pre = dot(x, w_in[...]) + bias[...].reshape(1, -1)
        t, hidden = gelu_parts(pre)
        slope = 0.5 * (1.0 + t) + 0.5 * pre * (1.0 - t * t) * GELU_A * (
            1.0 + 3.0 * GELU_B * pre * pre
        )
        hidden_all[first : first + size, :] = hidden
        slope_t[:, first : first + size] = slope.T
        if first < line_frames:
            vec = dot(hidden, w_out[...])
            for k in range(0, size, LANES):
                line = (first + k) // LANES
                line_vec[line] = vec[k : k + LANES].astype(bf16)
                line_vec_t[line] = vec[k : k + LANES].T.astype(bf16)
            total += jnp.sum(hidden.astype(f32), axis=0, keepdims=True)
    mean[...] = jnp.broadcast_to(total * (1.0 / line_frames), mean.shape)


def spread(meta, first, query_len):
    parts = []
    for b in range(meta.shape[0]):
        for c in range(CAP):
            parts.append(jnp.broadcast_to(meta[b, first + c : first + c + 1, :], (query_len, LANES)))
    return jnp.concatenate(parts, axis=0)


def match_kernel(
    place, counts, got, line_vec, line_vec_t, mean, send, weights, own, pads, label_rows, ids, sums, sem
):
    owner_count, rows, _ = weights.shape
    query_len = rows // CAP
    stride, out_stride = rows + ASK_ROWS, rows + BACK_ROWS
    line_count, _, vec_width = line_vec.shape
    scale = SCORE_SCALE / math.sqrt(vec_width)
    lane1 = lax.broadcasted_iota(jnp.int32, (1, LANES), 1)
    lane2 = lax.broadcasted_iota(jnp.int32, (ASK_ROWS, LANES), 1) % HALF
    labels = jnp.full((ASK_ROWS, LANES), UNUSED, f32)
    for b in range(owner_count):
        first = b * stride + rows
        labels = jnp.where(lane2 == b, got[first : first + ASK_ROWS, :].astype(f32), labels)
    rid_row, code_row = labels[0:1], labels[1:2]
    rid_row = jnp.where(rid_row < line_count, rid_row, 0.0)
    label_rows[...] = jnp.broadcast_to(rid_row, (META, LANES)).astype(jnp.int32)
    copy = pltpu.make_async_copy(label_rows, ids, sem)
    copy.start()
    for r in range(line_count):
        pads[r : r + 1, :] = jnp.where(lane1 < counts[place[0] * line_count + r], 0.0, FLOOR)
    sums[...] = jnp.zeros(sums.shape, f32)
    ones = jnp.ones((LANES, LANES), bf16)
    copy.wait()
    for b in range(owner_count):
        for c in range(CAP):
            slot = b + HALF * c
            r = ids[0, slot]
            first = b * stride + c * query_len
            logits = dot(got[first : first + query_len, :], line_vec_t[r]) * scale
            logits = logits + pads[pl.ds(r, 1), :]
            peak = jnp.max(logits, axis=1, keepdims=True)
            scaled = jnp.exp(logits - peak).astype(bf16)
            both = dot(scaled, jnp.concatenate([line_vec[r], ones], axis=1))
            totals = both[:, vec_width:]
            inverse = 1.0 / totals
            weights[b, c * query_len : (c + 1) * query_len, :] = (
                scaled.astype(f32) * inverse
            ).astype(bf16)
            first = b * out_stride + c * query_len
            send[first : first + query_len, :] = (both[:, :vec_width] * inverse).astype(bf16)
            log_total = peak + jnp.log(totals)
            sums[slot : slot + 1, :] = jnp.sum(log_total, axis=0, keepdims=True) * (1.0 / query_len)
    lane = lax.broadcasted_iota(jnp.int32, sums.shape, 1)
    row = lax.broadcasted_iota(jnp.int32, sums.shape, 0)
    match_row = jnp.sum(jnp.where(lane == row, sums[...], 0.0), axis=0, keepdims=True)
    high, low = (part.astype(f32) for part in split2(match_row))
    blocks = own_blocks(mean.shape[1])
    mean_row = mean[:, 0:LANES]
    for k in range(1, blocks):
        mean_row = jnp.where(place[0] % blocks == k, mean[:, k * LANES : (k + 1) * LANES], mean_row)
    sub = lax.broadcasted_iota(jnp.int32, (META, LANES), 0)
    own[...] = jnp.where(sub == 0, high + low, jnp.where(sub == 1, code_row, rid_row))
    sub = lax.broadcasted_iota(jnp.int32, (BACK_ROWS, LANES), 0)
    tile = jnp.where(
        sub == 0, high, jnp.where(sub == 1, low, jnp.where(sub == 2, code_row, mean_row[0:1]))
    ).astype(bf16)
    for b in range(owner_count):
        first = b * out_stride + rows
        send[first : first + BACK_ROWS, :] = tile


def own_blocks(hid):
    return hid // LANES


def grad_kernel(
    place, back, got, weights, own, xl, xq, hidden_all, slope_t, w_out, loss, keep, give, base_row, grads, own_scale, ask_scale, line_acc, query_acc, *, loss_factor
):
    owner_count, rows, _ = weights.shape
    stride, back_stride = rows + ASK_ROWS, rows + BACK_ROWS
    query_len = rows // CAP
    line_total = xl.shape[0]
    line_count = line_total // LANES
    query_frames = xq.shape[0]
    vec_width = w_out.shape[1]
    hid = w_out.shape[0]
    blocks = own_blocks(hid)
    me = place[0]

    shape3 = (owner_count, META, LANES)
    lane3 = lax.broadcasted_iota(jnp.int32, shape3, 2)
    sub3 = lax.broadcasted_iota(jnp.int32, shape3, 1)
    owner3 = lax.broadcasted_iota(jnp.int32, shape3, 0)
    subf = sub3.astype(f32)
    matches, codes = [], []
    shared = [jnp.zeros((1, LANES), f32) for _ in range(blocks)]
    for owner in range(owner_count):
        first = owner * back_stride + rows
        tile = back[first : first + BACK_ROWS, :].astype(f32)
        matches.append(jnp.broadcast_to(tile[0:1] + tile[1:2], (1, META, LANES)))
        codes.append(jnp.broadcast_to(tile[2:3], (1, META, LANES)))
        shared[owner % blocks] += tile[3:4]
    match = jnp.concatenate(matches, axis=0)
    code = jnp.concatenate(codes, axis=0)
    shared = [
        part * (1.0 / ((owner_count - k + blocks - 1) // blocks)) for k, part in enumerate(shared)
    ]
    shared = jnp.concatenate(shared, axis=1).astype(bf16).astype(f32)
    base_row[...] = jnp.broadcast_to(shared, base_row.shape)
    is_pos = (code >= 8.0) & (code < 16.0)
    query_of = jnp.where(is_pos, code - 8.0, code)
    here = query_of == subf
    peak = jnp.max(jnp.where(here, match, FLOOR), axis=0)
    peak = jnp.maximum(peak, pltpu.roll(peak, HALF, 1))
    raised = jnp.where(here, jnp.exp(match - peak[None]), 0.0)
    total = jnp.sum(raised, axis=0)
    total = total + pltpu.roll(total, HALF, 1)
    total = jnp.where(total > 0.0, total, 1.0)
    chosen = jnp.sum(jnp.where(here & is_pos, match, 0.0), axis=0)
    chosen = chosen + pltpu.roll(chosen, HALF, 1)
    log_total = peak + jnp.log(total)
    lane2 = lax.broadcasted_iota(jnp.int32, (META, LANES), 1)
    sub2 = lax.broadcasted_iota(jnp.int32, (META, LANES), 0).astype(f32)
    picked = jnp.sum(jnp.where(lane2 == me, log_total - chosen, 0.0), axis=1, keepdims=True)
    loss[...] = jnp.broadcast_to(picked, (META, LANES))

    factor = loss_factor * SCORE_SCALE / (math.sqrt(vec_width) * query_len)

    own_match = own[0:1, :]
    own_code = own[1:2, :]
    own_pos = (own_code >= 8.0) & (own_code < 16.0)
    own_query = jnp.where(own_pos, own_code - 8.0, own_code)
    own_grad = jnp.exp(jnp.minimum(own_match - log_total, 0.0)) - jnp.where(own_pos, 1.0, 0.0)
    own_grad = factor * jnp.sum(jnp.where(own_query == sub2, own_grad, 0.0), axis=0, keepdims=True)
    both = jnp.where(lane2 >= 0, jnp.where(sub2 < CAP, own_grad, own[2:3, :]), 0.0)
    slot3 = HALF * (sub3 % CAP)
    own_scale[...] = jnp.broadcast_to(
        jnp.sum(
            jnp.where(lane3 == owner3 + slot3, jnp.broadcast_to(both[None], shape3), 0.0),
            axis=2,
            keepdims=True,
        ),
        shape3,
    )

    ask_grad = raised * (1.0 / total)[None] - jnp.where(here & is_pos, 1.0, 0.0)
    ask_grad = factor * jnp.sum(ask_grad, axis=1, keepdims=True)
    both = jnp.where(sub3 < CAP, jnp.broadcast_to(ask_grad, shape3), query_of)
    ask_scale[...] = jnp.broadcast_to(
        jnp.sum(jnp.where(lane3 == me + slot3, both, 0.0), axis=2, keepdims=True), shape3
    )

    size = owner_count * rows
    frame = (lax.broadcasted_iota(jnp.int32, (size, LANES), 0) % query_len).astype(f32)
    lane = lax.broadcasted_iota(jnp.int32, (size, LANES), 1).astype(f32)
    zero = jnp.zeros((size, LANES), bf16)
    one = jnp.ones((size, LANES), bf16)

    labels = own_scale[...]
    queries = jnp.concatenate(
        [got[b * stride : b * stride + rows, :] for b in range(owner_count)], axis=0
    )
    rid = spread(labels, CAP, query_len).astype(bf16)
    weight = weights[...].reshape(size, LANES).astype(f32)
    score = (weight * spread(labels, 0, query_len)).astype(bf16)
    wide = jnp.concatenate([jnp.where(rid == r, score, zero) for r in range(line_count)], axis=1)
    line_acc[...] = dot(queries, wide, 0, 0)

    labels = ask_scale[...]
    target = spread(labels, CAP, query_len) * float(query_len) + frame
    pulled = jnp.concatenate(
        [back[b * back_stride : b * back_stride + rows, :] for b in range(owner_count)], axis=0
    )
    pulled = (pulled.astype(f32) * spread(labels, 0, query_len)).astype(bf16)
    wide = jnp.concatenate(
        [
            jnp.where(target == lane + float(k), one, zero)
            for k in range(0, query_acc.shape[1], LANES)
        ],
        axis=1,
    )
    query_acc[...] = dot(pulled, wide, 0, 0)

    grad_in = None
    grad_out = None
    grad_bias = None
    vec_sum = None
    spans = ((line_acc, xl, 0, line_total), (query_acc, xq, line_total, query_frames))
    for acc, x, first, span in spans:
        g_hi, g_lo = split2(acc[:, 0:span])
        grad_hidden = dot(w_out[...], g_hi) + dot(w_out[...], g_lo)
        grad_pre = grad_hidden * slope_t[:, first : first + span]
        p_hi = grad_pre.astype(bf16)
        hidden = hidden_all[first : first + span, :]
        ones = jnp.ones((META, span), bf16)
        part_in = dot(p_hi, x[...])
        part_out = dot(g_hi, hidden) + dot(g_lo, hidden)
        part_out -= jnp.sum(g_hi.astype(f32) + g_lo.astype(f32), axis=1, keepdims=True) * shared
        part_sum = dot(ones, g_hi, 1, 1) + dot(ones, g_lo, 1, 1)
        vec_sum = part_sum if vec_sum is None else vec_sum + part_sum
        part_bias = sum(grad_pre[:, k : k + LANES] for k in range(0, span, LANES))
        grad_in = part_in if grad_in is None else grad_in + part_in
        grad_out = part_out if grad_out is None else grad_out + part_out
        grad_bias = part_bias if grad_bias is None else grad_bias + part_bias
    grad_bias = jnp.sum(grad_bias.T, axis=0, keepdims=True)
    base = 0
    for k in range(0, x.shape[1], LANES):
        grads[base : base + hid, :] = grad_in[:, k : k + LANES]
        base += hid
    for k in range(0, hid, LANES):
        grads[base : base + vec_width, :] = grad_out[:, k : k + LANES]
        base += vec_width
    rest = grads.shape[0] - base
    singles = [grad_bias[0:1, k : k + LANES] for k in range(0, hid, LANES)] + [vec_sum[0:1, :]]
    grads[base:, :] = tail_tile(singles, rest)
    half = keep.shape[0]
    core = place[1]
    keep[...] = grads[pl.ds(pl.multiple_of(core * half, half), half), :]
    give[...] = grads[pl.ds(pl.multiple_of((1 - core) * half, half), half), :].astype(bf16)


def tail_tile(values, size):
    sub = lax.broadcasted_iota(jnp.int32, (size, LANES), 0)
    tile = jnp.zeros((size, LANES), f32)
    for i, value in enumerate(values):
        for p, part in enumerate(split3(value)):
            tile = jnp.where(sub == 3 * i + p, part, tile)
    return tile


def tail_values(tile, count):
    return [
        tile[3 * i : 3 * i + 1] + tile[3 * i + 1 : 3 * i + 2] + tile[3 * i + 2 : 3 * i + 3]
        for i in range(count)
    ]


def sum_core_kernel(place, keep, got, send, *, tail_rows, tail_count):
    total = keep[...] + got[...].astype(f32)
    send[...] = total.astype(bf16)

    @pl.when(place[1] == 1)
    def _():
        first = total.shape[0] - tail_rows
        values = tail_values(total[first:, :], tail_count)
        send[first:, :] = tail_tile(values, tail_rows).astype(bf16)


def sum_kernel(got, send):
    part = jnp.sum(got[...].astype(f32), axis=0).astype(bf16)
    for k in range(send.shape[0]):
        send[k] = part


def unpack_kernel(place, mine, other, base_row, grad_in, grad_bias, grad_out, got):
    feat, hid = grad_in.shape
    vec_width = grad_out.shape[1]
    half = mine.shape[0]
    core = place[1]
    got[pl.ds(pl.multiple_of(core * half, half), half), :] = mine[...]
    got[pl.ds(pl.multiple_of((1 - core) * half, half), half), :] = other[...]
    base = 0
    for k in range(0, feat, LANES):
        grad_in[k : k + LANES, :] = got[base : base + hid, :].astype(f32).T
        base += hid
    start = base + vec_width * (hid // LANES)
    values = tail_values(got[start : start + 16, :].astype(f32), hid // LANES + 1)
    vec_sum = values[-1]
    sub = lax.broadcasted_iota(jnp.int32, (META, LANES), 0)
    zero = jnp.zeros((META, LANES), f32)
    vec_rows = zero
    for p, part in enumerate(split3(vec_sum)):
        vec_rows = jnp.where(sub == p, part, vec_rows)
    vec_rows = vec_rows.astype(bf16)
    for i, k in enumerate(range(0, hid, LANES)):
        base_rows = base_row[:, k : k + LANES].astype(bf16)
        outer = dot(base_rows, vec_rows, 0, 0)
        grad_out[k : k + LANES, :] = got[base : base + vec_width, :].astype(f32).T + outer
        grad_bias[k : k + LANES] = values[i].reshape(LANES)
        base += vec_width


def exchange(x, axis):
    return lax.all_to_all(x, axis, split_axis=0, concat_axis=0, tiled=True)


def exchange_rows(x, axis, peers, tile):
    blocks = x.reshape(peers, x.shape[0] // (peers * tile), tile, x.shape[1])
    return exchange(blocks, axis).reshape(x.shape)


def shape_of(shape, dtype):
    return jax.ShapeDtypeStruct(shape, dtype)


def local(query_frames, line_frames, frame_count, line_home, mined, positive, w_in, bias_in, w_out):
    query_count, query_len, feat = query_frames.shape
    line_count, line_len, _ = line_frames.shape
    hid, vec_width = w_out.shape
    chip_count = lax.axis_size("chip")
    owner_count = chip_count * lax.axis_size("core")
    dp_count = lax.axis_size("dp")
    loss_factor = LOSS_SCALE / (query_count * owner_count * dp_count)
    frames_q = query_count * query_len
    frames_l = line_count * line_len
    frames = frames_q + frames_l
    rows = CAP * query_len
    xq = query_frames.reshape(frames_q, feat)
    xl = line_frames.reshape(frames_l, feat)
    place = jnp.stack([lax.axis_index(ARCHIVE), lax.axis_index("core")]).astype(jnp.int32)
    ask_wire = shape_of((owner_count * (rows + ASK_ROWS), vec_width), bf16)
    back_wire = shape_of((owner_count * (rows + BACK_ROWS), vec_width), bf16)
    head_flops = 2 * hid * (feat + vec_width)

    (asked,) = call(
        ask_kernel,
        [ask_wire],
        [mined, line_home, positive, xq, w_in, bias_in, w_out],
        0,
        [
            pltpu.SMEM(mined.shape, jnp.int32),
            pltpu.SMEM(line_home.shape, jnp.int32),
            pltpu.SMEM(positive.shape, jnp.int32),
            pltpu.VMEM(xq.shape, bf16),
            pltpu.VMEM(w_in.shape, bf16),
            pltpu.VMEM(bias_in.shape, f32),
            pltpu.VMEM(w_out.shape, bf16),
            pltpu.VMEM((frames_q, vec_width), bf16),
            pltpu.VMEM((owner_count, rows, vec_width), bf16),
            pltpu.SMEM((CAP, owner_count), jnp.int32),
            pltpu.SMEM((CAP, owner_count), jnp.int32),
            pltpu.SMEM((owner_count,), jnp.int32),
            pltpu.SMEM(mined.shape, jnp.int32),
            pltpu.SMEM(mined.shape, jnp.int32),
            pltpu.SemaphoreType.DMA((7,)),
        ],
        flops=frames_q * head_flops,
        where=pltpu.HBM,
        limit=63 << 20,
    )
    got = exchange_rows(asked, ARCHIVE, owner_count, ASK_ROWS)
    line_vec, line_vec_t, hidden_all, slope_t, mean = call(
        head_kernel,
        [
            shape_of((line_count, line_len, vec_width), bf16),
            shape_of((line_count, vec_width, line_len), bf16),
            shape_of((frames, hid), bf16),
            shape_of((hid, frames), f32),
            shape_of((META, hid), f32),
        ],
        [xl, xq, w_in, bias_in, w_out],
        0,
        flops=frames * head_flops,
        transcendentals=frames * hid,
    )
    match_flops = 2 * owner_count * rows * frames_l * vec_width
    answer, weights, own = call(
        match_kernel,
        [
            back_wire,
            shape_of((owner_count, rows, line_len), bf16),
            shape_of((META, LANES), f32),
        ],
        [place, frame_count, got, line_vec, line_vec_t, mean],
        2,
        [
            pltpu.VMEM((line_count, LANES), f32),
            pltpu.VMEM((META, LANES), jnp.int32),
            pltpu.SMEM((META, LANES), jnp.int32),
            pltpu.VMEM((LANES, LANES), f32),
            pltpu.SemaphoreType.DMA(()),
        ],
        flops=2 * match_flops,
    )
    back = exchange_rows(answer, ARCHIVE, owner_count, BACK_ROWS)
    unit = 16 * owner_count
    flat_rows = unit * -(-(LANES + (feat + vec_width) * hid // LANES) // unit)
    half = flat_rows // 2

    def grads_body(*refs):
        grad_kernel(*refs, loss_factor=loss_factor)

    loss, keep, give, base_row = call(
        grads_body,
        [
            shape_of((META, LANES), f32),
            shape_of((half, LANES), f32),
            shape_of((half, LANES), bf16),
            shape_of((META, hid), f32),
        ],
        [place, back, got, weights, own, xl, xq, hidden_all, slope_t, w_out],
        1,
        [
            pltpu.VMEM((flat_rows, LANES), f32),
            pltpu.VMEM((owner_count, META, LANES), f32),
            pltpu.VMEM((owner_count, META, LANES), f32),
            pltpu.VMEM((vec_width, frames_l), f32),
            pltpu.VMEM((vec_width, frames_q), f32),
        ],
        flops=match_flops + 4 * frames * head_flops,
    )
    swap = [(0, 1), (1, 0)]
    share = half // chip_count
    taken = lax.ppermute(give, "core", swap)
    tail_rows = flat_rows - (feat + vec_width) * hid // LANES

    def sum_core_body(*refs):
        sum_core_kernel(*refs, tail_rows=tail_rows, tail_count=hid // LANES + 1)

    (part,) = call(sum_core_body, [shape_of((half, LANES), bf16)], [place, keep, taken], 1)
    parts = exchange(part.reshape(chip_count, share, LANES), "chip")
    (part,) = call(sum_kernel, [shape_of((dp_count, share, LANES), bf16)], [parts], 0)
    parts = exchange(part, "dp")
    (part,) = call(sum_kernel, [shape_of((chip_count, share, LANES), bf16)], [parts], 0)
    mine = exchange(part, "chip").reshape(half, LANES)
    other = lax.ppermute(mine, "core", swap)
    grad_in, grad_bias, grad_out = call(
        unpack_kernel,
        [shape_of((feat, hid), f32), shape_of((hid,), f32), shape_of((hid, vec_width), f32)],
        [place, mine, other, base_row],
        1,
        [pltpu.VMEM((flat_rows, LANES), bf16)],
    )
    return (loss[:query_count, 0], grad_in, grad_bias, grad_out)


def solution(mesh):
    devices = mesh.devices
    archive, dp = devices.shape
    mesh = Mesh(devices.reshape(archive // 2, 2, dp), ("chip", "core", "dp"))
    everywhere = ARCHIVE + ("dp",)
    placed = (
        P(everywhere, None, None),
        P(ARCHIVE, None, None),
        P(),
        P(),
        P(everywhere, None),
        P(everywhere),
        P(),
        P(),
        P(),
    )
    return jax.shard_map(
        local,
        mesh=mesh,
        in_specs=placed,
        out_specs=(P(everywhere), P(), P(), P()),
        check_vma=False,
    )
```

```python
import math

import jax
import jax.numpy as jnp
from jax import lax
from jax.experimental import pallas as pl
from jax.experimental.pallas import tpu as pltpu
from jax.sharding import Mesh, PartitionSpec as P

LOSS_SCALE = 4096.0
SCORE_SCALE = 4.0
LANES = 128
CAP = 2
HALF = LANES // CAP
META = 8
ASK_ROWS = 2
BACK_ROWS = 4
UNUSED = 100.0
FLOOR = -1e30
GELU_A = math.sqrt(2.0 / math.pi)
GELU_B = 0.044715
ARCHIVE = ("chip", "core")

f32 = jnp.float32
bf16 = jnp.bfloat16


def dot(a, b, ca=1, cb=0):
    return lax.dot_general(a, b, (((ca,), (cb,)), ((), ())), preferred_element_type=f32)


def split2(x):
    hi = x.astype(bf16)
    return hi, (x - hi.astype(f32)).astype(bf16)


def split3(x):
    hi = x.astype(bf16).astype(f32)
    mid = (x - hi).astype(bf16).astype(f32)
    return hi, mid, (x - hi - mid).astype(bf16).astype(f32)


def call(body, outs, args, smem_count, scratch=(), flops=0, transcendentals=0, where=pltpu.VMEM, limit=40 << 20):
    nbytes = sum(a.size * a.dtype.itemsize for a in list(args) + list(outs))
    vmem = pl.BlockSpec(memory_space=pltpu.VMEM)
    smem = pl.BlockSpec(memory_space=pltpu.SMEM)
    rest = pl.BlockSpec(memory_space=where)
    return pl.pallas_call(
        body,
        out_shape=tuple(outs),
        in_specs=[smem] * smem_count + [rest] * (len(args) - smem_count),
        out_specs=tuple(vmem for _ in outs),
        scratch_shapes=list(scratch),
        compiler_params=pltpu.CompilerParams(vmem_limit_bytes=limit),
        cost_estimate=pl.CostEstimate(
            flops=flops, bytes_accessed=nbytes, transcendentals=transcendentals
        ),
    )(*args)


def gelu_parts(pre):
    t = jnp.tanh(GELU_A * (pre + GELU_B * pre * pre * pre))
    return t, (0.5 * pre * (1.0 + t)).astype(bf16)


def ask_kernel(
    mined_hbm, home_hbm, positive_hbm, x_hbm, w_in_hbm, bias_hbm, w_out_hbm, send, mined, home, positive, x, w_in, bias, w_out, vec, stage, rid, code, count, goal_owner, goal_rank, sems
):
    query_count, mined_count = mined.shape
    owner_count, rows, _ = stage.shape
    query_len = x.shape[0] // query_count
    line_count = home.shape[0] // owner_count
    stride = rows + ASK_ROWS
    pairs = (
        (mined_hbm, mined),
        (home_hbm, home),
        (positive_hbm, positive),
        (x_hbm, x),
        (w_in_hbm, w_in),
        (bias_hbm, bias),
        (w_out_hbm, w_out),
    )
    copies = [pltpu.make_async_copy(a, b, sems.at[i]) for i, (a, b) in enumerate(pairs)]
    for copy in copies:
        copy.start()

    def clear(owner, carry):
        count[owner] = 0
        for c in range(CAP):
            rid[c, owner] = int(UNUSED)
            code[c, owner] = int(UNUSED)
        return carry

    lax.fori_loop(0, owner_count, clear, 0, unroll=True)
    stage[...] = jnp.zeros(stage.shape, bf16)
    for copy in copies[:3]:
        copy.wait()

    def assign(query, carry):
        for j in range(mined_count):
            row = home[mined[query, j]]
            owner = row // line_count
            rank = count[owner]
            count[owner] = rank + 1
            rid[rank, owner] = row - owner * line_count
            code[rank, owner] = query + jnp.where(positive[query] == j, 8, 0)
            goal_owner[query, j] = owner
            goal_rank[query, j] = rank * query_len
        return carry

    lax.fori_loop(0, query_count, assign, 0, unroll=True)
    for copy in copies[3:]:
        copy.wait()
    _, hidden = gelu_parts(dot(x[...], w_in[...]) + bias[...].reshape(1, -1))
    vec[...] = dot(hidden, w_out[...]).astype(bf16)

    sub = lax.broadcasted_iota(jnp.int32, (ASK_ROWS, LANES), 0)
    low = lax.broadcasted_iota(jnp.int32, (ASK_ROWS, LANES), 1) < HALF
    for owner in range(owner_count):
        tile = jnp.where(
            sub == 0,
            jnp.where(low, rid[0, owner], rid[1, owner]),
            jnp.where(low, code[0, owner], code[1, owner]),
        )
        first = owner * stride + rows
        send[first : first + ASK_ROWS, :] = tile.astype(f32).astype(bf16)
    def place(query, carry):
        block = vec[pl.ds(pl.multiple_of(query * query_len, query_len), query_len), :]
        for j in range(mined_count):
            first = pl.multiple_of(goal_rank[query, j], query_len)
            stage[goal_owner[query, j], pl.ds(first, query_len), :] = block
        return carry

    lax.fori_loop(0, query_count, place, 0, unroll=True)
    for owner in range(owner_count):
        send[owner * stride : owner * stride + rows, :] = stage[owner]


def head_kernel(xl, xq, w_in, bias, w_out, line_vec, line_vec_t, hidden_all, slope_t, mean):
    step = 256
    line_frames = xl.shape[0]
    total = jnp.zeros((1, hidden_all.shape[1]), f32)
    for first in range(0, line_frames + xq.shape[0], step):
        if first < line_frames:
            x = xl[first : first + step, :]
        else:
            x = xq[first - line_frames : first - line_frames + step, :]
        size = x.shape[0]
        pre = dot(x, w_in[...]) + bias[...].reshape(1, -1)
        t, hidden = gelu_parts(pre)
        slope = 0.5 * (1.0 + t) + 0.5 * pre * (1.0 - t * t) * GELU_A * (
            1.0 + 3.0 * GELU_B * pre * pre
        )
        hidden_all[first : first + size, :] = hidden
        slope_t[:, first : first + size] = slope.T
        if first < line_frames:
            vec = dot(hidden, w_out[...])
            for k in range(0, size, LANES):
                line = (first + k) // LANES
                line_vec[line] = vec[k : k + LANES].astype(bf16)
                line_vec_t[line] = vec[k : k + LANES].T.astype(bf16)
            total += jnp.sum(hidden.astype(f32), axis=0, keepdims=True)
    mean[...] = jnp.broadcast_to(total * (1.0 / line_frames), mean.shape)


def spread(meta, first, query_len):
    parts = []
    for b in range(meta.shape[0]):
        for c in range(CAP):
            parts.append(jnp.broadcast_to(meta[b, first + c : first + c + 1, :], (query_len, LANES)))
    return jnp.concatenate(parts, axis=0)


def match_kernel(
    place, counts, got, line_vec, line_vec_t, mean, send, weights, own, pads, label_rows, ids, sums, sem
):
    owner_count, rows, _ = weights.shape
    query_len = rows // CAP
    stride, out_stride = rows + ASK_ROWS, rows + BACK_ROWS
    line_count, _, vec_width = line_vec.shape
    scale = SCORE_SCALE / math.sqrt(vec_width)
    lane1 = lax.broadcasted_iota(jnp.int32, (1, LANES), 1)
    lane2 = lax.broadcasted_iota(jnp.int32, (ASK_ROWS, LANES), 1) % HALF
    labels = jnp.full((ASK_ROWS, LANES), UNUSED, f32)
    for b in range(owner_count):
        first = b * stride + rows
        labels = jnp.where(lane2 == b, got[first : first + ASK_ROWS, :].astype(f32), labels)
    rid_row, code_row = labels[0:1], labels[1:2]
    rid_row = jnp.where(rid_row < line_count, rid_row, 0.0)
    label_rows[...] = jnp.broadcast_to(rid_row, (META, LANES)).astype(jnp.int32)
    copy = pltpu.make_async_copy(label_rows, ids, sem)
    copy.start()
    for r in range(line_count):
        pads[r : r + 1, :] = jnp.where(lane1 < counts[place[0] * line_count + r], 0.0, FLOOR)
    sums[...] = jnp.zeros(sums.shape, f32)
    ones = jnp.ones((LANES, LANES), bf16)
    copy.wait()
    for b in range(owner_count):
        for c in range(CAP):
            slot = b + HALF * c
            r = ids[0, slot]
            first = b * stride + c * query_len
            logits = dot(got[first : first + query_len, :], line_vec_t[r]) * scale
            logits = logits + pads[pl.ds(r, 1), :]
            peak = jnp.max(logits, axis=1, keepdims=True)
            scaled = jnp.exp(logits - peak).astype(bf16)
            both = dot(scaled, jnp.concatenate([line_vec[r], ones], axis=1))
            totals = both[:, vec_width:]
            inverse = 1.0 / totals
            weights[b, c * query_len : (c + 1) * query_len, :] = (
                scaled.astype(f32) * inverse
            ).astype(bf16)
            first = b * out_stride + c * query_len
            send[first : first + query_len, :] = (both[:, :vec_width] * inverse).astype(bf16)
            log_total = peak + jnp.log(totals)
            sums[slot : slot + 1, :] = jnp.sum(log_total, axis=0, keepdims=True) * (1.0 / query_len)
    lane = lax.broadcasted_iota(jnp.int32, sums.shape, 1)
    row = lax.broadcasted_iota(jnp.int32, sums.shape, 0)
    match_row = jnp.sum(jnp.where(lane == row, sums[...], 0.0), axis=0, keepdims=True)
    high, low = (part.astype(f32) for part in split2(match_row))
    blocks = own_blocks(mean.shape[1])
    mean_row = mean[:, 0:LANES]
    for k in range(1, blocks):
        mean_row = jnp.where(place[0] % blocks == k, mean[:, k * LANES : (k + 1) * LANES], mean_row)
    sub = lax.broadcasted_iota(jnp.int32, (META, LANES), 0)
    own[...] = jnp.where(sub == 0, high + low, jnp.where(sub == 1, code_row, rid_row))
    sub = lax.broadcasted_iota(jnp.int32, (BACK_ROWS, LANES), 0)
    tile = jnp.where(
        sub == 0, high, jnp.where(sub == 1, low, jnp.where(sub == 2, code_row, mean_row[0:1]))
    ).astype(bf16)
    for b in range(owner_count):
        first = b * out_stride + rows
        send[first : first + BACK_ROWS, :] = tile


def own_blocks(hid):
    return hid // LANES


def grad_kernel(
    place, back, got, weights, own, xl, xq, hidden_all, slope_t, w_out, loss, keep, give, base_row, grads, own_scale, ask_scale, line_acc, query_acc, *, loss_factor
):
    owner_count, rows, _ = weights.shape
    stride, back_stride = rows + ASK_ROWS, rows + BACK_ROWS
    query_len = rows // CAP
    line_total = xl.shape[0]
    line_count = line_total // LANES
    query_frames = xq.shape[0]
    vec_width = w_out.shape[1]
    hid = w_out.shape[0]
    blocks = own_blocks(hid)
    me = place[0]

    shape3 = (owner_count, META, LANES)
    lane3 = lax.broadcasted_iota(jnp.int32, shape3, 2)
    sub3 = lax.broadcasted_iota(jnp.int32, shape3, 1)
    owner3 = lax.broadcasted_iota(jnp.int32, shape3, 0)
    subf = sub3.astype(f32)
    matches, codes = [], []
    shared = [jnp.zeros((1, LANES), f32) for _ in range(blocks)]
    for owner in range(owner_count):
        first = owner * back_stride + rows
        tile = back[first : first + BACK_ROWS, :].astype(f32)
        matches.append(jnp.broadcast_to(tile[0:1] + tile[1:2], (1, META, LANES)))
        codes.append(jnp.broadcast_to(tile[2:3], (1, META, LANES)))
        shared[owner % blocks] += tile[3:4]
    match = jnp.concatenate(matches, axis=0)
    code = jnp.concatenate(codes, axis=0)
    shared = [
        part * (1.0 / ((owner_count - k + blocks - 1) // blocks)) for k, part in enumerate(shared)
    ]
    shared = jnp.concatenate(shared, axis=1).astype(bf16).astype(f32)
    base_row[...] = jnp.broadcast_to(shared, base_row.shape)
    is_pos = (code >= 8.0) & (code < 16.0)
    query_of = jnp.where(is_pos, code - 8.0, code)
    here = query_of == subf
    peak = jnp.max(jnp.where(here, match, FLOOR), axis=0)
    peak = jnp.maximum(peak, pltpu.roll(peak, HALF, 1))
    raised = jnp.where(here, jnp.exp(match - peak[None]), 0.0)
    total = jnp.sum(raised, axis=0)
    total = total + pltpu.roll(total, HALF, 1)
    total = jnp.where(total > 0.0, total, 1.0)
    chosen = jnp.sum(jnp.where(here & is_pos, match, 0.0), axis=0)
    chosen = chosen + pltpu.roll(chosen, HALF, 1)
    log_total = peak + jnp.log(total)
    lane2 = lax.broadcasted_iota(jnp.int32, (META, LANES), 1)
    sub2 = lax.broadcasted_iota(jnp.int32, (META, LANES), 0).astype(f32)
    picked = jnp.sum(jnp.where(lane2 == me, log_total - chosen, 0.0), axis=1, keepdims=True)
    loss[...] = jnp.broadcast_to(picked, (META, LANES))

    factor = loss_factor * SCORE_SCALE / (math.sqrt(vec_width) * query_len)

    own_match = own[0:1, :]
    own_code = own[1:2, :]
    own_pos = (own_code >= 8.0) & (own_code < 16.0)
    own_query = jnp.where(own_pos, own_code - 8.0, own_code)
    own_grad = jnp.exp(jnp.minimum(own_match - log_total, 0.0)) - jnp.where(own_pos, 1.0, 0.0)
    own_grad = factor * jnp.sum(jnp.where(own_query == sub2, own_grad, 0.0), axis=0, keepdims=True)
    both = jnp.where(lane2 >= 0, jnp.where(sub2 < CAP, own_grad, own[2:3, :]), 0.0)
    slot3 = HALF * (sub3 % CAP)
    own_scale[...] = jnp.broadcast_to(
        jnp.sum(
            jnp.where(lane3 == owner3 + slot3, jnp.broadcast_to(both[None], shape3), 0.0),
            axis=2,
            keepdims=True,
        ),
        shape3,
    )

    ask_grad = raised * (1.0 / total)[None] - jnp.where(here & is_pos, 1.0, 0.0)
    ask_grad = factor * jnp.sum(ask_grad, axis=1, keepdims=True)
    both = jnp.where(sub3 < CAP, jnp.broadcast_to(ask_grad, shape3), query_of)
    ask_scale[...] = jnp.broadcast_to(
        jnp.sum(jnp.where(lane3 == me + slot3, both, 0.0), axis=2, keepdims=True), shape3
    )

    size = owner_count * rows
    frame = (lax.broadcasted_iota(jnp.int32, (size, LANES), 0) % query_len).astype(f32)
    lane = lax.broadcasted_iota(jnp.int32, (size, LANES), 1).astype(f32)
    zero = jnp.zeros((size, LANES), bf16)
    one = jnp.ones((size, LANES), bf16)

    labels = own_scale[...]
    queries = jnp.concatenate(
        [got[b * stride : b * stride + rows, :] for b in range(owner_count)], axis=0
    )
    rid = spread(labels, CAP, query_len).astype(bf16)
    weight = weights[...].reshape(size, LANES).astype(f32)
    score = (weight * spread(labels, 0, query_len)).astype(bf16)
    wide = jnp.concatenate([jnp.where(rid == r, score, zero) for r in range(line_count)], axis=1)
    line_acc[...] = dot(queries, wide, 0, 0)

    labels = ask_scale[...]
    target = spread(labels, CAP, query_len) * float(query_len) + frame
    pulled = jnp.concatenate(
        [back[b * back_stride : b * back_stride + rows, :] for b in range(owner_count)], axis=0
    )
    pulled = (pulled.astype(f32) * spread(labels, 0, query_len)).astype(bf16)
    wide = jnp.concatenate(
        [
            jnp.where(target == lane + float(k), one, zero)
            for k in range(0, query_acc.shape[1], LANES)
        ],
        axis=1,
    )
    query_acc[...] = dot(pulled, wide, 0, 0)

    grad_in = None
    grad_out = None
    grad_bias = None
    vec_sum = None
    spans = ((line_acc, xl, 0, line_total), (query_acc, xq, line_total, query_frames))
    for acc, x, first, span in spans:
        g_hi, g_lo = split2(acc[:, 0:span])
        grad_hidden = dot(w_out[...], g_hi) + dot(w_out[...], g_lo)
        grad_pre = grad_hidden * slope_t[:, first : first + span]
        p_hi = grad_pre.astype(bf16)
        hidden = hidden_all[first : first + span, :]
        ones = jnp.ones((META, span), bf16)
        part_in = dot(p_hi, x[...])
        part_out = dot(g_hi, hidden) + dot(g_lo, hidden)
        part_out -= jnp.sum(g_hi.astype(f32) + g_lo.astype(f32), axis=1, keepdims=True) * shared
        part_sum = dot(ones, g_hi, 1, 1) + dot(ones, g_lo, 1, 1)
        vec_sum = part_sum if vec_sum is None else vec_sum + part_sum
        part_bias = sum(grad_pre[:, k : k + LANES] for k in range(0, span, LANES))
        grad_in = part_in if grad_in is None else grad_in + part_in
        grad_out = part_out if grad_out is None else grad_out + part_out
        grad_bias = part_bias if grad_bias is None else grad_bias + part_bias
    grad_bias = jnp.sum(grad_bias.T, axis=0, keepdims=True)
    base = 0
    for k in range(0, x.shape[1], LANES):
        grads[base : base + hid, :] = grad_in[:, k : k + LANES]
        base += hid
    for k in range(0, hid, LANES):
        grads[base : base + vec_width, :] = grad_out[:, k : k + LANES]
        base += vec_width
    rest = grads.shape[0] - base
    singles = [grad_bias[0:1, k : k + LANES] for k in range(0, hid, LANES)] + [vec_sum[0:1, :]]
    grads[base:, :] = tail_tile(singles, rest)
    half = keep.shape[0]
    core = place[1]
    keep[...] = grads[pl.ds(pl.multiple_of(core * half, half), half), :]
    give[...] = grads[pl.ds(pl.multiple_of((1 - core) * half, half), half), :].astype(bf16)


def tail_tile(values, size):
    sub = lax.broadcasted_iota(jnp.int32, (size, LANES), 0)
    tile = jnp.zeros((size, LANES), f32)
    for i, value in enumerate(values):
        for p, part in enumerate(split3(value)):
            tile = jnp.where(sub == 3 * i + p, part, tile)
    return tile


def tail_values(tile, count):
    return [
        tile[3 * i : 3 * i + 1] + tile[3 * i + 1 : 3 * i + 2] + tile[3 * i + 2 : 3 * i + 3]
        for i in range(count)
    ]


def sum_core_kernel(place, keep, got, send, *, tail_rows, tail_count):
    total = keep[...] + got[...].astype(f32)
    send[...] = total.astype(bf16)

    @pl.when(place[1] == 1)
    def _():
        first = total.shape[0] - tail_rows
        values = tail_values(total[first:, :], tail_count)
        send[first:, :] = tail_tile(values, tail_rows).astype(bf16)


def sum_kernel(got, send):
    part = jnp.sum(got[...].astype(f32), axis=0).astype(bf16)
    for k in range(send.shape[0]):
        send[k] = part


def unpack_kernel(place, mine, other, base_row, grad_in, grad_bias, grad_out, got):
    feat, hid = grad_in.shape
    vec_width = grad_out.shape[1]
    half = mine.shape[0]
    core = place[1]
    got[pl.ds(pl.multiple_of(core * half, half), half), :] = mine[...]
    got[pl.ds(pl.multiple_of((1 - core) * half, half), half), :] = other[...]
    base = 0
    for k in range(0, feat, LANES):
        grad_in[k : k + LANES, :] = got[base : base + hid, :].astype(f32).T
        base += hid
    start = base + vec_width * (hid // LANES)
    values = tail_values(got[start : start + 16, :].astype(f32), hid // LANES + 1)
    vec_sum = values[-1]
    sub = lax.broadcasted_iota(jnp.int32, (META, LANES), 0)
    zero = jnp.zeros((META, LANES), f32)
    vec_rows = zero
    for p, part in enumerate(split3(vec_sum)):
        vec_rows = jnp.where(sub == p, part, vec_rows)
    vec_rows = vec_rows.astype(bf16)
    for i, k in enumerate(range(0, hid, LANES)):
        base_rows = base_row[:, k : k + LANES].astype(bf16)
        outer = dot(base_rows, vec_rows, 0, 0)
        grad_out[k : k + LANES, :] = got[base : base + vec_width, :].astype(f32).T + outer
        grad_bias[k : k + LANES] = values[i].reshape(LANES)
        base += vec_width


def exchange(x, axis):
    return lax.all_to_all(x, axis, split_axis=0, concat_axis=0, tiled=True)


def exchange_rows(x, axis, peers, tile):
    blocks = x.reshape(peers, x.shape[0] // (peers * tile), tile, x.shape[1])
    return exchange(blocks, axis).reshape(x.shape)


def shape_of(shape, dtype):
    return jax.ShapeDtypeStruct(shape, dtype)


def local(query_frames, line_frames, frame_count, line_home, mined, positive, w_in, bias_in, w_out):
    query_count, query_len, feat = query_frames.shape
    line_count, line_len, _ = line_frames.shape
    hid, vec_width = w_out.shape
    chip_count = lax.axis_size("chip")
    owner_count = chip_count * lax.axis_size("core")
    dp_count = lax.axis_size("dp")
    loss_factor = LOSS_SCALE / (query_count * owner_count * dp_count)
    frames_q = query_count * query_len
    frames_l = line_count * line_len
    frames = frames_q + frames_l
    rows = CAP * query_len
    xq = query_frames.reshape(frames_q, feat)
    xl = line_frames.reshape(frames_l, feat)
    place = jnp.stack([lax.axis_index(ARCHIVE), lax.axis_index("core")]).astype(jnp.int32)
    ask_wire = shape_of((owner_count * (rows + ASK_ROWS), vec_width), bf16)
    back_wire = shape_of((owner_count * (rows + BACK_ROWS), vec_width), bf16)
    head_flops = 2 * hid * (feat + vec_width)

    (asked,) = call(
        ask_kernel,
        [ask_wire],
        [mined, line_home, positive, xq, w_in, bias_in, w_out],
        0,
        [
            pltpu.SMEM(mined.shape, jnp.int32),
            pltpu.SMEM(line_home.shape, jnp.int32),
            pltpu.SMEM(positive.shape, jnp.int32),
            pltpu.VMEM(xq.shape, bf16),
            pltpu.VMEM(w_in.shape, bf16),
            pltpu.VMEM(bias_in.shape, f32),
            pltpu.VMEM(w_out.shape, bf16),
            pltpu.VMEM((frames_q, vec_width), bf16),
            pltpu.VMEM((owner_count, rows, vec_width), bf16),
            pltpu.SMEM((CAP, owner_count), jnp.int32),
            pltpu.SMEM((CAP, owner_count), jnp.int32),
            pltpu.SMEM((owner_count,), jnp.int32),
            pltpu.SMEM(mined.shape, jnp.int32),
            pltpu.SMEM(mined.shape, jnp.int32),
            pltpu.SemaphoreType.DMA((7,)),
        ],
        flops=frames_q * head_flops,
        where=pltpu.HBM,
        limit=63 << 20,
    )
    got = exchange_rows(asked, ARCHIVE, owner_count, ASK_ROWS)
    line_vec, line_vec_t, hidden_all, slope_t, mean = call(
        head_kernel,
        [
            shape_of((line_count, line_len, vec_width), bf16),
            shape_of((line_count, vec_width, line_len), bf16),
            shape_of((frames, hid), bf16),
            shape_of((hid, frames), f32),
            shape_of((META, hid), f32),
        ],
        [xl, xq, w_in, bias_in, w_out],
        0,
        flops=frames * head_flops,
        transcendentals=frames * hid,
    )
    match_flops = 2 * owner_count * rows * frames_l * vec_width
    answer, weights, own = call(
        match_kernel,
        [
            back_wire,
            shape_of((owner_count, rows, line_len), bf16),
            shape_of((META, LANES), f32),
        ],
        [place, frame_count, got, line_vec, line_vec_t, mean],
        2,
        [
            pltpu.VMEM((line_count, LANES), f32),
            pltpu.VMEM((META, LANES), jnp.int32),
            pltpu.SMEM((META, LANES), jnp.int32),
            pltpu.VMEM((LANES, LANES), f32),
            pltpu.SemaphoreType.DMA(()),
        ],
        flops=2 * match_flops,
    )
    back = exchange_rows(answer, ARCHIVE, owner_count, BACK_ROWS)
    unit = 16 * owner_count
    flat_rows = unit * -(-(LANES + (feat + vec_width) * hid // LANES) // unit)
    half = flat_rows // 2

    def grads_body(*refs):
        grad_kernel(*refs, loss_factor=loss_factor)

    loss, keep, give, base_row = call(
        grads_body,
        [
            shape_of((META, LANES), f32),
            shape_of((half, LANES), f32),
            shape_of((half, LANES), bf16),
            shape_of((META, hid), f32),
        ],
        [place, back, got, weights, own, xl, xq, hidden_all, slope_t, w_out],
        1,
        [
            pltpu.VMEM((flat_rows, LANES), f32),
            pltpu.VMEM((owner_count, META, LANES), f32),
            pltpu.VMEM((owner_count, META, LANES), f32),
            pltpu.VMEM((vec_width, frames_l), f32),
            pltpu.VMEM((vec_width, frames_q), f32),
        ],
        flops=match_flops + 4 * frames * head_flops,
    )
    swap = [(0, 1), (1, 0)]
    share = half // chip_count
    taken = lax.ppermute(give, "core", swap)
    tail_rows = flat_rows - (feat + vec_width) * hid // LANES

    def sum_core_body(*refs):
        sum_core_kernel(*refs, tail_rows=tail_rows, tail_count=hid // LANES + 1)

    (part,) = call(sum_core_body, [shape_of((half, LANES), bf16)], [place, keep, taken], 1)
    parts = exchange_rows(part, "chip", chip_count, 4).reshape(chip_count, share, LANES)
    (part,) = call(sum_kernel, [shape_of((dp_count, share, LANES), bf16)], [parts], 0)
    part = part.reshape(dp_count * share, LANES)
    parts = exchange_rows(part, "dp", dp_count, 4).reshape(dp_count, share, LANES)
    (part,) = call(sum_kernel, [shape_of((chip_count, share, LANES), bf16)], [parts], 0)
    mine = exchange_rows(part.reshape(half, LANES), "chip", chip_count, 4)
    other = lax.ppermute(mine, "core", swap)
    grad_in, grad_bias, grad_out = call(
        unpack_kernel,
        [shape_of((feat, hid), f32), shape_of((hid,), f32), shape_of((hid, vec_width), f32)],
        [place, mine, other, base_row],
        1,
        [pltpu.VMEM((flat_rows, LANES), bf16)],
    )
    return (loss[:query_count, 0], grad_in, grad_bias, grad_out)


def solution(mesh):
    devices = mesh.devices
    archive, dp = devices.shape
    mesh = Mesh(devices.reshape(archive // 2, 2, dp), ("chip", "core", "dp"))
    everywhere = ARCHIVE + ("dp",)
    placed = (
        P(everywhere, None, None),
        P(ARCHIVE, None, None),
        P(),
        P(),
        P(everywhere, None),
        P(everywhere),
        P(),
        P(),
        P(),
    )
    return jax.shard_map(
        local,
        mesh=mesh,
        in_specs=placed,
        out_specs=(P(everywhere), P(), P(), P()),
        check_vma=False,
    )
```
